32 devices in a mesh: clip: 4 (over y, core), frame: 8 (over z, x).
Axes of the slice: x: 2, y: 2, z: 4, core: 2. Of those that a mesh axis runs over, the one named last changes fastest.
Arguments:
- x_in: bfloat16 [64, 20, 20, 1024], P(('clip', 'frame')), may hold values from -8 to 8
- cotangent: bfloat16 [64, 20, 20, 1024], P(('clip', 'frame')), may hold values from -6 to 6
- w_reduce: bfloat16 [1024, 256], P('frame'), may hold values from -0.1875 to 0.1875
- w_spatial: bfloat16 [3, 3, 256, 256], P(None, None, 'frame'), may hold values from -0.125 to 0.125
- w_expand: bfloat16 [256, 1024], P('frame'), may hold values from -0.375 to 0.375
- gain_one: bfloat16 [256], P('frame'), may hold values from 0.5 to 1.5
- shift_one: bfloat16 [256], P('frame'), may hold values from -2 to 2
- gain_two: bfloat16 [256], P('frame'), may hold values from 0.5 to 1.5
- shift_two: bfloat16 [256], P('frame'), may hold values from -2 to 2
- gain_three: bfloat16 [1024], P('frame'), may hold values from 0.5 to 1.5
- shift_three: bfloat16 [1024], P('frame'), may hold values from -2 to 2
- bucket: int32 [64], P(('clip', 'frame')), may hold values from 0 to 1
- frame_count: int32 [32], P(('clip', 'frame')), may hold values from 1 to 2, as said below
Outputs:
- output: bfloat16 [64, 20, 20, 1024], P(('clip', 'frame'))
- grad_in: bfloat16 [64, 20, 20, 1024], P(('clip', 'frame'))
- grad_reduce: float32 [1024, 256], P('frame')
- grad_spatial: float32 [3, 3, 256, 256], P(None, None, 'frame')
- grad_expand: float32 [256, 1024], P('frame')
- grad_gain_one: float32 [256], P('frame')
- grad_shift_one: float32 [256], P('frame')
- grad_gain_two: float32 [256], P('frame')
- grad_shift_two: float32 [256], P('frame')
- grad_gain_three: float32 [1024], P('frame')
- grad_shift_three: float32 [1024], P('frame')
The draws below stay inside these ranges and needn't reach their ends.
Inputs may be any that keep to these rules, and one draw needn't show every extreme that they name: A device's used frames fill its first frame_count slots; in every draw some device uses all 2 slots.
All inputs are finite; a program needn't handle non-finite values.
Results may differ from the reference program's by a relative error of at most 0.017.
Values may be sent and summed in bfloat16 or wider, within the bound.
A program may use at most 64 MiB of HBM per device.

```python
import jax
import jax.numpy as jnp
from jax import lax

CHANNELS = 1024
BOTTLENECK = 256
FRAME_SIDE = 20
SMALL_SIDE = 14
FRAMES_DEV = 2
GROUPS = 32
FRAMES = 64


def draw_x_in(key, part):
    key = jax.random.fold_in(key, 11)
    first, second = jax.random.split(key, 2)
    offset = 0.5 * jax.random.normal(second, (CHANNELS,), jnp.float32)
    rising = jnp.arange(FRAMES, dtype=jnp.float32) / FRAMES
    shape = (FRAMES, FRAME_SIDE, FRAME_SIDE, CHANNELS)
    base = jax.random.normal(first, shape, jnp.float32)
    factor = 0.6 + 1.2 * rising
    values = (base + offset) * factor[:, None, None, None]
    return jnp.clip(values, -8.0, 8.0).astype(jnp.bfloat16)


def draw_frame_count(key, part):
    key = jax.random.fold_in(key, 23)
    first, second = jax.random.split(key)
    lowest = FRAMES_DEV - FRAMES_DEV // 2
    counts = jax.random.randint(first, (GROUPS,), lowest, FRAMES_DEV + 1)
    fullest = jax.random.randint(second, (), 0, GROUPS)
    return jnp.where(jnp.arange(GROUPS) == fullest, FRAMES_DEV, counts).astype(jnp.int32)


def set_ends(result, own_key, least, top_value):
    longest = result.shape.index(max(result.shape))
    spots = []
    for shift in (0, 1):
        where = [jax.random.randint(jax.random.fold_in(own_key, axis), (), 0, length) for axis, length in enumerate(result.shape)]
        where[longest] = (where[longest] + shift) % result.shape[longest]
        spots.append(tuple(where))
    return result.at[spots[0]].set(least).at[spots[1]].set(top_value)


def level_of(own_key, shape, cuts, smallest, top_value):
    def one(dim, shards_of):
        heights = jax.random.uniform(jax.random.fold_in(jax.random.fold_in(own_key, 6), dim), (shards_of,), jnp.float32, smallest / len(cuts), top_value / len(cuts))
        return jnp.repeat(jnp.exp(heights), shape[dim] // shards_of).reshape((-1,) + (1,) * (len(shape) - dim - 1))

    level = one(*cuts[0])
    for cut in cuts[1:]:
        level = level * one(*cut)
    return level


def bell_draw(key, dims, width, limit, shards=(), kind=jnp.bfloat16):
    level = level_of(key, dims, shards, -0.22, 0.18) if shards else 1.0
    drawn = jax.random.normal(key, dims, jnp.float32) * width * level
    return jnp.minimum(jnp.maximum(drawn, -limit), limit).astype(kind)


def setup_inputs(seed: int = 0) -> dict:
    streams_of = jax.random.split(jax.random.key(seed), 14)
    return {
        "x_in": draw_x_in(jax.random.fold_in(streams_of[13], 71), 0),
        "cotangent": bell_draw(streams_of[1], (FRAMES, FRAME_SIDE, FRAME_SIDE, CHANNELS), 1.0, 6.0, ((0, 32),)),
        "w_reduce": bell_draw(streams_of[2], (CHANNELS, BOTTLENECK), CHANNELS ** -0.5, 0.1875, ((0, 8),)),
        "w_spatial": bell_draw(streams_of[3], (3, 3, BOTTLENECK, BOTTLENECK), (9 * BOTTLENECK) ** -0.5, 0.125, ((2, 8),)),
        "w_expand": bell_draw(streams_of[4], (BOTTLENECK, CHANNELS), BOTTLENECK ** -0.5, 0.375, ((0, 8),)),
        "gain_one": jnp.clip(1.0 + 0.1 * jax.random.normal(streams_of[5], (BOTTLENECK,), jnp.float32), 0.5, 1.5).astype(jnp.bfloat16),
        "shift_one": bell_draw(streams_of[6], (BOTTLENECK,), 0.5, 2.0, ((0, 8),)),
        "gain_two": jnp.clip(1.0 + 0.1 * jax.random.normal(streams_of[7], (BOTTLENECK,), jnp.float32), 0.5, 1.5).astype(jnp.bfloat16),
        "shift_two": bell_draw(streams_of[8], (BOTTLENECK,), 0.5, 2.0, ((0, 8),)),
        "gain_three": jnp.clip(1.0 + 0.1 * jax.random.normal(streams_of[9], (CHANNELS,), jnp.float32), 0.5, 1.5).astype(jnp.bfloat16),
        "shift_three": bell_draw(streams_of[10], (CHANNELS,), 0.5, 2.0, ((0, 8),)),
        "bucket": set_ends(jax.random.randint(streams_of[11], (FRAMES,), 0, 2), jax.random.fold_in(streams_of[11], 1), 0, 1).astype(jnp.int32),
        "frame_count": draw_frame_count(jax.random.fold_in(streams_of[13], 71), 0),
    }


@jax.custom_vjp
def low(v):
    return lax.optimization_barrier(v.astype(jnp.bfloat16)).astype(jnp.float32)

@jax.custom_vjp
def low_back(v):
    return v

def low_keep(v):
    return (low(v), None)

def low_pass(kept, grad):
    return (grad,)

def back_keep(v):
    return (v, None)

def back_low(kept, grad):
    return (low(grad),)
low.defvjp(low_keep, low_pass)
low_back.defvjp(back_keep, back_low)
eps_norm = 1e-05
highest = lax.Precision.HIGHEST

def build_mask(bucket, frame_count):
    slots = jnp.arange(FRAMES, dtype=jnp.int32)
    owner = (slots // FRAMES_DEV).astype(jnp.int32)
    live = slots % FRAMES_DEV < frame_count[owner]
    extent = jnp.where(bucket == 0, SMALL_SIDE, FRAME_SIDE)
    places = jnp.arange(FRAME_SIDE, dtype=jnp.int32)
    inside = (places[None, :, None] < extent[:, None, None]) & (places[None, None, :] < extent[:, None, None]) & live[:, None, None]
    return inside.astype(jnp.float32)[..., None]

def batch_norm(values, gain, shift, pixel_mask):
    count = jnp.sum(pixel_mask)
    total = lax.optimization_barrier(jnp.sum(pixel_mask * values, axis=(0, 1, 2)))
    squares = lax.optimization_barrier(jnp.sum(pixel_mask * values * values, axis=(0, 1, 2)))
    mean = total / count
    var = squares / count - mean * mean
    return (values - mean) * lax.rsqrt(var + eps_norm) * gain + shift

def reference(x_in, cotangent, w_reduce, w_spatial, w_expand, gain_one, shift_one, gain_two, shift_two, gain_three, shift_three, bucket, frame_count):
    pixel_mask = build_mask(bucket, frame_count)

    def forward(inputs, wr, ws, we, g1, b1, g2, b2, g3, b3):
        masked = inputs * pixel_mask
        pre_one = low_back(jnp.einsum('fhwc,cd->fhwd', masked, wr, precision=highest))
        act_one = low(pixel_mask * jax.nn.silu(batch_norm(pre_one, g1, b1, pixel_mask)))
        pre_two = low_back(lax.conv_general_dilated(act_one, ws, (1, 1), 'SAME', dimension_numbers=('NHWC', 'HWIO', 'NHWC'), precision=highest))
        act_two = low(pixel_mask * jax.nn.silu(batch_norm(pre_two, g2, b2, pixel_mask)))
        pre_three = low_back(jnp.einsum('fhwd,dc->fhwc', act_two, we, precision=highest))
        total = batch_norm(pre_three, g3, b3, pixel_mask) + masked
        return pixel_mask * jax.nn.silu(total)
    primals = [a.astype(jnp.float32) for a in (x_in, w_reduce, w_spatial, w_expand, gain_one, shift_one, gain_two, shift_two, gain_three, shift_three)]
    output, pullback = jax.vjp(forward, *primals)
    grads = pullback(cotangent.astype(jnp.float32))
    return (output.astype(jnp.bfloat16), grads[0].astype(jnp.bfloat16), grads[1], grads[2], grads[3], grads[4], grads[5], grads[6], grads[7], grads[8], grads[9])
```

```python
import functools

import jax
import jax.numpy as jnp
from jax import lax
from jax.experimental import pallas as pl
from jax.experimental.pallas import tpu as pltpu
from jax.sharding import PartitionSpec as P

SMALL_SIDE = 14
EPS = 1e-05
LANES = 128
BLOCK = 80
MESH = pl.DeviceIdType.MESH
F32 = jnp.float32
BF16 = jnp.bfloat16


def sigmoid(v):
    return 0.5 * jnp.tanh(0.5 * v) + 0.5


def part_sum(v):
    rows, width = v.shape
    return jnp.sum(v.reshape(rows // 8, 8, width), axis=0)


def dot(a, b):
    return jnp.dot(a, b, preferred_element_type=F32)


def dot_tn(a, b):
    return lax.dot_general(a, b, (((0,), (0,)), ((), ())), preferred_element_type=F32)


def rows_to_vec(tile, first, count):
    return jnp.concatenate([tile[first + i : first + i + 1] for i in range(count)], axis=1)


def block_kernel(
    dims,
    x_hbm,
    ct_hbm,
    wr_hbm,
    ws_hbm,
    we_hbm,
    g1_ref,
    b1_ref,
    g2_ref,
    b2_ref,
    g3_ref,
    b3_ref,
    bucket_ref,
    count_ref,
    out_hbm,
    gin_hbm,
    gr_out,
    gs_out,
    ge_out,
    vec1_gain,
    vec1_shift,
    vec2_gain,
    vec2_shift,
    vec3_gain,
    vec3_shift,
    xs,
    cs,
    os,
    xm,
    mask,
    left_ok,
    right_ok,
    wr,
    ws,
    we,
    wst,
    wet,
    wrt,
    pre1,
    slope1,
    pre2,
    slope2,
    dz,
    spad,
    act2,
    nine,
    pre3,
    gt,
    gp3,
    gp1,
    par,
    st1,
    st2,
    st3,
    st4,
    st5,
    st6,
    local_sem,
    wsend,
    wrecv,
    fsend,
    frecv,
    st_send,
    st_recv,
    out_sem,
    gr_ref,
    gs_ref,
    ge_ref,
    gr_core,
    gs_core,
    ge_core,
    gr_got,
    gs_got,
    ge_got,
    gr_fin,
    gs_fin,
    ge_fin,
    rs_send,
    rs_recv,
):
    clips, frames, side, own_gather = dims
    devices = clips * frames
    clip = lax.axis_index("clip")
    frame = lax.axis_index("frame")
    me = clip * frames + frame
    core = lax.rem(clip, 2)
    partner = (clip + 1 - 2 * core, frame)
    rows = xm.shape[0]
    channels = xm.shape[1]
    narrow = wr.shape[1]
    wide_tiles = channels // LANES
    nar_tiles = narrow // LANES
    blocks = rows // BLOCK
    pad = 2 * side

    def other(k):
        return (lax.rem(clip + lax.div(k, frames), clips), lax.rem(frame + lax.rem(k, frames), frames))

    for j in range(wide_tiles):
        lanes = pl.ds(LANES * j, LANES)
        pltpu.make_async_copy(x_hbm.at[:, :, lanes], xs.at[j], local_sem.at[0]).start()
    if own_gather:
        part_r = wr_hbm.shape[0]
        part_s = ws_hbm.shape[1]
        part_e = we_hbm.shape[0]
        own_r = wr.at[pl.ds(pl.multiple_of(frame * part_r, part_r), part_r)]
        own_s = ws.at[:, pl.ds(pl.multiple_of(frame * part_s, part_s), part_s)]
        own_e = we.at[pl.ds(pl.multiple_of(frame * part_e, part_e), part_e)]
    else:
        own_r, own_s, own_e = wr, ws, we
    own_copies = [
        pltpu.make_async_copy(wr_hbm, own_r, local_sem.at[2]),
        pltpu.make_async_copy(ws_hbm, own_s, local_sem.at[3]),
        pltpu.make_async_copy(we_hbm, own_e, local_sem.at[4]),
    ]
    for copy in own_copies:
        copy.start()
    for j in range(wide_tiles):
        lanes = pl.ds(LANES * j, LANES)
        pltpu.make_async_copy(ct_hbm.at[:, :, lanes], cs.at[j], local_sem.at[1]).start()

    barrier = pltpu.get_barrier_semaphore()

    def greet(k, carry):
        pl.semaphore_signal(barrier, inc=1, device_id=other(k), device_id_type=MESH)
        return carry

    lax.fori_loop(1, devices, greet, 0)

    row_id = lax.broadcasted_iota(jnp.int32, (rows, LANES), 0)
    pixel = row_id >> 1
    slot = row_id & 1
    line = (pixel * 3277) >> 16
    col = pixel - line * side
    extent = [jnp.where(bucket_ref[f] == 0, SMALL_SIDE, side) for f in range(2)]
    limit = [jnp.where(count_ref[0] > f, extent[f], 0) for f in range(2)]
    bound = jnp.where(slot == 0, limit[0], limit[1])
    live = ((line < bound) & (col < bound)).astype(F32)
    mask[...] = live
    left_ok[...] = (col >= 1).astype(F32)
    right_ok[...] = (col <= side - 2).astype(F32)

    tile = jnp.zeros((8, LANES), F32)
    par[me] = tile
    for i, ref in enumerate((g1_ref, b1_ref, g2_ref, b2_ref, g3_ref, b3_ref)):
        width = ref.shape[0]
        par[me, i : i + 1, 0:width] = ref[...].astype(F32).reshape(1, width)
    par[me, 6:7, :] = jnp.sum(live, axis=0, keepdims=True)

    pl.semaphore_wait(barrier, devices - 1)

    def gather_to_all(buf, index):
        def send(k, carry):
            pltpu.make_async_remote_copy(
                src_ref=buf.at[me],
                dst_ref=buf.at[me],
                send_sem=st_send.at[index],
                recv_sem=st_recv.at[index],
                device_id=other(k),
                device_id_type=MESH,
            ).start()
            return carry

        lax.fori_loop(1, devices, send, 0)

    def arrived(buf, index):
        most = buf.at[pl.ds(0, devices - 1)]
        pltpu.make_async_copy(most, most, st_recv.at[index]).wait()
        pltpu.make_async_copy(most, most, st_send.at[index]).wait()
        return jnp.sum(buf[...], axis=0)

    own_copies[0].wait()
    own_copies[1].wait()
    own_copies[2].wait()
    gather_to_all(par, 0)
    if own_gather:

        def halves(ref, axis, part):
            half = part // 2

            def view(owner):
                at = pl.ds(pl.multiple_of(owner * part + core * half, half), half)
                return ref.at[at] if axis == 0 else ref.at[:, at]

            return view

        views = (halves(wr, 0, part_r), halves(ws, 1, part_s), halves(we, 0, part_e))

        def weight_send(index):
            view = views[index]

            def send(b, carry):
                pltpu.make_async_remote_copy(
                    src_ref=view(frame),
                    dst_ref=view(frame),
                    send_sem=wsend.at[index, b],
                    recv_sem=wrecv.at[index, b],
                    device_id=(clip, lax.rem(frame + b, frames)),
                    device_id_type=MESH,
                ).start()
                return carry

            lax.fori_loop(1, frames, send, 0)

        def weight_pass(index):
            view = views[index]

            def step(b, carry):
                owner = lax.rem(frame - b + frames, frames)
                pltpu.make_async_remote_copy(
                    src_ref=view(owner),
                    dst_ref=view(owner),
                    send_sem=wsend.at[index, b],
                    recv_sem=wrecv.at[index, b],
                    device_id=partner,
                    device_id_type=MESH,
                ).wait()
                pltpu.make_async_remote_copy(
                    src_ref=view(owner),
                    dst_ref=view(owner),
                    send_sem=fsend.at[index, b],
                    recv_sem=frecv.at[index, b],
                    device_id=partner,
                    device_id_type=MESH,
                ).start()
                return carry

            lax.fori_loop(1, frames, step, 0)

        def weight_wait(index):
            view = views[index]

            def step(b, carry):
                owner = lax.rem(frame - b + frames, frames)
                pltpu.make_async_remote_copy(
                    src_ref=view(owner),
                    dst_ref=view(owner),
                    send_sem=fsend.at[index, b],
                    recv_sem=frecv.at[index, b],
                    device_id=partner,
                    device_id_type=MESH,
                ).wait()
                return carry

            lax.fori_loop(1, frames, step, 0)

        for index in range(3):
            weight_send(index)
    else:

        def weight_pass(index):
            pass

        def weight_wait(index):
            pass

    pltpu.make_async_copy(xs, xs, local_sem.at[0]).wait()
    xs_rows = xs.reshape(wide_tiles, rows, LANES)
    cs_rows = cs.reshape(wide_tiles, rows, LANES)
    os_rows = os.reshape(wide_tiles, rows, LANES)

    def block_at(i):
        return pl.ds(pl.multiple_of(i * BLOCK, BLOCK), BLOCK)

    def mask_in(i, carry):
        at = block_at(i)
        m = mask[at, :].astype(BF16)
        for j in range(wide_tiles):
            xm[at, LANES * j : LANES * (j + 1)] = xs_rows[j, at, :] * m
        return carry

    lax.fori_loop(0, blocks, mask_in, 0)
    edge = jnp.zeros((3, pad, narrow), F32)
    spad[:, 0:pad, :] = edge
    spad[:, pad + rows : 2 * pad + rows, :] = edge

    weight_pass(0)
    weight_wait(0)

    all_par = arrived(par, 0)
    count = all_par[6:7, :]
    part_n = g1_ref.shape[0]
    part_w = g3_ref.shape[0]
    acc_n = [jnp.zeros((8, LANES), F32) for _ in range(nar_tiles)]
    acc_w = [jnp.zeros((8, LANES), F32) for _ in range(wide_tiles)]
    for f in range(frames):
        tile = par[f]
        spot = f * part_n
        shift = spot % LANES
        acc_n[spot // LANES] += pltpu.roll(tile, shift, 1) if shift else tile
        spot = f * part_w
        shift = spot % LANES
        acc_w[spot // LANES] += pltpu.roll(tile, shift, 1) if shift else tile
    gain1, bias1, gain2, bias2 = [jnp.concatenate([a[i : i + 1] for a in acc_n], axis=1) for i in range(4)]
    gain3, bias3 = [jnp.concatenate([a[i : i + 1] for a in acc_w], axis=1) for i in (4, 5)]
    inv_count = 1.0 / count
    inv_n = jnp.concatenate([inv_count] * nar_tiles, axis=1)
    inv_w = jnp.concatenate([inv_count] * wide_tiles, axis=1)

    def send_sums(buf, index, first, second):
        tiles = first.shape[1] // LANES
        first = jnp.sum(first, axis=0, keepdims=True)
        second = jnp.sum(second, axis=0, keepdims=True)
        for i in range(tiles):
            buf[me, i : i + 1, :] = first[:, LANES * i : LANES * (i + 1)]
            buf[me, tiles + i : tiles + i + 1, :] = second[:, LANES * i : LANES * (i + 1)]
        gather_to_all(buf, index)

    def get_sums(buf, index):
        total = arrived(buf, index)
        tiles = total.shape[0] // 2
        return rows_to_vec(total, 0, tiles), rows_to_vec(total, tiles, tiles)

    def moments(buf, index, inv):
        total, squares = get_sums(buf, index)
        mean = total * inv
        var = squares * inv - mean * mean
        return mean, lax.rsqrt(var + EPS)

    zero_n = jnp.zeros((8, narrow), F32)

    grads = (
        (gr_ref, gr_core, gr_got, gr_fin),
        (gs_ref, gs_core, gs_got, gs_fin),
        (ge_ref, ge_core, ge_got, ge_fin),
    )
    lines = clips // 2
    line_me = lax.div(clip, 2)
    peers = frames * lines

    def scatter_cores(index):
        full, pair, _, _ = grads[index]
        half = pair.shape[1]
        view = full.reshape(frames, 2 * half, full.shape[1])
        theirs = pl.ds(pl.multiple_of((1 - core) * half, half), half)
        return pltpu.make_async_remote_copy(
            src_ref=view.at[:, theirs],
            dst_ref=pair,
            send_sem=rs_send.at[index, 0],
            recv_sem=rs_recv.at[index, 0],
            device_id=partner,
            device_id_type=MESH,
        )

    def scatter_chips(index):
        full, pair, got, _ = grads[index]
        scatter_cores(index).wait()
        half, width = pair.shape[1], pair.shape[2]
        mine = pl.ds(pl.multiple_of(core * half, half), half)
        view = full.reshape(frames, 2 * half, width)

        def add(f, carry):
            pair[f] = (pair[f].astype(F32) + view[f, mine, :].astype(F32)).astype(BF16)
            return carry

        lax.fori_loop(0, frames, add, 0)
        cut = width // lines
        slot_me = line_me * frames + frame

        def block(line, owner):
            return pair.at[owner, :, pl.ds(pl.multiple_of(line * cut, LANES), cut)]

        def send(k, carry):
            line = lax.rem(line_me + lax.div(k, frames), lines)
            owner = lax.rem(frame + lax.rem(k, frames), frames)
            pltpu.make_async_remote_copy(
                src_ref=block(line, owner),
                dst_ref=got.at[slot_me],
                send_sem=rs_send.at[index, 1],
                recv_sem=rs_recv.at[index, 1],
                device_id=(line * 2 + core, owner),
                device_id_type=MESH,
            ).start()
            return carry

        lax.fori_loop(1, peers, send, 0)
        own = pltpu.make_async_copy(block(line_me, frame), got.at[slot_me], rs_send.at[index, 2])
        own.start()
        own.wait()

    def gather_owners(index):
        _, pair, got, fin = grads[index]
        half, width = pair.shape[1], pair.shape[2]
        cut = width // lines
        most = got.at[pl.ds(0, peers - 1)]
        pltpu.make_async_copy(most, most, rs_recv.at[index, 1]).wait()
        pltpu.make_async_copy(most, most, rs_send.at[index, 1]).wait()
        spot = fin.at[
            pl.ds(pl.multiple_of(core * half, half), half), pl.ds(pl.multiple_of(line_me * cut, LANES), cut)
        ]
        spot[...] = jnp.sum(got[...].astype(F32), axis=0).astype(BF16)

        def send(k, carry):
            pltpu.make_async_remote_copy(
                src_ref=spot,
                dst_ref=spot,
                send_sem=rs_send.at[index, 2],
                recv_sem=rs_recv.at[index, 2],
                device_id=(lax.rem(clip + k, clips), frame),
                device_id_type=MESH,
            ).start()
            return carry

        lax.fori_loop(1, clips, send, 0)

    def finish_owners(index):
        _, _, got, fin = grads[index]
        most = got.at[pl.ds(0, clips - 1)]
        pltpu.make_async_copy(most, most, rs_recv.at[index, 2]).wait()
        pltpu.make_async_copy(most, most, rs_send.at[index, 2]).wait()
        return fin

    big = rows // 2

    def conv_one(i, carry):
        at = pl.ds(pl.multiple_of(i * big, big), big)
        v = dot(xm[at, :], wr[...])
        pre1[at, :] = v
        return carry[0] + part_sum(v), carry[1] + part_sum(v * v)

    sums = lax.fori_loop(0, 2, conv_one, (zero_n, zero_n))
    send_sums(st1, 1, *sums)
    weight_pass(1)
    mean1, inv1 = moments(st1, 1, inv_n)
    scale1 = inv1 * gain1
    offset1 = bias1 - mean1 * scale1

    def both(v):
        return jnp.concatenate([v] * nar_tiles, axis=1)

    def act_one(i, carry):
        at = block_at(i)
        z = pre1[at, :] * scale1 + offset1
        s = sigmoid(z)
        m = both(mask[at, :])
        ms = m * s
        spad[1, pl.ds(pl.multiple_of(i * BLOCK + pad, 8), BLOCK), :] = ms * z
        slope1[at, :] = ms * (1.0 + z * (1.0 - s))
        return carry

    lax.fori_loop(0, blocks, act_one, 0)

    def spread():
        def shifted(i, carry):
            at = block_at(i)
            v = spad[1, pl.ds(pl.multiple_of(i * BLOCK + pad - 8, 8), BLOCK + 16), :]
            here = pl.ds(pl.multiple_of(i * BLOCK + pad, 8), BLOCK)
            spad[0, here, :] = pltpu.roll(v, 2, 0)[8 : 8 + BLOCK] * both(left_ok[at, :])
            spad[2, here, :] = pltpu.roll(v, BLOCK + 14, 0)[8 : 8 + BLOCK] * both(right_ok[at, :])
            return carry

        lax.fori_loop(0, blocks, shifted, 0)

    def gather_nine(flip):
        def step(i, carry):
            at = block_at(i)
            for tap in range(9):
                row_off, col_off = (tap // 3, tap % 3) if not flip else (2 - tap // 3, 2 - tap % 3)
                src = pl.ds(pl.multiple_of(i * BLOCK + pad * row_off, 8), BLOCK)
                nine[at, narrow * tap : narrow * (tap + 1)] = spad[col_off, src, :].astype(BF16)
            return carry

        lax.fori_loop(0, blocks, step, 0)

    spread()
    gather_nine(False)
    weight_wait(1)

    def conv_two(i, carry):
        at = pl.ds(pl.multiple_of(i * big, big), big)
        v = dot(nine[at, :], ws[...].reshape(9 * narrow, narrow))
        pre2[at, :] = v
        mv = both(mask[at, :]) * v
        return carry[0] + part_sum(mv), carry[1] + part_sum(mv * v)

    sums = lax.fori_loop(0, 2, conv_two, (zero_n, zero_n))
    send_sums(st2, 2, *sums)
    weight_pass(2)
    weight_wait(2)
    wet[...] = we[...].T
    wrt[...] = wr[...].T
    mean2, inv2 = moments(st2, 2, inv_n)
    scale2 = inv2 * gain2
    offset2 = bias2 - mean2 * scale2

    def act_two(i, carry):
        at = block_at(i)
        z = pre2[at, :] * scale2 + offset2
        s = sigmoid(z)
        ms = both(mask[at, :]) * s
        act2[at, :] = (ms * z).astype(BF16)
        slope2[at, :] = ms * (1.0 + z * (1.0 - s))
        return carry

    lax.fori_loop(0, blocks, act_two, 0)

    zero_w = jnp.zeros((8, channels), F32)

    def conv_three(i, carry):
        at = block_at(i)
        v = dot(act2[at, :], we[...])
        pre3[at, :] = v
        return carry[0] + part_sum(v), carry[1] + part_sum(v * v)

    sums = lax.fori_loop(0, blocks, conv_three, (zero_w, zero_w))
    send_sums(st3, 3, *sums)
    for tap in range(9):
        wst[narrow * tap : narrow * (tap + 1), :] = ws[tap].T
    pltpu.make_async_copy(cs, cs, local_sem.at[1]).wait()
    mean3, inv3 = moments(st3, 3, inv_w)
    scale3 = inv3 * gain3
    offset3 = bias3 - mean3 * scale3

    def finish(i, carry):
        at = block_at(i)
        m = mask[at, :]
        first, second = [], []
        for j in range(wide_tiles):
            lanes = slice(LANES * j, LANES * (j + 1))
            p = pre3[at, lanes]
            t = p * scale3[:, lanes] + offset3[:, lanes] + xm[at, lanes].astype(F32)
            s = sigmoid(t)
            ms = m * s
            os_rows[j, at, :] = (ms * t).astype(BF16)
            g = cs_rows[j, at, :].astype(F32) * (ms * (1.0 + t * (1.0 - s)))
            gt[at, lanes] = g
            first.append(part_sum(g))
            second.append(part_sum(g * ((p - mean3[:, lanes]) * inv3[:, lanes])))
        return carry[0] + jnp.concatenate(first, axis=1), carry[1] + jnp.concatenate(second, axis=1)

    sums = lax.fori_loop(0, blocks, finish, (zero_w, zero_w))
    send_sums(st4, 4, *sums)
    for j in range(wide_tiles):
        lanes = pl.ds(LANES * j, LANES)
        pltpu.make_async_copy(os.at[j], out_hbm.at[:, :, lanes], out_sem.at[0]).start()
    shift3, slope_gain3 = get_sums(st4, 4)

    def back_terms(scale, inv, mean, shift_sum, gain_sum, inv_cnt):
        along = scale * inv * gain_sum * inv_cnt
        return along, scale * shift_sum * inv_cnt - mean * along

    along3, flat3 = back_terms(scale3, inv3, mean3, shift3, slope_gain3, inv_w)

    def back_three(i, carry):
        at = block_at(i)
        m = mask[at, :]
        for j in range(wide_tiles):
            lanes = slice(LANES * j, LANES * (j + 1))
            g = gt[at, lanes] * scale3[:, lanes] - pre3[at, lanes] * along3[:, lanes] - m * flat3[:, lanes]
            gp3[at, lanes] = g.astype(BF16)
        return carry

    lax.fori_loop(0, blocks, back_three, 0)

    def back_expand(i, carry):
        at = pl.ds(pl.multiple_of(i * big, big), big)
        d = dot(gp3[at, :], wet[...]) * slope2[at, :]
        dz[at, :] = d
        return carry[0] + part_sum(d), carry[1] + part_sum(d * ((pre2[at, :] - mean2) * inv2))

    sums = lax.fori_loop(0, 2, back_expand, (zero_n, zero_n))
    send_sums(st5, 5, *sums)

    def grad_expand(i, carry):
        lanes = pl.ds(pl.multiple_of(i * 256, 256), 256)
        ge_ref[:, lanes] = dot_tn(act2[...], gp3[:, lanes]).astype(BF16)
        return carry

    lax.fori_loop(0, channels // 256, grad_expand, 0)
    if own_gather:
        scatter_cores(2).start()
    shift2, slope_gain2 = get_sums(st5, 5)
    along2, flat2 = back_terms(scale2, inv2, mean2, shift2, slope_gain2, inv_n)

    def back_two(i, carry):
        at = block_at(i)
        here = pl.ds(pl.multiple_of(i * BLOCK + pad, 8), BLOCK)
        act2[at, :] = spad[1, here, :].astype(BF16)
        m = both(mask[at, :])
        spad[1, here, :] = dz[at, :] * scale2 - m * (pre2[at, :] * along2 + flat2)
        return carry

    lax.fori_loop(0, blocks, back_two, 0)
    spread()
    gather_nine(True)

    def back_spatial(i, carry):
        at = pl.ds(pl.multiple_of(i * big, big), big)
        d = dot(nine[at, :], wst[...]) * slope1[at, :]
        dz[at, :] = d
        return carry[0] + part_sum(d), carry[1] + part_sum(d * ((pre1[at, :] - mean1) * inv1))

    sums = lax.fori_loop(0, 2, back_spatial, (zero_n, zero_n))
    send_sums(st6, 6, *sums)

    def grad_spatial(i, carry):
        lanes = pl.ds(pl.multiple_of(i * narrow, narrow), narrow)
        gs_ref[:, lanes] = dot_tn(act2[...], nine[:, lanes]).astype(BF16)
        return carry

    lax.fori_loop(0, 9, grad_spatial, 0)
    if own_gather:
        scatter_cores(1).start()
        scatter_chips(2)
        scatter_chips(1)
    shift1, slope_gain1 = get_sums(st6, 6)
    along1, flat1 = back_terms(scale1, inv1, mean1, shift1, slope_gain1, inv_n)

    def back_one(i, carry):
        at = block_at(i)
        g = dz[at, :] * scale1 - both(mask[at, :]) * (pre1[at, :] * along1 + flat1)
        gp1[at, :] = g.astype(BF16)
        return carry

    lax.fori_loop(0, blocks, back_one, 0)

    def grad_reduce(i, carry):
        lanes = pl.ds(pl.multiple_of(i * 256, 256), 256)
        gr_ref[lanes, :] = dot_tn(xm[:, lanes], gp1[...]).astype(BF16)
        return carry

    lax.fori_loop(0, channels // 256, grad_reduce, 0)
    if own_gather:
        scatter_cores(0).start()
    pltpu.make_async_copy(os, os, out_sem.at[0]).wait()

    def grad_in(i, carry):
        at = block_at(i)
        m = mask[at, :]
        back = dot(gp1[at, :], wrt[...])
        for j in range(wide_tiles):
            lanes = slice(LANES * j, LANES * (j + 1))
            os_rows[j, at, :] = (m * back[:, lanes] + gt[at, lanes]).astype(BF16)
        return carry

    lax.fori_loop(0, blocks, grad_in, 0)
    for j in range(wide_tiles):
        lanes = pl.ds(LANES * j, LANES)
        pltpu.make_async_copy(os.at[j], gin_hbm.at[:, :, lanes], out_sem.at[1]).start()

    def own_part(ref, v):
        width = ref.shape[0]
        spot = frame * width
        tile = jnp.zeros((1, LANES), F32)
        for t in range(v.shape[1] // LANES):
            tile = jnp.where(lax.div(spot, LANES) == t, v[:, LANES * t : LANES * (t + 1)], tile)
        tile = pltpu.roll(jnp.concatenate([tile] * 8, axis=0), lax.rem(LANES - lax.rem(spot, LANES), LANES), 1)
        ref[...] = tile[0, 0:width]

    own_part(vec1_gain, slope_gain1)
    own_part(vec1_shift, shift1)
    own_part(vec2_gain, slope_gain2)
    own_part(vec2_shift, shift2)
    own_part(vec3_gain, slope_gain3)
    own_part(vec3_shift, shift3)

    if own_gather:
        scatter_chips(0)
        for index in (2, 1, 0):
            gather_owners(index)
        ge_out[...] = finish_owners(2)[...].astype(F32)
        fin = finish_owners(1)
        for tap in range(9):
            gs_out[tap] = fin[:, narrow * tap : narrow * (tap + 1)].astype(F32)
        gr_out[...] = finish_owners(0)[...].astype(F32)
    else:
        gr_out[...] = gr_ref[...]
        gs_out[...] = gs_ref[...]
        ge_out[...] = ge_ref[...]
    pltpu.make_async_copy(os, os, out_sem.at[1]).wait()


def on_device(
    dims,
    x_in,
    cotangent,
    w_reduce,
    w_spatial,
    w_expand,
    gain_one,
    shift_one,
    gain_two,
    shift_two,
    gain_three,
    shift_three,
    bucket,
    frame_count,
):
    clips, frames = dims
    slots, side, _, channels = x_in.shape
    narrow = w_reduce.shape[1]
    pixels = side * side
    rows = pixels * slots
    tiles = channels // LANES
    devices = clips * frames
    own_gather = all(n % 32 == 0 for n in (w_reduce.shape[0], w_spatial.shape[2], w_expand.shape[0]))
    w_spatial = w_spatial.reshape(9, -1, narrow)
    if not own_gather:
        w_reduce = lax.all_gather(w_reduce, "frame", axis=0, tiled=True)
        w_spatial = lax.all_gather(w_spatial, "frame", axis=1, tiled=True)
        w_expand = lax.all_gather(w_expand, "frame", axis=0, tiled=True)

    def by_pixel(v):
        return jnp.transpose(v, (1, 2, 0, 3)).reshape(pixels, slots, channels)

    any_spec = pl.BlockSpec(memory_space=pl.ANY)
    vmem = pl.BlockSpec(memory_space=pltpu.VMEM)
    smem = pl.BlockSpec(memory_space=pltpu.SMEM)
    big = jax.ShapeDtypeStruct((pixels, slots, channels), BF16)
    staged = pltpu.VMEM((tiles, pixels, slots, LANES), BF16)
    narrow_f32 = pltpu.VMEM((rows, narrow), F32)
    wide_f32 = pltpu.VMEM((rows, channels), F32)
    lanes_f32 = pltpu.VMEM((rows, LANES), F32)

    def stats(count):
        return pltpu.VMEM((devices, count, LANES), F32)

    def pieces(part, width, lead):
        half, lines = part // 2, clips // 2
        if lead == 0:
            return pltpu.VMEM((frames, half, width), BF16)
        if lead == 1:
            return pltpu.VMEM((frames * lines, half, width // lines), BF16)
        return pltpu.VMEM((part, width), BF16)

    if own_gather:
        parts = ((channels // frames, narrow), (narrow // frames, 9 * narrow), (narrow // frames, channels))
        grad_shapes = (
            jax.ShapeDtypeStruct((channels // frames, narrow), F32),
            jax.ShapeDtypeStruct((9, narrow // frames, narrow), F32),
            jax.ShapeDtypeStruct((narrow // frames, channels), F32),
        )
    else:
        parts = ((32, 256),) * 3
        grad_shapes = (
            jax.ShapeDtypeStruct((channels, narrow), BF16),
            jax.ShapeDtypeStruct((narrow, 9 * narrow), BF16),
            jax.ShapeDtypeStruct((narrow, channels), BF16),
        )
    piece_scratch = [pieces(part, width, lead) for lead in range(3) for part, width in parts]

    out, gin, gr, gs, ge, *vectors = pl.pallas_call(
        functools.partial(block_kernel, (clips, frames, side, own_gather)),
        out_shape=(
            big,
            big,
            *grad_shapes,
            *(jax.ShapeDtypeStruct((narrow // frames,), F32),) * 4,
            *(jax.ShapeDtypeStruct((channels // frames,), F32),) * 2,
        ),
        in_specs=[any_spec] * 5 + [vmem] * 6 + [smem] * 2,
        out_specs=(any_spec, any_spec) + (vmem,) * 9,
        scratch_shapes=[
            staged,
            staged,
            staged,
            pltpu.VMEM((rows, channels), BF16),
            lanes_f32,
            lanes_f32,
            lanes_f32,
            pltpu.VMEM((channels, narrow), BF16),
            pltpu.VMEM((9, narrow, narrow), BF16),
            pltpu.VMEM((narrow, channels), BF16),
            pltpu.VMEM((9 * narrow, narrow), BF16),
            pltpu.VMEM((channels, narrow), BF16),
            pltpu.VMEM((narrow, channels), BF16),
            narrow_f32,
            narrow_f32,
            narrow_f32,
            narrow_f32,
            narrow_f32,
            pltpu.VMEM((3, rows + 4 * side, narrow), F32),
            pltpu.VMEM((rows, narrow), BF16),
            pltpu.VMEM((rows, 9 * narrow), BF16),
            wide_f32,
            wide_f32,
            pltpu.VMEM((rows, channels), BF16),
            pltpu.VMEM((rows, narrow), BF16),
            stats(8),
            stats(2 * narrow // LANES),
            stats(2 * narrow // LANES),
            stats(2 * tiles),
            stats(2 * tiles),
            stats(2 * narrow // LANES),
            stats(2 * narrow // LANES),
            pltpu.SemaphoreType.DMA((5,)),
            pltpu.SemaphoreType.DMA((3, frames)),
            pltpu.SemaphoreType.DMA((3, frames)),
            pltpu.SemaphoreType.DMA((3, frames)),
            pltpu.SemaphoreType.DMA((3, frames)),
            pltpu.SemaphoreType.DMA((7,)),
            pltpu.SemaphoreType.DMA((7,)),
            pltpu.SemaphoreType.DMA((2,)),
            pltpu.VMEM((channels, narrow), BF16),
            pltpu.VMEM((narrow, 9 * narrow), BF16),
            pltpu.VMEM((narrow, channels), BF16),
            *piece_scratch,
            pltpu.SemaphoreType.DMA((3, 3)),
            pltpu.SemaphoreType.DMA((3, 3)),
        ],
        compiler_params=pltpu.CompilerParams(
            collective_id=0, has_side_effects=True, vmem_limit_bytes=58 * 1024 * 1024
        ),
    )(
        by_pixel(x_in),
        by_pixel(cotangent),
        w_reduce,
        w_spatial,
        w_expand,
        gain_one,
        shift_one,
        gain_two,
        shift_two,
        gain_three,
        shift_three,
        bucket,
        frame_count,
    )

    def by_frame(v):
        return jnp.transpose(v.reshape(side, side, slots, channels), (2, 0, 1, 3))

    def owned(v):
        part = lax.psum_scatter(v, "frame", scatter_dimension=0, tiled=True)
        return lax.psum(part, "clip").astype(F32)

    if not own_gather:
        gr, gs, ge = owned(gr), owned(gs), owned(ge)
        gs = gs.reshape(-1, 9, narrow).transpose(1, 0, 2)
    return (by_frame(out), by_frame(gin), gr, gs.reshape(3, 3, -1, narrow), ge, *vectors)


def solution(mesh):
    by_device = P(("clip", "frame"))
    shard = P("frame")
    spatial = P(None, None, "frame", None)
    return jax.shard_map(
        functools.partial(on_device, (mesh.shape["clip"], mesh.shape["frame"])),
        mesh=mesh,
        in_specs=(by_device, by_device, shard, spatial) + (shard,) * 7 + (by_device, by_device),
        out_specs=(by_device, by_device, shard, spatial) + (shard,) * 7,
        check_vma=False,
    )
```

```python
import functools

import jax
import jax.numpy as jnp
from jax import lax
from jax.experimental import pallas as pl
from jax.experimental.pallas import tpu as pltpu
from jax.sharding import PartitionSpec as P

SMALL_SIDE = 14
EPS = 1e-05
LANES = 128
BLOCK = 80
MESH = pl.DeviceIdType.MESH
X_FIRST = (False, True, False, True, True)
F32 = jnp.float32
BF16 = jnp.bfloat16


def sigmoid(v):
    return 0.5 * jnp.tanh(0.5 * v) + 0.5


def part_sum(v):
    rows, width = v.shape
    return jnp.sum(v.reshape(rows // 8, 8, width), axis=0)


def dot(a, b):
    return jnp.dot(a, b, preferred_element_type=F32)


def rows_to_vec(tile, first, count):
    return jnp.concatenate([tile[first + i : first + i + 1] for i in range(count)], axis=1)


def block_kernel(
    dims,
    x_hbm,
    ct_hbm,
    wr_hbm,
    ws_hbm,
    we_hbm,
    g1_ref,
    b1_ref,
    g2_ref,
    b2_ref,
    g3_ref,
    b3_ref,
    bucket_ref,
    count_ref,
    out_hbm,
    gin_hbm,
    gr_out,
    gs_out,
    ge_out,
    vec1_gain,
    vec1_shift,
    vec2_gain,
    vec2_shift,
    vec3_gain,
    vec3_shift,
    xs,
    cs,
    os,
    x_rows,
    ct_rows,
    out_rows,
    xm,
    xt,
    a1t,
    a2t,
    mask,
    left_ok,
    right_ok,
    wr,
    ws,
    we,
    wst,
    wet,
    wrt,
    pre1,
    slope1,
    pre2,
    slope2,
    dz,
    spad,
    act2,
    nine,
    pre3,
    gt,
    gp3,
    gp1,
    par,
    counts,
    st1,
    st2,
    st3,
    st4,
    st5,
    st6,
    local_sem,
    wsend,
    wrecv,
    st_send,
    st_recv,
    out_sem,
    rs_send,
    rs_recv,
    *unit_refs,
):
    clips, frames, side, own_gather = dims
    units = len(X_FIRST)
    full_refs, pair_refs, mid_refs, got_refs, fin_refs = [unit_refs[units * i : units * (i + 1)] for i in range(5)]
    gr_ref, *gs_refs, ge_ref = full_refs
    devices = clips * frames
    clip = lax.axis_index("clip")
    frame = lax.axis_index("frame")
    me = clip * frames + frame
    core = lax.rem(clip, 2)
    partner = (clip + 1 - 2 * core, frame)
    rows = xm.shape[0]
    channels = xm.shape[1]
    narrow = wr.shape[1]
    wide_tiles = channels // LANES
    nar_tiles = narrow // LANES
    blocks = rows // BLOCK
    pad = 2 * side

    def other(k):
        return (lax.rem(clip + lax.div(k, frames), clips), lax.rem(frame + lax.rem(k, frames), frames))

    for j in range(wide_tiles):
        lanes = pl.ds(LANES * j, LANES)
        pltpu.make_async_copy(x_hbm.at[:, :, lanes], xs.at[j], local_sem.at[0]).start()
    if own_gather:
        part_r = wr_hbm.shape[0]
        part_s = ws_hbm.shape[1]
        part_e = we_hbm.shape[0]
        own_r = wr.at[pl.ds(pl.multiple_of(frame * part_r, part_r), part_r)]
        own_s = ws.at[:, pl.ds(pl.multiple_of(frame * part_s, part_s), part_s)]
        own_e = we.at[pl.ds(pl.multiple_of(frame * part_e, part_e), part_e)]
    else:
        own_r, own_s, own_e = wr, ws, we
    own_copies = [
        pltpu.make_async_copy(wr_hbm, own_r, local_sem.at[2]),
        pltpu.make_async_copy(ws_hbm, own_s, local_sem.at[3]),
        pltpu.make_async_copy(we_hbm, own_e, local_sem.at[4]),
    ]
    for copy in own_copies:
        copy.start()
    for j in range(wide_tiles):
        lanes = pl.ds(LANES * j, LANES)
        pltpu.make_async_copy(ct_hbm.at[:, :, lanes], cs.at[j], local_sem.at[1]).start()

    def copies_in(staged, index):
        return pltpu.make_async_copy(staged, staged, local_sem.at[index])

    def to_rows(staged, native, index):
        return pltpu.make_async_copy(staged.reshape(wide_tiles, rows, LANES), native, local_sem.at[index])

    barrier = pltpu.get_barrier_semaphore()

    def greet(k, carry):
        pl.semaphore_signal(barrier, inc=1, device_id=other(k), device_id_type=MESH)
        return carry

    lax.fori_loop(1, devices, greet, 0)

    row_id = lax.broadcasted_iota(jnp.int32, (rows, LANES), 0)
    pixel = row_id >> 1
    slot = row_id & 1
    line = (pixel * 3277) >> 16
    col = pixel - line * side
    extent = [jnp.where(bucket_ref[f] == 0, SMALL_SIDE, side) for f in range(2)]
    limit = [jnp.where(count_ref[0] > f, extent[f], 0) for f in range(2)]
    bound = jnp.where(slot == 0, limit[0], limit[1])
    live = ((line < bound) & (col < bound)).astype(F32)
    mask[...] = live
    left_ok[...] = (col >= 1).astype(F32)
    right_ok[...] = (col <= side - 2).astype(F32)

    par[frame] = jnp.zeros((8, LANES), F32)
    for i, ref in enumerate((g1_ref, b1_ref, g2_ref, b2_ref, g3_ref, b3_ref)):
        width = ref.shape[0]
        par[frame, i : i + 1, 0:width] = ref[...].astype(F32).reshape(1, width)
    counts[me] = jnp.sum(live, axis=0, keepdims=True)

    copies_in(xs, 0).wait()
    to_rows(xs, x_rows, 0).start()
    to_rows(xs, x_rows, 0).wait()

    def block_at(i):
        return pl.ds(pl.multiple_of(i * BLOCK, BLOCK), BLOCK)

    def mask_in(i, carry):
        at = block_at(i)
        m = mask[at, :].astype(BF16)
        for j in range(wide_tiles):
            xm[at, LANES * j : LANES * (j + 1)] = x_rows[j, at, :] * m
        return carry

    lax.fori_loop(0, blocks, mask_in, 0)
    edge = jnp.zeros((3, pad, narrow), F32)
    spad[:, 0:pad, :] = edge
    spad[:, pad + rows : 2 * pad + rows, :] = edge
    for copy in own_copies:
        copy.wait()

    pl.semaphore_wait(barrier, devices - 1)

    def gather_to_all(buf, index):
        for a in range(clips):
            to_clip = lax.rem(clip + a, clips)

            def send(b, carry):
                pltpu.make_async_remote_copy(
                    src_ref=buf.at[me],
                    dst_ref=buf.at[me],
                    send_sem=st_send.at[index],
                    recv_sem=st_recv.at[index],
                    device_id=(to_clip, lax.rem(frame + b, frames)),
                    device_id_type=MESH,
                ).start()
                return carry

            lax.fori_loop(0 if a else 1, frames, send, 0)

    def arrived(buf, index):
        most = buf.at[pl.ds(0, devices - 1)]
        pltpu.make_async_copy(most, most, st_recv.at[index]).wait()
        pltpu.make_async_copy(most, most, st_send.at[index]).wait()
        return jnp.sum(buf[...], axis=0)

    across = lax.rem(frame, 2)
    along = lax.div(frame, 2)
    depth = frames // 2
    x_peer = (clip, along * 2 + 1 - across)

    def owner_at(d, side_x):
        return lax.rem(along - d + depth, depth) * 2 + side_x

    if own_gather:

        def halves(ref, axis, part):
            half = part // 2

            def view(owner):
                at = pl.ds(pl.multiple_of(owner * part + core * half, half), half)
                return ref.at[at] if axis == 0 else ref.at[:, at]

            return view

        views = (halves(wr, 0, part_r), halves(ws, 1, part_s), halves(we, 0, part_e))

        def weight_copy(index, hop, d, owner, target):
            part = views[index](owner)
            return pltpu.make_async_remote_copy(
                src_ref=part,
                dst_ref=part,
                send_sem=wsend.at[index, hop, d],
                recv_sem=wrecv.at[index, hop, d],
                device_id=target,
                device_id_type=MESH,
            )

        def along_z(index):
            for d in range(1, depth):
                target = (clip, lax.rem(along + d, depth) * 2 + across)
                weight_copy(index, 0, d, frame, target).start()

        def along_x(index, d):
            if d:
                weight_copy(index, 0, d, owner_at(d, across), x_peer).wait_recv()
            weight_copy(index, 1, d, owner_at(d, across), x_peer).start()

        def to_core(index, d):
            if d:
                weight_copy(index, 2, d, owner_at(d, across), partner).start()

        def to_core_late(index, d):
            owner = owner_at(d, 1 - across)
            weight_copy(index, 1, d, owner, partner).wait_recv()
            weight_copy(index, 3, d, owner, partner).start()

        def weight_ready(index):
            for d in range(depth):
                if d:
                    weight_copy(index, 2, d, owner_at(d, across), partner).wait_recv()
                weight_copy(index, 3, d, owner_at(d, 1 - across), partner).wait_recv()

        def weight_sent(index):
            for d in range(depth):
                if d:
                    weight_copy(index, 0, d, frame, partner).wait_send()
                    weight_copy(index, 2, d, frame, partner).wait_send()
                weight_copy(index, 1, d, frame, partner).wait_send()
                weight_copy(index, 3, d, frame, partner).wait_send()

    else:

        def nothing(*args):
            pass

        along_z = along_x = to_core = to_core_late = weight_ready = weight_sent = nothing

    def send_params():
        def send(b, carry):
            pltpu.make_async_remote_copy(
                src_ref=par.at[frame],
                dst_ref=par.at[frame],
                send_sem=st_send.at[0],
                recv_sem=st_recv.at[0],
                device_id=(clip, lax.rem(frame + b, frames)),
                device_id_type=MESH,
            ).start()
            return carry

        lax.fori_loop(1, frames, send, 0)

    along_z(0)
    along_x(0, 0)
    along_z(1)
    along_x(1, 0)
    gather_to_all(counts, 7)
    send_params()
    for d in range(1, depth):
        along_x(0, d)
        to_core(0, d)
    for d in range(depth):
        to_core_late(0, d)

    weight_ready(0)

    def send_sums(buf, index, first, second):
        tiles = first.shape[1] // LANES
        first = jnp.sum(first, axis=0, keepdims=True)
        second = jnp.sum(second, axis=0, keepdims=True)
        for i in range(tiles):
            buf[me, i : i + 1, :] = first[:, LANES * i : LANES * (i + 1)]
            buf[me, tiles + i : tiles + i + 1, :] = second[:, LANES * i : LANES * (i + 1)]
        gather_to_all(buf, index)

    def get_sums(buf, index):
        total = arrived(buf, index)
        tiles = total.shape[0] // 2
        return rows_to_vec(total, 0, tiles), rows_to_vec(total, tiles, tiles)

    def moments(buf, index, inv):
        total, squares = get_sums(buf, index)
        mean = total * inv
        var = squares * inv - mean * mean
        return mean, lax.rsqrt(var + EPS)

    zero_n = jnp.zeros((8, narrow), F32)

    lines = clips // 2
    line_me = lax.div(clip, 2)
    peers = frames
    y_peer = (lax.rem(clip + 2, clips), frame)

    def unit_copy(unit, stage, src, dst, target):
        return pltpu.make_async_remote_copy(
            src_ref=src,
            dst_ref=dst,
            send_sem=rs_send.at[unit, stage],
            recv_sem=rs_recv.at[unit, stage],
            device_id=target,
            device_id_type=MESH,
        )

    def columns(line, cut):
        return pl.ds(pl.multiple_of(line * cut, LANES), cut)

    def cores(unit):
        full, pair = full_refs[unit], pair_refs[unit]
        half = pair.shape[1]
        view = full.reshape(frames, 2 * half, full.shape[1])
        theirs = pl.ds(pl.multiple_of((1 - core) * half, half), half)
        return unit_copy(unit, 0, view.at[:, theirs], pair, partner)

    def near_copy(unit):
        pair, mid = pair_refs[unit], mid_refs[unit]
        half, width = pair.shape[1], pair.shape[2]
        if X_FIRST[unit]:
            return unit_copy(unit, 1, pair.reshape(depth, 2, half, width).at[:, 1 - across], mid, x_peer)
        return unit_copy(unit, 1, pair.at[:, :, columns(1 - line_me, width // lines)], mid, y_peer)

    def near(unit):
        full, pair = full_refs[unit], pair_refs[unit]
        cores(unit).wait()
        half = pair.shape[1]
        mine = pl.ds(pl.multiple_of(core * half, half), half)
        view = full.reshape(frames, 2 * half, full.shape[1])

        def add(f, carry):
            pair[f] = (pair[f].astype(F32) + view[f, mine, :].astype(F32)).astype(BF16)
            return carry

        lax.fori_loop(0, frames, add, 0)
        near_copy(unit).start()

    def far(unit):
        pair, mid, got = pair_refs[unit], mid_refs[unit], got_refs[unit]
        cut = pair.shape[2] // lines
        near_copy(unit).wait()

        def add(k, carry):
            own = pair[2 * k + across] if X_FIRST[unit] else pair[k, :, columns(line_me, cut)]
            mid[k] = (mid[k].astype(F32) + own.astype(F32)).astype(BF16)
            return carry

        lax.fori_loop(0, mid.shape[0], add, 0)
        if X_FIRST[unit]:
            slot_me = line_me * depth + along
            got[slot_me] = mid[along, :, columns(line_me, cut)]

            def send(k, carry):
                line = lax.rem(line_me + lax.div(k, depth), lines)
                deep = lax.rem(along + lax.rem(k, depth), depth)
                src = mid.at[deep, :, columns(line, cut)]
                unit_copy(unit, 2, src, got.at[slot_me], (line * 2 + core, deep * 2 + across)).start()
                return carry

        else:
            got[frame] = mid[frame]

            def send(k, carry):
                owner = lax.rem(frame + k, frames)
                unit_copy(unit, 2, mid.at[owner], got.at[frame], (clip, owner)).start()
                return carry

        lax.fori_loop(1, peers, send, 0)

    def owners(unit):
        got, fin = got_refs[unit], fin_refs[unit]
        half, cut = got.shape[1], got.shape[2]
        most = got.at[pl.ds(0, peers - 1)]
        unit_copy(unit, 2, most, most, partner).wait()
        spot = fin.at[pl.ds(pl.multiple_of(core * half, half), half), columns(line_me, cut)]
        spot[...] = jnp.sum(got[...].astype(F32), axis=0).astype(BF16)

        def send(k, carry):
            unit_copy(unit, 3, spot, spot, (lax.rem(clip + k, clips), frame)).start()
            return carry

        lax.fori_loop(1, clips, send, 0)

    def finished(unit):
        most = got_refs[unit].at[pl.ds(0, clips - 1)]
        unit_copy(unit, 3, most, most, partner).wait()
        return fin_refs[unit]

    big = rows // 2

    def conv_one(i, carry):
        at = pl.ds(pl.multiple_of(i * big, big), big)
        v = dot(xm[at, :], wr[...])
        pre1[at, :] = v
        return carry[0] + part_sum(v), carry[1] + part_sum(v * v)

    sums = lax.fori_loop(0, 2, conv_one, (zero_n, zero_n))
    send_sums(st1, 1, *sums)
    for d in range(1, depth):
        along_x(1, d)
        to_core(1, d)
    along_z(2)
    along_x(2, 0)
    for d in range(depth):
        to_core_late(1, d)
    xt[...] = xm[...].T

    most = par.at[pl.ds(0, frames - 1)]
    pltpu.make_async_copy(most, most, st_recv.at[0]).wait()
    pltpu.make_async_copy(most, most, st_send.at[0]).wait()
    part_n = g1_ref.shape[0]
    part_w = g3_ref.shape[0]
    acc_n = [jnp.zeros((8, LANES), F32) for _ in range(nar_tiles)]
    acc_w = [jnp.zeros((8, LANES), F32) for _ in range(wide_tiles)]
    for f in range(frames):
        tile = par[f]
        spot = f * part_n
        shift = spot % LANES
        acc_n[spot // LANES] += pltpu.roll(tile, shift, 1) if shift else tile
        spot = f * part_w
        shift = spot % LANES
        acc_w[spot // LANES] += pltpu.roll(tile, shift, 1) if shift else tile
    gain1, bias1, gain2, bias2 = [jnp.concatenate([a[i : i + 1] for a in acc_n], axis=1) for i in range(4)]
    gain3, bias3 = [jnp.concatenate([a[i : i + 1] for a in acc_w], axis=1) for i in (4, 5)]
    inv_count = 1.0 / arrived(counts, 7)
    inv_n = jnp.concatenate([inv_count] * nar_tiles, axis=1)
    inv_w = jnp.concatenate([inv_count] * wide_tiles, axis=1)

    mean1, inv1 = moments(st1, 1, inv_n)
    scale1 = inv1 * gain1
    offset1 = bias1 - mean1 * scale1

    def both(v):
        return jnp.concatenate([v] * nar_tiles, axis=1)

    def act_one(i, carry):
        at = block_at(i)
        z = pre1[at, :] * scale1 + offset1
        s = sigmoid(z)
        m = both(mask[at, :])
        ms = m * s
        spad[1, pl.ds(pl.multiple_of(i * BLOCK + pad, 8), BLOCK), :] = ms * z
        slope1[at, :] = ms * (1.0 + z * (1.0 - s))
        return carry

    lax.fori_loop(0, blocks, act_one, 0)

    def spread():
        def shifted(i, carry):
            at = block_at(i)
            v = spad[1, pl.ds(pl.multiple_of(i * BLOCK + pad - 8, 8), BLOCK + 16), :]
            here = pl.ds(pl.multiple_of(i * BLOCK + pad, 8), BLOCK)
            spad[0, here, :] = pltpu.roll(v, 2, 0)[8 : 8 + BLOCK] * both(left_ok[at, :])
            spad[2, here, :] = pltpu.roll(v, BLOCK + 14, 0)[8 : 8 + BLOCK] * both(right_ok[at, :])
            return carry

        lax.fori_loop(0, blocks, shifted, 0)

    def gather_nine(flip):
        def step(i, carry):
            at = block_at(i)
            for tap in range(9):
                row_off, col_off = (tap // 3, tap % 3) if not flip else (2 - tap // 3, 2 - tap % 3)
                src = pl.ds(pl.multiple_of(i * BLOCK + pad * row_off, 8), BLOCK)
                nine[at, narrow * tap : narrow * (tap + 1)] = spad[col_off, src, :].astype(BF16)
            return carry

        lax.fori_loop(0, blocks, step, 0)

    spread()
    gather_nine(False)
    weight_ready(1)
    for d in range(1, depth):
        along_x(2, d)
        to_core(2, d)

    def conv_two(i, carry):
        at = pl.ds(pl.multiple_of(i * big, big), big)
        v = dot(nine[at, :], ws[...].reshape(9 * narrow, narrow))
        pre2[at, :] = v
        mv = both(mask[at, :]) * v
        return carry[0] + part_sum(mv), carry[1] + part_sum(mv * v)

    sums = lax.fori_loop(0, 2, conv_two, (zero_n, zero_n))
    send_sums(st2, 2, *sums)
    wrt[...] = wr[...].T
    a1t[...] = spad[1, pad : pad + rows, :].astype(BF16).T
    for d in range(depth):
        to_core_late(2, d)

    mean2, inv2 = moments(st2, 2, inv_n)
    scale2 = inv2 * gain2
    offset2 = bias2 - mean2 * scale2

    def act_two(i, carry):
        at = block_at(i)
        z = pre2[at, :] * scale2 + offset2
        s = sigmoid(z)
        ms = both(mask[at, :]) * s
        act2[at, :] = (ms * z).astype(BF16)
        slope2[at, :] = ms * (1.0 + z * (1.0 - s))
        return carry

    lax.fori_loop(0, blocks, act_two, 0)

    weight_ready(2)
    zero_w = jnp.zeros((8, channels), F32)

    wide = 2 * BLOCK

    def conv_three(i, carry):
        at = pl.ds(pl.multiple_of(i * wide, wide), wide)
        v = dot(act2[at, :], we[...])
        pre3[at, :] = v
        return carry[0] + part_sum(v), carry[1] + part_sum(v * v)

    sums = lax.fori_loop(0, rows // wide, conv_three, (zero_w, zero_w))
    send_sums(st3, 3, *sums)
    for tap in range(9):
        wst[narrow * tap : narrow * (tap + 1), :] = ws[tap].T
    wet[...] = we[...].T
    a2t[...] = act2[...].T
    copies_in(cs, 1).wait()
    to_rows(cs, ct_rows, 1).start()
    to_rows(cs, ct_rows, 1).wait()
    mean3, inv3 = moments(st3, 3, inv_w)
    scale3 = inv3 * gain3
    offset3 = bias3 - mean3 * scale3

    def from_rows():
        return pltpu.make_async_copy(out_rows, os.reshape(wide_tiles, rows, LANES), out_sem.at[2])

    def send_out(ref, index):
        for j in range(wide_tiles):
            lanes = pl.ds(LANES * j, LANES)
            pltpu.make_async_copy(os.at[j], ref.at[:, :, lanes], out_sem.at[index]).start()

    def finish(i, carry):
        at = block_at(i)
        m = mask[at, :]
        first, second = [], []
        for j in range(wide_tiles):
            lanes = slice(LANES * j, LANES * (j + 1))
            p = pre3[at, lanes]
            t = p * scale3[:, lanes] + offset3[:, lanes] + xm[at, lanes].astype(F32)
            s = sigmoid(t)
            ms = m * s
            out_rows[j, at, :] = (ms * t).astype(BF16)
            g = ct_rows[j, at, :].astype(F32) * (ms * (1.0 + t * (1.0 - s)))
            gt[at, lanes] = g
            first.append(part_sum(g))
            second.append(part_sum(g * ((p - mean3[:, lanes]) * inv3[:, lanes])))
        return carry[0] + jnp.concatenate(first, axis=1), carry[1] + jnp.concatenate(second, axis=1)

    sums = lax.fori_loop(0, blocks, finish, (zero_w, zero_w))
    send_sums(st4, 4, *sums)
    from_rows().start()
    from_rows().wait()
    send_out(out_hbm, 0)
    shift3, slope_gain3 = get_sums(st4, 4)

    def back_terms(scale, inv, mean, shift_sum, gain_sum, inv_cnt):
        along = scale * inv * gain_sum * inv_cnt
        return along, scale * shift_sum * inv_cnt - mean * along

    along3, flat3 = back_terms(scale3, inv3, mean3, shift3, slope_gain3, inv_w)

    def back_three(i, carry):
        at = block_at(i)
        m = mask[at, :]
        for j in range(wide_tiles):
            lanes = slice(LANES * j, LANES * (j + 1))
            g = gt[at, lanes] * scale3[:, lanes] - pre3[at, lanes] * along3[:, lanes] - m * flat3[:, lanes]
            gp3[at, lanes] = g.astype(BF16)
        return carry

    lax.fori_loop(0, blocks, back_three, 0)

    def back_expand(i, carry):
        at = pl.ds(pl.multiple_of(i * big, big), big)
        d = dot(gp3[at, :], wet[...]) * slope2[at, :]
        dz[at, :] = d
        return carry[0] + part_sum(d), carry[1] + part_sum(d * ((pre2[at, :] - mean2) * inv2))

    sums = lax.fori_loop(0, 2, back_expand, (zero_n, zero_n))
    send_sums(st5, 5, *sums)

    def grad_expand(i, carry):
        lanes = pl.ds(pl.multiple_of(i * 256, 256), 256)
        ge_ref[:, lanes] = dot(a2t[...], gp3[:, lanes]).astype(BF16)
        return carry

    lax.fori_loop(0, channels // 256, grad_expand, 0)
    if own_gather:
        cores(4).start()
        near(4)

    shift2, slope_gain2 = get_sums(st5, 5)
    along2, flat2 = back_terms(scale2, inv2, mean2, shift2, slope_gain2, inv_n)

    def back_two(i, carry):
        at = block_at(i)
        here = pl.ds(pl.multiple_of(i * BLOCK + pad, 8), BLOCK)
        m = both(mask[at, :])
        spad[1, here, :] = dz[at, :] * scale2 - m * (pre2[at, :] * along2 + flat2)
        return carry

    lax.fori_loop(0, blocks, back_two, 0)
    spread()
    gather_nine(True)

    def back_spatial(i, carry):
        at = pl.ds(pl.multiple_of(i * big, big), big)
        d = dot(nine[at, :], wst[...]) * slope1[at, :]
        dz[at, :] = d
        return carry[0] + part_sum(d), carry[1] + part_sum(d * ((pre1[at, :] - mean1) * inv1))

    sums = lax.fori_loop(0, 2, back_spatial, (zero_n, zero_n))
    send_sums(st6, 6, *sums)

    if own_gather:
        far(4)

    def grad_spatial(row):
        wide_row = 3 * narrow
        gs_refs[row][...] = dot(a1t[...], nine[:, wide_row * row : wide_row * (row + 1)]).astype(BF16)
        if own_gather:
            cores(1 + row).start()

    grad_spatial(0)
    grad_spatial(1)
    if own_gather:
        near(1)
    grad_spatial(2)
    if own_gather:
        near(2)
        near(3)

    shift1, slope_gain1 = get_sums(st6, 6)
    along1, flat1 = back_terms(scale1, inv1, mean1, shift1, slope_gain1, inv_n)

    def back_one(i, carry):
        at = block_at(i)
        g = dz[at, :] * scale1 - both(mask[at, :]) * (pre1[at, :] * along1 + flat1)
        gp1[at, :] = g.astype(BF16)
        return carry

    lax.fori_loop(0, blocks, back_one, 0)

    def grad_reduce(i, carry):
        lanes = pl.ds(pl.multiple_of(i * 256, 256), 256)
        gr_ref[lanes, :] = dot(xt[lanes, :], gp1[...]).astype(BF16)
        return carry

    lax.fori_loop(0, channels // 256, grad_reduce, 0)
    if own_gather:
        cores(0).start()
        far(1)
    pltpu.make_async_copy(os, os, out_sem.at[0]).wait()

    def grad_in(i, carry):
        at = pl.ds(pl.multiple_of(i * wide, wide), wide)
        m = mask[at, :]
        back = dot(gp1[at, :], wrt[...])
        for j in range(wide_tiles):
            lanes = slice(LANES * j, LANES * (j + 1))
            out_rows[j, at, :] = (m * back[:, lanes] + gt[at, lanes]).astype(BF16)
        return carry

    lax.fori_loop(0, rows // wide, grad_in, 0)
    if own_gather:
        near(0)
        far(2)
    from_rows().start()
    from_rows().wait()
    send_out(gin_hbm, 1)

    def own_part(ref, v):
        width = ref.shape[0]
        spot = frame * width
        tile = jnp.zeros((1, LANES), F32)
        for t in range(v.shape[1] // LANES):
            tile = jnp.where(lax.div(spot, LANES) == t, v[:, LANES * t : LANES * (t + 1)], tile)
        tile = pltpu.roll(jnp.concatenate([tile] * 8, axis=0), lax.rem(LANES - lax.rem(spot, LANES), LANES), 1)
        ref[...] = tile[0, 0:width]

    own_part(vec1_gain, slope_gain1)
    own_part(vec1_shift, shift1)
    own_part(vec2_gain, slope_gain2)
    own_part(vec2_shift, shift2)
    own_part(vec3_gain, slope_gain3)
    own_part(vec3_shift, shift3)

    if own_gather:
        owners(4)
        far(3)
        owners(1)
        far(0)
        for unit in (2, 3, 0):
            owners(unit)
        ge_out[...] = finished(4)[...].astype(F32)
        for row in range(3):
            fin = finished(1 + row)
            for c in range(3):
                gs_out[3 * row + c] = fin[:, narrow * c : narrow * (c + 1)].astype(F32)
        gr_out[...] = finished(0)[...].astype(F32)
    else:
        gr_out[...] = gr_ref[...]
        for row in range(3):
            gs_out[:, 3 * narrow * row : 3 * narrow * (row + 1)] = gs_refs[row][...]
        ge_out[...] = ge_ref[...]
    for index in range(3):
        weight_sent(index)
    pltpu.make_async_copy(os, os, out_sem.at[1]).wait()


def deliver_kernel(count, *refs):
    sources, targets, staged, sems = refs[:count], refs[count : 2 * count], refs[2 * count : 3 * count], refs[3 * count]
    pieces = []
    for i in range(count):
        cuts = 4 if sources[i].shape[0] % 16 == 0 and len(sources[i].shape) == 3 else 1
        size = sources[i].shape[0] // cuts
        for c in range(cuts):
            pieces.append((i, pl.ds(c * size, size), len(pieces)))
    into = [pltpu.make_async_copy(sources[i].at[at], staged[i].at[at], sems.at[0, k]) for i, at, k in pieces]
    away = [pltpu.make_async_copy(staged[i].at[at], targets[i].at[at], sems.at[1, k]) for i, at, k in pieces]
    for copy in into:
        copy.start()
    for arrive, leave in zip(into, away):
        arrive.wait()
        leave.start()
    for copy in away:
        copy.wait()


def deliver(arrays):
    return pl.pallas_call(
        functools.partial(deliver_kernel, len(arrays)),
        out_shape=tuple(jax.ShapeDtypeStruct(a.shape, a.dtype) for a in arrays),
        in_specs=[pl.BlockSpec(memory_space=pl.ANY)] * len(arrays),
        out_specs=(pl.BlockSpec(memory_space=pl.ANY),) * len(arrays),
        scratch_shapes=[pltpu.VMEM(a.shape, a.dtype) for a in arrays] + [pltpu.SemaphoreType.DMA((2, 64))],
    )(*arrays)


def on_device(
    dims,
    x_in,
    cotangent,
    w_reduce,
    w_spatial,
    w_expand,
    gain_one,
    shift_one,
    gain_two,
    shift_two,
    gain_three,
    shift_three,
    bucket,
    frame_count,
):
    clips, frames = dims
    slots, side, _, channels = x_in.shape
    narrow = w_reduce.shape[1]
    pixels = side * side
    rows = pixels * slots
    tiles = channels // LANES
    devices = clips * frames
    own_gather = all(n % 32 == 0 for n in (w_reduce.shape[0], w_spatial.shape[2], w_expand.shape[0]))
    w_spatial = w_spatial.reshape(9, -1, narrow)
    if not own_gather:
        w_reduce = lax.all_gather(w_reduce, "frame", axis=0, tiled=True)
        w_spatial = lax.all_gather(w_spatial, "frame", axis=1, tiled=True)
        w_expand = lax.all_gather(w_expand, "frame", axis=0, tiled=True)

    def by_pixel(v):
        return jnp.transpose(v, (1, 2, 0, 3)).reshape(pixels, slots, channels)

    any_spec = pl.BlockSpec(memory_space=pl.ANY)
    vmem = pl.BlockSpec(memory_space=pltpu.VMEM)
    smem = pl.BlockSpec(memory_space=pltpu.SMEM)
    big = jax.ShapeDtypeStruct((pixels, slots, channels), BF16)
    staged = pltpu.VMEM((tiles, pixels, slots, LANES), BF16)
    native = pltpu.VMEM((tiles, rows, LANES), BF16)
    narrow_f32 = pltpu.VMEM((rows, narrow), F32)
    wide_f32 = pltpu.VMEM((rows, channels), F32)
    lanes_f32 = pltpu.VMEM((rows, LANES), F32)

    def stats(count):
        return pltpu.VMEM((devices, count, LANES), F32)

    if own_gather:
        grad_shapes = (
            jax.ShapeDtypeStruct((channels // frames, narrow), F32),
            jax.ShapeDtypeStruct((9, narrow // frames, narrow), F32),
            jax.ShapeDtypeStruct((narrow // frames, channels), F32),
        )
    else:
        grad_shapes = (
            jax.ShapeDtypeStruct((channels, narrow), BF16),
            jax.ShapeDtypeStruct((narrow, 9 * narrow), BF16),
            jax.ShapeDtypeStruct((narrow, channels), BF16),
        )
    wholes = ((channels, narrow), *(((narrow, 3 * narrow),) * 3), (narrow, channels))
    lines = clips // 2
    unit_scratch = [pltpu.VMEM(shape, BF16) for shape in wholes]
    if own_gather:
        cuts = [(height // frames // 2, width) for height, width in wholes]
        unit_scratch += [pltpu.VMEM((frames, half, width), BF16) for half, width in cuts]
        unit_scratch += [
            pltpu.VMEM((frames // 2, half, width) if x_first else (frames, half, width // lines), BF16)
            for (half, width), x_first in zip(cuts, X_FIRST)
        ]
        unit_scratch += [pltpu.VMEM((frames, half, width // lines), BF16) for half, width in cuts]
        unit_scratch += [pltpu.VMEM((2 * half, width), BF16) for half, width in cuts]

    out, gin, gr, gs, ge, *vectors = pl.pallas_call(
        functools.partial(block_kernel, (clips, frames, side, own_gather)),
        out_shape=(
            big,
            big,
            *grad_shapes,
            *(jax.ShapeDtypeStruct((narrow // frames,), F32),) * 4,
            *(jax.ShapeDtypeStruct((channels // frames,), F32),) * 2,
        ),
        in_specs=[any_spec] * 5 + [vmem] * 6 + [smem] * 2,
        out_specs=(any_spec, any_spec) + (vmem,) * 9,
        scratch_shapes=[
            staged,
            staged,
            staged,
            native,
            native,
            native,
            pltpu.VMEM((rows, channels), BF16),
            pltpu.VMEM((channels, rows), BF16),
            pltpu.VMEM((narrow, rows), BF16),
            pltpu.VMEM((narrow, rows), BF16),
            lanes_f32,
            lanes_f32,
            lanes_f32,
            pltpu.VMEM((channels, narrow), BF16),
            pltpu.VMEM((9, narrow, narrow), BF16),
            pltpu.VMEM((narrow, channels), BF16),
            pltpu.VMEM((9 * narrow, narrow), BF16),
            pltpu.VMEM((channels, narrow), BF16),
            pltpu.VMEM((narrow, channels), BF16),
            narrow_f32,
            narrow_f32,
            narrow_f32,
            narrow_f32,
            narrow_f32,
            pltpu.VMEM((3, rows + 4 * side, narrow), F32),
            pltpu.VMEM((rows, narrow), BF16),
            pltpu.VMEM((rows, 9 * narrow), BF16),
            wide_f32,
            wide_f32,
            pltpu.VMEM((rows, channels), BF16),
            pltpu.VMEM((rows, narrow), BF16),
            pltpu.VMEM((frames, 8, LANES), F32),
            stats(1),
            stats(2 * narrow // LANES),
            stats(2 * narrow // LANES),
            stats(2 * tiles),
            stats(2 * tiles),
            stats(2 * narrow // LANES),
            stats(2 * narrow // LANES),
            pltpu.SemaphoreType.DMA((5,)),
            pltpu.SemaphoreType.DMA((3, 4, frames // 2)),
            pltpu.SemaphoreType.DMA((3, 4, frames // 2)),
            pltpu.SemaphoreType.DMA((8,)),
            pltpu.SemaphoreType.DMA((8,)),
            pltpu.SemaphoreType.DMA((3,)),
            pltpu.SemaphoreType.DMA((5, 4)),
            pltpu.SemaphoreType.DMA((5, 4)),
            *unit_scratch,
        ],
        compiler_params=pltpu.CompilerParams(
            collective_id=0, has_side_effects=True, vmem_limit_bytes=58 * 1024 * 1024
        ),
    )(
        by_pixel(x_in),
        by_pixel(cotangent),
        w_reduce,
        w_spatial,
        w_expand,
        gain_one,
        shift_one,
        gain_two,
        shift_two,
        gain_three,
        shift_three,
        bucket,
        frame_count,
    )

    def by_frame(v):
        return jnp.transpose(v.reshape(side, side, slots, channels), (2, 0, 1, 3))

    def owned(v):
        part = lax.psum_scatter(v, "frame", scatter_dimension=0, tiled=True)
        return lax.psum(part, "clip").astype(F32)

    if not own_gather:
        gr, gs, ge = owned(gr), owned(gs), owned(ge)
        gs = gs.reshape(-1, 9, narrow).transpose(1, 0, 2)
    out, gin, gr, gs, ge, *vectors = deliver((out, gin, gr, gs, ge, *vectors))
    return (by_frame(out), by_frame(gin), gr, gs.reshape(3, 3, -1, narrow), ge, *vectors)


def solution(mesh):
    by_device = P(("clip", "frame"))
    shard = P("frame")
    spatial = P(None, None, "frame", None)
    return jax.shard_map(
        functools.partial(on_device, (mesh.shape["clip"], mesh.shape["frame"])),
        mesh=mesh,
        in_specs=(by_device, by_device, shard, spatial) + (shard,) * 7 + (by_device, by_device),
        out_specs=(by_device, by_device, shard, spatial) + (shard,) * 7,
        check_vma=False,
    )
```

```python
import functools

import jax
import jax.numpy as jnp
from jax import lax
from jax.experimental import pallas as pl
from jax.experimental.pallas import tpu as pltpu
from jax.sharding import PartitionSpec as P

SMALL_SIDE = 14
EPS = 1e-05
LANES = 128
BLOCK = 80
VMEM_BYTES = 52 * 1024 * 1024
MESH = pl.DeviceIdType.MESH
X_FIRST = (True, False, False, True, False, True)
F32 = jnp.float32
BF16 = jnp.bfloat16


def sigmoid(v):
    return 0.5 * jnp.tanh(0.5 * v) + 0.5


def part_sum(v):
    rows, width = v.shape
    return jnp.sum(v.reshape(rows // 8, 8, width), axis=0)


def dot(a, b):
    return jnp.dot(a, b, preferred_element_type=F32)


def rows_to_vec(tile, first, count):
    return jnp.concatenate([tile[first + i : first + i + 1] for i in range(count)], axis=1)


def block_kernel(
    dims,
    x_hbm,
    ct_hbm,
    wr_hbm,
    ws_hbm,
    we_hbm,
    g1_ref,
    b1_ref,
    g2_ref,
    b2_ref,
    g3_ref,
    b3_ref,
    bucket_ref,
    count_ref,
    out_ref,
    gin_ref,
    gr_out,
    gs_out,
    ge_out,
    vec1_gain,
    vec1_shift,
    vec2_gain,
    vec2_shift,
    vec3_gain,
    vec3_shift,
    xs,
    cs,
    x_rows,
    ct_rows,
    out_rows,
    xm,
    xt,
    a1t,
    a2t,
    mask,
    left_ok,
    right_ok,
    wr,
    ws,
    we,
    wst,
    wet,
    wrt,
    pre1,
    slope1,
    pre2,
    slope2,
    dz,
    spad,
    act2,
    nine,
    pre3,
    gt,
    gp3,
    gp1,
    par,
    counts,
    st1,
    st2,
    st3,
    st4,
    st5,
    st6,
    local_sem,
    wsend,
    wrecv,
    st_send,
    st_recv,
    out_sem,
    rs_send,
    rs_recv,
    *unit_refs,
):
    clips, frames, side, own_gather = dims
    units = len(X_FIRST)
    full_refs, pair_refs, mid_refs, got_refs, fin_refs = [unit_refs[units * i : units * (i + 1)] for i in range(5)]
    gr_refs, gs_refs, ge_ref = full_refs[0:2], full_refs[2:5], full_refs[5]
    devices = clips * frames
    clip = lax.axis_index("clip")
    frame = lax.axis_index("frame")
    me = clip * frames + frame
    core = lax.rem(clip, 2)
    partner = (clip + 1 - 2 * core, frame)
    rows = xm.shape[0]
    channels = xm.shape[1]
    narrow = wr.shape[1]
    wide_tiles = channels // LANES
    nar_tiles = narrow // LANES
    blocks = rows // BLOCK
    pad = 2 * side

    def other(k):
        return (lax.rem(clip + lax.div(k, frames), clips), lax.rem(frame + lax.rem(k, frames), frames))

    for j in range(wide_tiles):
        lanes = pl.ds(LANES * j, LANES)
        pltpu.make_async_copy(x_hbm.at[:, :, lanes], xs.at[j], local_sem.at[0]).start()
    if own_gather:
        part_r = wr_hbm.shape[0]
        part_s = ws_hbm.shape[1]
        part_e = we_hbm.shape[0]
        own_r = wr.at[pl.ds(pl.multiple_of(frame * part_r, part_r), part_r)]
        own_s = ws.at[:, pl.ds(pl.multiple_of(frame * part_s, part_s), part_s)]
        own_e = we.at[pl.ds(pl.multiple_of(frame * part_e, part_e), part_e)]
    else:
        own_r, own_s, own_e = wr, ws, we
    own_copies = [
        pltpu.make_async_copy(wr_hbm, own_r, local_sem.at[2]),
        pltpu.make_async_copy(ws_hbm, own_s, local_sem.at[3]),
        pltpu.make_async_copy(we_hbm, own_e, local_sem.at[4]),
    ]
    for copy in own_copies:
        copy.start()
    for j in range(wide_tiles):
        lanes = pl.ds(LANES * j, LANES)
        pltpu.make_async_copy(ct_hbm.at[:, :, lanes], cs.at[j], local_sem.at[1]).start()

    def copies_in(staged, index):
        return pltpu.make_async_copy(staged, staged, local_sem.at[index])

    def to_rows(staged, native, index):
        return pltpu.make_async_copy(staged.reshape(wide_tiles, rows, LANES), native, local_sem.at[index])

    barrier = pltpu.get_barrier_semaphore()

    def greet(k, carry):
        pl.semaphore_signal(barrier, inc=1, device_id=other(k), device_id_type=MESH)
        return carry

    lax.fori_loop(1, devices, greet, 0)

    row_id = lax.broadcasted_iota(jnp.int32, (rows, LANES), 0)
    pixel = row_id >> 1
    slot = row_id & 1
    line = (pixel * 3277) >> 16
    col = pixel - line * side
    extent = [jnp.where(bucket_ref[f] == 0, SMALL_SIDE, side) for f in range(2)]
    limit = [jnp.where(count_ref[0] > f, extent[f], 0) for f in range(2)]
    bound = jnp.where(slot == 0, limit[0], limit[1])
    live = ((line < bound) & (col < bound)).astype(F32)
    mask[...] = live
    left_ok[...] = (col >= 1).astype(F32)
    right_ok[...] = (col <= side - 2).astype(F32)

    par[frame] = jnp.zeros((8, LANES), F32)
    for i, ref in enumerate((g1_ref, b1_ref, g2_ref, b2_ref, g3_ref, b3_ref)):
        width = ref.shape[0]
        par[frame, i : i + 1, 0:width] = ref[...].astype(F32).reshape(1, width)
    counts[me] = jnp.sum(live, axis=0, keepdims=True)

    copies_in(xs, 0).wait()
    to_rows(xs, x_rows, 0).start()
    to_rows(xs, x_rows, 0).wait()

    def block_at(i):
        return pl.ds(pl.multiple_of(i * BLOCK, BLOCK), BLOCK)

    def mask_in(i, carry):
        at = block_at(i)
        m = mask[at, :].astype(BF16)
        for j in range(wide_tiles):
            xm[at, LANES * j : LANES * (j + 1)] = x_rows[j, at, :] * m
        return carry

    lax.fori_loop(0, blocks, mask_in, 0)
    edge = jnp.zeros((3, pad, narrow), F32)
    spad[:, 0:pad, :] = edge
    spad[:, pad + rows : 2 * pad + rows, :] = edge
    turned = xm[...].T
    if own_gather:
        piece = part_r // 2
        for f in range(2 * frames):
            spot = (f % 2) * frames + f // 2
            xt[piece * spot : piece * (spot + 1), :] = turned[piece * f : piece * (f + 1)]
    else:
        xt[...] = turned
    for copy in own_copies:
        copy.wait()

    pl.semaphore_wait(barrier, devices - 1)

    def gather_to_all(buf, index):
        for a in range(clips):
            to_clip = lax.rem(clip + a, clips)

            def send(b, carry):
                pltpu.make_async_remote_copy(
                    src_ref=buf.at[me],
                    dst_ref=buf.at[me],
                    send_sem=st_send.at[index],
                    recv_sem=st_recv.at[index],
                    device_id=(to_clip, lax.rem(frame + b, frames)),
                    device_id_type=MESH,
                ).start()
                return carry

            lax.fori_loop(0 if a else 1, frames, send, 0)

    def arrived(buf, index):
        most = buf.at[pl.ds(0, devices - 1)]
        pltpu.make_async_copy(most, most, st_recv.at[index]).wait()
        pltpu.make_async_copy(most, most, st_send.at[index]).wait()
        return jnp.sum(buf[...].astype(F32), axis=0)

    across = lax.rem(frame, 2)
    along = lax.div(frame, 2)
    depth = frames // 2
    x_peer = (clip, along * 2 + 1 - across)

    def owner_at(d, side_x):
        return lax.rem(along - d + depth, depth) * 2 + side_x

    if own_gather:

        def halves(ref, axis, part):
            half = part // 2

            def view(owner):
                at = pl.ds(pl.multiple_of(owner * part + core * half, half), half)
                return ref.at[at] if axis == 0 else ref.at[:, at]

            return view

        views = (halves(wr, 0, part_r), halves(ws, 1, part_s), halves(we, 0, part_e))

        def weight_copy(index, hop, d, owner, target):
            part = views[index](owner)
            return pltpu.make_async_remote_copy(
                src_ref=part,
                dst_ref=part,
                send_sem=wsend.at[index, hop, d],
                recv_sem=wrecv.at[index, hop, d],
                device_id=target,
                device_id_type=MESH,
            )

        def along_z(index):
            for d in range(1, depth):
                target = (clip, lax.rem(along + d, depth) * 2 + across)
                weight_copy(index, 0, d, frame, target).start()

        def along_x(index, d):
            if d:
                weight_copy(index, 0, d, owner_at(d, across), x_peer).wait_recv()
            weight_copy(index, 1, d, owner_at(d, across), x_peer).start()

        def to_core(index, d):
            if d:
                weight_copy(index, 2, d, owner_at(d, across), partner).start()

        def to_core_late(index, d):
            owner = owner_at(d, 1 - across)
            weight_copy(index, 1, d, owner, partner).wait_recv()
            weight_copy(index, 3, d, owner, partner).start()

        def weight_ready(index):
            for d in range(depth):
                if d:
                    weight_copy(index, 2, d, owner_at(d, across), partner).wait_recv()
                weight_copy(index, 3, d, owner_at(d, 1 - across), partner).wait_recv()

        def weight_sent(index):
            for d in range(depth):
                if d:
                    weight_copy(index, 0, d, frame, partner).wait_send()
                    weight_copy(index, 2, d, frame, partner).wait_send()
                weight_copy(index, 1, d, frame, partner).wait_send()
                weight_copy(index, 3, d, frame, partner).wait_send()

    else:

        def nothing(*args):
            pass

        along_z = along_x = to_core = to_core_late = weight_ready = weight_sent = nothing

    def send_params():
        def send(b, carry):
            pltpu.make_async_remote_copy(
                src_ref=par.at[frame],
                dst_ref=par.at[frame],
                send_sem=st_send.at[0],
                recv_sem=st_recv.at[0],
                device_id=(clip, lax.rem(frame + b, frames)),
                device_id_type=MESH,
            ).start()
            return carry

        lax.fori_loop(1, frames, send, 0)

    along_z(0)
    along_x(0, 0)
    along_z(1)
    along_x(1, 0)
    gather_to_all(counts, 7)
    send_params()
    for d in range(1, depth):
        along_x(0, d)
        to_core(0, d)
    along_x(1, 1)
    to_core(1, 1)
    for d in range(depth):
        to_core_late(0, d)

    weight_ready(0)

    def send_sums(buf, index, first, second):
        tiles = first.shape[1] // LANES
        first = jnp.sum(first, axis=0, keepdims=True)
        second = jnp.sum(second, axis=0, keepdims=True)
        for i in range(tiles):
            buf[me, i : i + 1, :] = first[:, LANES * i : LANES * (i + 1)]
            buf[me, tiles + i : tiles + i + 1, :] = second[:, LANES * i : LANES * (i + 1)]
        gather_to_all(buf, index)

    def get_sums(buf, index):
        total = arrived(buf, index)
        tiles = total.shape[0] // 2
        return rows_to_vec(total, 0, tiles), rows_to_vec(total, tiles, tiles)

    def moments(buf, index, inv):
        total, squares = get_sums(buf, index)
        mean = total * inv
        var = squares * inv - mean * mean
        return mean, lax.rsqrt(var + EPS)

    zero_n = jnp.zeros((8, narrow), F32)

    lines = clips // 2
    line_me = lax.div(clip, 2)
    peers = frames
    y_peer = (lax.rem(clip + 2, clips), frame)

    def unit_copy(unit, stage, src, dst, target):
        return pltpu.make_async_remote_copy(
            src_ref=src,
            dst_ref=dst,
            send_sem=rs_send.at[unit, stage],
            recv_sem=rs_recv.at[unit, stage],
            device_id=target,
            device_id_type=MESH,
        )

    def columns(line, cut):
        return pl.ds(pl.multiple_of(line * cut, LANES), cut)

    def cores(unit):
        full, pair = full_refs[unit], pair_refs[unit]
        half = pair.shape[1]
        view = full.reshape(frames, 2 * half, full.shape[1])
        theirs = pl.ds(pl.multiple_of((1 - core) * half, half), half)
        return unit_copy(unit, 0, view.at[:, theirs], pair, partner)

    def near_copy(unit):
        pair, mid = pair_refs[unit], mid_refs[unit]
        half, width = pair.shape[1], pair.shape[2]
        if X_FIRST[unit]:
            return unit_copy(unit, 1, pair.reshape(depth, 2, half, width).at[:, 1 - across], mid, x_peer)
        return unit_copy(unit, 1, pair.at[:, :, columns(1 - line_me, width // lines)], mid, y_peer)

    def near(unit):
        full, pair = full_refs[unit], pair_refs[unit]
        cores(unit).wait()
        half = pair.shape[1]
        mine = pl.ds(pl.multiple_of(core * half, half), half)
        view = full.reshape(frames, 2 * half, full.shape[1])

        def add(f, carry):
            pair[f] = (pair[f].astype(F32) + view[f, mine, :].astype(F32)).astype(BF16)
            return carry

        lax.fori_loop(0, frames, add, 0)
        near_copy(unit).start()

    def far(unit):
        pair, mid, got = pair_refs[unit], mid_refs[unit], got_refs[unit]
        cut = pair.shape[2] // lines
        near_copy(unit).wait()

        def add(k, carry):
            own = pair[2 * k + across] if X_FIRST[unit] else pair[k, :, columns(line_me, cut)]
            mid[k] = (mid[k].astype(F32) + own.astype(F32)).astype(BF16)
            return carry

        lax.fori_loop(0, mid.shape[0], add, 0)
        if X_FIRST[unit]:
            slot_me = line_me * depth + along
            got[slot_me] = mid[along, :, columns(line_me, cut)]

            def send(k, carry):
                line = lax.rem(line_me + lax.div(k, depth), lines)
                deep = lax.rem(along + lax.rem(k, depth), depth)
                src = mid.at[deep, :, columns(line, cut)]
                unit_copy(unit, 2, src, got.at[slot_me], (line * 2 + core, deep * 2 + across)).start()
                return carry

        else:
            got[frame] = mid[frame]

            def send(k, carry):
                owner = lax.rem(frame + k, frames)
                unit_copy(unit, 2, mid.at[owner], got.at[frame], (clip, owner)).start()
                return carry

        lax.fori_loop(1, peers, send, 0)

    def owners(unit):
        got, fin = got_refs[unit], fin_refs[unit]
        half, cut = got.shape[1], got.shape[2]
        most = got.at[pl.ds(0, peers - 1)]
        unit_copy(unit, 2, most, most, partner).wait()
        spot = fin.at[pl.ds(pl.multiple_of(core * half, half), half), columns(line_me, cut)]
        spot[...] = jnp.sum(got[...].astype(F32), axis=0).astype(BF16)

        def send(k, carry):
            unit_copy(unit, 3, spot, spot, (lax.rem(clip + k, clips), frame)).start()
            return carry

        lax.fori_loop(1, clips, send, 0)

    def finished(unit):
        most = got_refs[unit].at[pl.ds(0, clips - 1)]
        unit_copy(unit, 3, most, most, partner).wait()
        return fin_refs[unit]

    big = rows // 2

    def conv_one(i, carry):
        at = pl.ds(pl.multiple_of(i * big, big), big)
        v = dot(xm[at, :], wr[...])
        pre1[at, :] = v
        return carry[0] + part_sum(v), carry[1] + part_sum(v * v)

    sums = lax.fori_loop(0, 2, conv_one, (zero_n, zero_n))
    send_sums(st1, 1, *sums)
    for d in range(2, depth):
        along_x(1, d)
        to_core(1, d)
    along_z(2)
    along_x(2, 0)
    for d in range(depth):
        to_core_late(1, d)
    most = par.at[pl.ds(0, frames - 1)]
    pltpu.make_async_copy(most, most, st_recv.at[0]).wait()
    pltpu.make_async_copy(most, most, st_send.at[0]).wait()
    part_n = g1_ref.shape[0]
    part_w = g3_ref.shape[0]
    acc_n = [jnp.zeros((8, LANES), F32) for _ in range(nar_tiles)]
    acc_w = [jnp.zeros((8, LANES), F32) for _ in range(wide_tiles)]
    for f in range(frames):
        tile = par[f]
        spot = f * part_n
        shift = spot % LANES
        acc_n[spot // LANES] += pltpu.roll(tile, shift, 1) if shift else tile
        spot = f * part_w
        shift = spot % LANES
        acc_w[spot // LANES] += pltpu.roll(tile, shift, 1) if shift else tile
    gain1, bias1, gain2, bias2 = [jnp.concatenate([a[i : i + 1] for a in acc_n], axis=1) for i in range(4)]
    gain3, bias3 = [jnp.concatenate([a[i : i + 1] for a in acc_w], axis=1) for i in (4, 5)]
    inv_count = 1.0 / arrived(counts, 7)
    inv_n = jnp.concatenate([inv_count] * nar_tiles, axis=1)
    inv_w = jnp.concatenate([inv_count] * wide_tiles, axis=1)

    mean1, inv1 = moments(st1, 1, inv_n)
    scale1 = inv1 * gain1
    offset1 = bias1 - mean1 * scale1

    def both(v):
        return jnp.concatenate([v] * nar_tiles, axis=1)

    def act_one(i, carry):
        at = block_at(i)
        z = pre1[at, :] * scale1 + offset1
        s = sigmoid(z)
        m = both(mask[at, :])
        ms = m * s
        spad[1, pl.ds(pl.multiple_of(i * BLOCK + pad, 8), BLOCK), :] = ms * z
        slope1[at, :] = ms * (1.0 + z * (1.0 - s))
        return carry

    lax.fori_loop(0, blocks, act_one, 0)

    def spread():
        def shifted(i, carry):
            at = block_at(i)
            v = spad[1, pl.ds(pl.multiple_of(i * BLOCK + pad - 8, 8), BLOCK + 16), :]
            here = pl.ds(pl.multiple_of(i * BLOCK + pad, 8), BLOCK)
            spad[0, here, :] = pltpu.roll(v, 2, 0)[8 : 8 + BLOCK] * both(left_ok[at, :])
            spad[2, here, :] = pltpu.roll(v, BLOCK + 14, 0)[8 : 8 + BLOCK] * both(right_ok[at, :])
            return carry

        lax.fori_loop(0, blocks, shifted, 0)

    def gather_nine(flip):
        def step(i, carry):
            at = block_at(i)
            for tap in range(9):
                row_off, col_off = (tap // 3, tap % 3) if not flip else (2 - tap // 3, 2 - tap % 3)
                src = pl.ds(pl.multiple_of(i * BLOCK + pad * row_off, 8), BLOCK)
                nine[at, narrow * tap : narrow * (tap + 1)] = spad[col_off, src, :].astype(BF16)
            return carry

        lax.fori_loop(0, blocks, step, 0)

    spread()
    gather_nine(False)
    weight_ready(1)
    for d in range(1, depth):
        along_x(2, d)
        to_core(2, d)

    def conv_two(i, carry):
        at = pl.ds(pl.multiple_of(i * big, big), big)
        v = dot(nine[at, :], ws[...].reshape(9 * narrow, narrow))
        pre2[at, :] = v
        mv = both(mask[at, :]) * v
        return carry[0] + part_sum(mv), carry[1] + part_sum(mv * v)

    sums = lax.fori_loop(0, 2, conv_two, (zero_n, zero_n))
    send_sums(st2, 2, *sums)
    wrt[...] = wr[...].T
    a1t[...] = spad[1, pad : pad + rows, :].astype(BF16).T
    for d in range(depth):
        to_core_late(2, d)

    mean2, inv2 = moments(st2, 2, inv_n)
    scale2 = inv2 * gain2
    offset2 = bias2 - mean2 * scale2

    def act_two(i, carry):
        at = block_at(i)
        z = pre2[at, :] * scale2 + offset2
        s = sigmoid(z)
        ms = both(mask[at, :]) * s
        a = (ms * z).astype(BF16)
        act2[at, :] = a
        slope2[at, :] = ms * (1.0 + z * (1.0 - s))
        return carry + part_sum(a.astype(F32))

    act_sum = lax.fori_loop(0, blocks, act_two, zero_n)

    weight_ready(2)
    zero_w = jnp.zeros((8, channels), F32)

    wide = big

    def conv_three(i, carry):
        at = pl.ds(pl.multiple_of(i * wide, wide), wide)
        v = dot(act2[at, :], we[...])
        pre3[at, :] = v
        return carry + part_sum(v * v)

    squares = lax.fori_loop(0, rows // wide, conv_three, zero_w)
    st3[me, :, 0:narrow] = jnp.sum(act_sum, axis=0, keepdims=True)
    st3[me, :, narrow : narrow + channels] = jnp.sum(squares, axis=0, keepdims=True)
    gather_to_all(st3, 3)
    for tap in range(9):
        wst[narrow * tap : narrow * (tap + 1), :] = ws[tap].T
    wet[...] = we[...].T
    a2t[...] = act2[...].T
    copies_in(cs, 1).wait()
    to_rows(cs, ct_rows, 1).start()
    to_rows(cs, ct_rows, 1).wait()
    both_sums = arrived(st3, 3)
    left = both_sums[:, 0:narrow]
    parts = []
    for _ in range(3):
        parts.append(left.astype(BF16).astype(F32))
        left = left - parts[-1]
    exact = jnp.concatenate(parts + [jnp.zeros((5, narrow), F32)], axis=0).astype(BF16)
    mean3 = jnp.sum(dot(exact, we[...]), axis=0, keepdims=True) * inv_w
    inv3 = lax.rsqrt(both_sums[:, narrow:] * inv_w - mean3 * mean3 + EPS)
    scale3 = inv3 * gain3
    offset3 = bias3 - mean3 * scale3

    def from_rows(ref, index):
        return pltpu.make_async_copy(out_rows, ref.reshape(wide_tiles, rows, LANES), out_sem.at[index])

    def finish(i, carry):
        at = block_at(i)
        m = mask[at, :]
        first, second = [], []
        for j in range(wide_tiles):
            lanes = slice(LANES * j, LANES * (j + 1))
            p = pre3[at, lanes]
            t = p * scale3[:, lanes] + offset3[:, lanes] + xm[at, lanes].astype(F32)
            s = sigmoid(t)
            ms = m * s
            o = ms * t
            out_rows[j, at, :] = o.astype(BF16)
            g = ct_rows[j, at, :].astype(F32) * (ms + o * (1.0 - s))
            gt[at, lanes] = g
            first.append(part_sum(g))
            second.append(part_sum(g * p))
        return carry[0] + jnp.concatenate(first, axis=1), carry[1] + jnp.concatenate(second, axis=1)

    shift_own, slope_own = lax.fori_loop(0, blocks, finish, (zero_w, zero_w))
    shift_own = jnp.sum(shift_own, axis=0, keepdims=True)
    slope_own = (jnp.sum(slope_own, axis=0, keepdims=True) - mean3 * shift_own) * inv3
    pieces = [v[:, LANES * j : LANES * (j + 1)] for v in (shift_own, slope_own) for j in range(wide_tiles)]
    st4[me] = jnp.concatenate(pieces, axis=0).astype(BF16)
    gather_to_all(st4, 4)
    from_rows(out_ref, 0).start()
    shift3, slope_gain3 = get_sums(st4, 4)

    def back_terms(scale, inv, mean, shift_sum, gain_sum, inv_cnt):
        along = scale * inv * gain_sum * inv_cnt
        return along, scale * shift_sum * inv_cnt - mean * along

    along3, flat3 = back_terms(scale3, inv3, mean3, shift3, slope_gain3, inv_w)

    def back_three(i, carry):
        at = block_at(i)
        m = mask[at, :]
        for j in range(wide_tiles):
            lanes = slice(LANES * j, LANES * (j + 1))
            g = gt[at, lanes] * scale3[:, lanes] - pre3[at, lanes] * along3[:, lanes] - m * flat3[:, lanes]
            gp3[at, lanes] = g.astype(BF16)
        return carry

    lax.fori_loop(0, blocks, back_three, 0)

    d = dot(gp3[...], wet[...]) * slope2[...]
    dz[...] = d
    send_sums(st5, 5, part_sum(d), part_sum(d * ((pre2[...] - mean2) * inv2)))

    def grad_expand(i, carry):
        lanes = pl.ds(pl.multiple_of(i * 256, 256), 256)
        ge_ref[:, lanes] = dot(a2t[...], gp3[:, lanes]).astype(BF16)
        return carry

    lax.fori_loop(0, channels // 256, grad_expand, 0)
    if own_gather:
        cores(5).start()
        near(5)

    shift2, slope_gain2 = get_sums(st5, 5)
    along2, flat2 = back_terms(scale2, inv2, mean2, shift2, slope_gain2, inv_n)

    def back_two(i, carry):
        at = block_at(i)
        here = pl.ds(pl.multiple_of(i * BLOCK + pad, 8), BLOCK)
        m = both(mask[at, :])
        spad[1, here, :] = dz[at, :] * scale2 - m * (pre2[at, :] * along2 + flat2)
        return carry

    lax.fori_loop(0, blocks, back_two, 0)
    spread()
    gather_nine(True)

    def grad_spatial(row):
        wide_row = 3 * narrow
        gs_refs[row][...] = dot(a1t[...], nine[:, wide_row * row : wide_row * (row + 1)]).astype(BF16)
        if own_gather:
            cores(2 + row).start()

    grad_spatial(0)

    def back_spatial(i, carry):
        at = pl.ds(pl.multiple_of(i * big, big), big)
        d = dot(nine[at, :], wst[...]) * slope1[at, :]
        dz[at, :] = d
        return carry[0] + part_sum(d), carry[1] + part_sum(d * ((pre1[at, :] - mean1) * inv1))

    sums = lax.fori_loop(0, 2, back_spatial, (zero_n, zero_n))
    send_sums(st6, 6, *sums)
    if own_gather:
        near(2)
        far(5)
    grad_spatial(1)
    grad_spatial(2)
    if own_gather:
        near(3)
        near(4)

    shift1, slope_gain1 = get_sums(st6, 6)
    along1, flat1 = back_terms(scale1, inv1, mean1, shift1, slope_gain1, inv_n)

    def back_one(i, carry):
        at = block_at(i)
        g = dz[at, :] * scale1 - both(mask[at, :]) * (pre1[at, :] * along1 + flat1)
        gp1[at, :] = g.astype(BF16)
        return carry

    lax.fori_loop(0, blocks, back_one, 0)

    for i in range(2):
        height = channels // 2
        gr_refs[i][...] = dot(xt[height * i : height * (i + 1), :], gp1[...]).astype(BF16)
        if own_gather:
            cores(i).start()
    if own_gather:
        far(2)
        near(0)
        near(1)
    from_rows(out_ref, 0).wait()

    def grad_in(i, carry):
        at = pl.ds(pl.multiple_of(i * wide, wide), wide)
        m = mask[at, :]
        back = dot(gp1[at, :], wrt[...])
        for j in range(wide_tiles):
            lanes = slice(LANES * j, LANES * (j + 1))
            out_rows[j, at, :] = (m * back[:, lanes] + gt[at, lanes]).astype(BF16)
        return carry

    lax.fori_loop(0, rows // wide, grad_in, 0)
    if own_gather:
        far(3)
        far(4)
    from_rows(gin_ref, 1).start()

    def own_part(ref, v):
        width = ref.shape[0]
        spot = frame * width
        tile = jnp.zeros((1, LANES), F32)
        for t in range(v.shape[1] // LANES):
            tile = jnp.where(lax.div(spot, LANES) == t, v[:, LANES * t : LANES * (t + 1)], tile)
        tile = pltpu.roll(jnp.concatenate([tile] * 8, axis=0), lax.rem(LANES - lax.rem(spot, LANES), LANES), 1)
        ref[...] = tile[0, 0:width]

    own_part(vec1_gain, slope_gain1)
    own_part(vec1_shift, shift1)
    own_part(vec2_gain, slope_gain2)
    own_part(vec2_shift, shift2)
    own_part(vec3_gain, slope_gain3)
    own_part(vec3_shift, shift3)

    if own_gather:
        owners(5)
        far(0)
        far(1)
        for unit in (2, 3, 4, 0, 1):
            owners(unit)
        ge_out[...] = finished(5)[...].astype(F32)
        for row in range(3):
            fin = finished(2 + row)
            for c in range(3):
                gs_out[3 * row + c] = fin[:, narrow * c : narrow * (c + 1)].astype(F32)
        for i in range(2):
            gr_out[piece * i : piece * (i + 1), :] = finished(i)[...].astype(F32)
    else:
        for i in range(2):
            gr_out[channels // 2 * i : channels // 2 * (i + 1), :] = gr_refs[i][...]
        for row in range(3):
            gs_out[:, 3 * narrow * row : 3 * narrow * (row + 1)] = gs_refs[row][...]
        ge_out[...] = ge_ref[...]
    for index in range(3):
        weight_sent(index)
    from_rows(gin_ref, 1).wait()


def deliver_kernel(count, *refs):
    sources, targets, sems = refs[:count], refs[count : 2 * count], refs[2 * count]
    copies = []
    for i in range(2):
        for j in range(sources[i].shape[0]):
            part = targets[i].at[:, :, LANES * j : LANES * (j + 1)]
            copies.append(pltpu.make_async_copy(sources[i].at[j], part, sems.at[len(copies)]))
    for i in range(2, count):
        copies.append(pltpu.make_async_copy(sources[i], targets[i], sems.at[len(copies)]))
    for copy in copies:
        copy.start()
    for copy in copies:
        copy.wait()


def deliver(arrays, big):
    count = len(arrays)
    shapes = [big, big] + [jax.ShapeDtypeStruct(a.shape, a.dtype) for a in arrays[2:]]
    return pl.pallas_call(
        functools.partial(deliver_kernel, count),
        out_shape=tuple(shapes),
        in_specs=[pl.BlockSpec(memory_space=pltpu.VMEM)] * count,
        out_specs=(pl.BlockSpec(memory_space=pl.ANY),) * count,
        scratch_shapes=[pltpu.SemaphoreType.DMA((2 * arrays[0].shape[0] + count,))],
        compiler_params=pltpu.CompilerParams(vmem_limit_bytes=1024 * 1024),
    )(*arrays)


def on_device(
    dims,
    x_in,
    cotangent,
    w_reduce,
    w_spatial,
    w_expand,
    gain_one,
    shift_one,
    gain_two,
    shift_two,
    gain_three,
    shift_three,
    bucket,
    frame_count,
):
    clips, frames = dims
    slots, side, _, channels = x_in.shape
    narrow = w_reduce.shape[1]
    pixels = side * side
    rows = pixels * slots
    tiles = channels // LANES
    devices = clips * frames
    own_gather = all(n % 32 == 0 for n in (w_reduce.shape[0], w_spatial.shape[2], w_expand.shape[0]))
    w_spatial = w_spatial.reshape(9, -1, narrow)
    if not own_gather:
        w_reduce = lax.all_gather(w_reduce, "frame", axis=0, tiled=True)
        w_spatial = lax.all_gather(w_spatial, "frame", axis=1, tiled=True)
        w_expand = lax.all_gather(w_expand, "frame", axis=0, tiled=True)

    def by_pixel(v):
        return jnp.transpose(v, (1, 2, 0, 3)).reshape(pixels, slots, channels)

    any_spec = pl.BlockSpec(memory_space=pl.ANY)
    vmem = pl.BlockSpec(memory_space=pltpu.VMEM)
    smem = pl.BlockSpec(memory_space=pltpu.SMEM)
    big = jax.ShapeDtypeStruct((pixels, slots, channels), BF16)
    staged = pltpu.VMEM((tiles, pixels, slots, LANES), BF16)
    native = pltpu.VMEM((tiles, rows, LANES), BF16)
    narrow_f32 = pltpu.VMEM((rows, narrow), F32)
    wide_f32 = pltpu.VMEM((rows, channels), F32)
    lanes_f32 = pltpu.VMEM((rows, LANES), F32)

    def stats(count):
        return pltpu.VMEM((devices, count, LANES), F32)

    if own_gather:
        grad_shapes = (
            pltpu.VMEM((channels // frames, narrow), F32),
            pltpu.VMEM((9, narrow // frames, narrow), F32),
            pltpu.VMEM((narrow // frames, channels), F32),
        )
    else:
        grad_shapes = (
            jax.ShapeDtypeStruct((channels, narrow), BF16),
            jax.ShapeDtypeStruct((narrow, 9 * narrow), BF16),
            jax.ShapeDtypeStruct((narrow, channels), BF16),
        )
    wholes = (*(((channels // 2, narrow),) * 2), *(((narrow, 3 * narrow),) * 3), (narrow, channels))
    lines = clips // 2
    unit_scratch = [pltpu.VMEM(shape, BF16) for shape in wholes]
    if own_gather:
        cuts = [(height // frames // 2, width) for height, width in wholes]
        unit_scratch += [pltpu.VMEM((frames, half, width), BF16) for half, width in cuts]
        unit_scratch += [
            pltpu.VMEM((frames // 2, half, width) if x_first else (frames, half, width // lines), BF16)
            for (half, width), x_first in zip(cuts, X_FIRST)
        ]
        unit_scratch += [pltpu.VMEM((frames, half, width // lines), BF16) for half, width in cuts]
        unit_scratch += [pltpu.VMEM((2 * half, width), BF16) for half, width in cuts]

    results = pl.pallas_call(
        functools.partial(block_kernel, (clips, frames, side, own_gather)),
        out_shape=(
            staged,
            staged,
            *grad_shapes,
            *(pltpu.VMEM((narrow // frames,), F32),) * 4,
            *(pltpu.VMEM((channels // frames,), F32),) * 2,
        ),
        in_specs=[any_spec] * 5 + [vmem] * 6 + [smem] * 2,
        out_specs=(vmem,) * 11,
        scratch_shapes=[
            staged,
            staged,
            native,
            native,
            native,
            pltpu.VMEM((rows, channels), BF16),
            pltpu.VMEM((channels, rows), BF16),
            pltpu.VMEM((narrow, rows), BF16),
            pltpu.VMEM((narrow, rows), BF16),
            lanes_f32,
            lanes_f32,
            lanes_f32,
            pltpu.VMEM((channels, narrow), BF16),
            pltpu.VMEM((9, narrow, narrow), BF16),
            pltpu.VMEM((narrow, channels), BF16),
            pltpu.VMEM((9 * narrow, narrow), BF16),
            pltpu.VMEM((channels, narrow), BF16),
            pltpu.VMEM((narrow, channels), BF16),
            narrow_f32,
            narrow_f32,
            narrow_f32,
            narrow_f32,
            narrow_f32,
            pltpu.VMEM((3, rows + 4 * side, narrow), F32),
            pltpu.VMEM((rows, narrow), BF16),
            pltpu.VMEM((rows, 9 * narrow), BF16),
            wide_f32,
            wide_f32,
            pltpu.VMEM((rows, channels), BF16),
            pltpu.VMEM((rows, narrow), BF16),
            pltpu.VMEM((frames, 8, LANES), F32),
            stats(1),
            stats(2 * narrow // LANES),
            stats(2 * narrow // LANES),
            pltpu.VMEM((devices, 1, narrow + channels), F32),
            pltpu.VMEM((devices, 2 * tiles, LANES), BF16),
            stats(2 * narrow // LANES),
            stats(2 * narrow // LANES),
            pltpu.SemaphoreType.DMA((5,)),
            pltpu.SemaphoreType.DMA((3, 4, frames // 2)),
            pltpu.SemaphoreType.DMA((3, 4, frames // 2)),
            pltpu.SemaphoreType.DMA((8,)),
            pltpu.SemaphoreType.DMA((8,)),
            pltpu.SemaphoreType.DMA((2,)),
            pltpu.SemaphoreType.DMA((len(X_FIRST), 4)),
            pltpu.SemaphoreType.DMA((len(X_FIRST), 4)),
            *unit_scratch,
        ],
        compiler_params=pltpu.CompilerParams(
            collective_id=0, has_side_effects=True, vmem_limit_bytes=VMEM_BYTES
        ),
    )(
        by_pixel(x_in),
        by_pixel(cotangent),
        w_reduce,
        w_spatial,
        w_expand,
        gain_one,
        shift_one,
        gain_two,
        shift_two,
        gain_three,
        shift_three,
        bucket,
        frame_count,
    )

    def by_frame(v):
        return jnp.transpose(v.reshape(side, side, slots, channels), (2, 0, 1, 3))

    def owned(v):
        part = lax.psum_scatter(v, "frame", scatter_dimension=0, tiled=True)
        return lax.psum(part, "clip").astype(F32)

    if own_gather:
        out, gin, gr, gs, ge, *vectors = deliver(results, big)
    else:
        gr, gs, ge = [owned(v) for v in results[2:5]]
        gs = gs.reshape(-1, 9, narrow).transpose(1, 0, 2)
        out, gin, gr, gs, ge, *vectors = deliver((*results[:2], gr, gs, ge, *results[5:]), big)
    return (by_frame(out), by_frame(gin), gr, gs.reshape(3, 3, -1, narrow), ge, *vectors)


def solution(mesh):
    by_device = P(("clip", "frame"))
    shard = P("frame")
    spatial = P(None, None, "frame", None)
    return jax.shard_map(
        functools.partial(on_device, (mesh.shape["clip"], mesh.shape["frame"])),
        mesh=mesh,
        in_specs=(by_device, by_device, shard, spatial) + (shard,) * 7 + (by_device, by_device),
        out_specs=(by_device, by_device, shard, spatial) + (shard,) * 7,
        check_vma=False,
    )
```

```python
import functools

import jax
import jax.numpy as jnp
from jax import lax
from jax.experimental import pallas as pl
from jax.experimental.pallas import tpu as pltpu
from jax.sharding import PartitionSpec as P

SMALL_SIDE = 14
EPS = 1e-05
LANES = 128
BLOCK = 80
VMEM_BYTES = 52 * 1024 * 1024
MESH = pl.DeviceIdType.MESH
NEAR = ("x", "y", "y", "x", "y", "x")
F32 = jnp.float32
BF16 = jnp.bfloat16


def sigmoid(v):
    return 0.5 * jnp.tanh(0.5 * v) + 0.5


def part_sum(v):
    rows, width = v.shape
    return jnp.sum(v.reshape(rows // 8, 8, width), axis=0)


def dot(a, b):
    return jnp.dot(a, b, preferred_element_type=F32)


def rows_to_vec(tile, first, count):
    return jnp.concatenate([tile[first + i : first + i + 1] for i in range(count)], axis=1)


def block_kernel(
    dims,
    x_hbm,
    ct_hbm,
    wr_hbm,
    ws_hbm,
    we_hbm,
    g1_ref,
    b1_ref,
    g2_ref,
    b2_ref,
    g3_ref,
    b3_ref,
    bucket_ref,
    count_ref,
    out_ref,
    gin_ref,
    gr_out,
    gs_out,
    ge_out,
    vec1_gain,
    vec1_shift,
    vec2_gain,
    vec2_shift,
    vec3_gain,
    vec3_shift,
    xs,
    cs,
    x_rows,
    ct_rows,
    out_rows,
    xm,
    xt,
    a1t,
    a2t,
    mask,
    left_ok,
    right_ok,
    wr,
    ws,
    we,
    wst,
    wet,
    wrt,
    pre1,
    slope1,
    pre2,
    slope2,
    dz,
    spad,
    act2,
    nine,
    pre3,
    gt,
    gp3,
    gp1,
    par,
    counts,
    st1,
    st2,
    st3,
    st4,
    st5,
    st6,
    local_sem,
    wsend,
    wrecv,
    st_send,
    st_recv,
    out_sem,
    rs_send,
    rs_recv,
    *unit_refs,
):
    clips, frames, side, own_gather = dims
    units = len(NEAR)
    full_refs, pair_refs, mid_refs, got_refs, fin_refs = [unit_refs[units * i : units * (i + 1)] for i in range(5)]
    gr_refs, gs_refs, ge_ref = full_refs[0:2], full_refs[2:5], full_refs[5]
    devices = clips * frames
    clip = lax.axis_index("clip")
    frame = lax.axis_index("frame")
    me = clip * frames + frame
    core = lax.rem(clip, 2)
    partner = (clip + 1 - 2 * core, frame)
    rows = xm.shape[0]
    channels = xm.shape[1]
    narrow = wr.shape[1]
    wide_tiles = channels // LANES
    nar_tiles = narrow // LANES
    blocks = rows // BLOCK
    pad = 2 * side
    lines = clips // 2
    line_me = lax.div(clip, 2)
    y_peer = (lax.rem(clip + 2, clips), frame)

    small = devices <= 32 and clips & (clips - 1) == 0 and frames & (frames - 1) == 0

    def flips(v, size):
        return [(1 - 2 * lax.rem(lax.div(v, 1 << i), 2)) * (1 << i) for i in range(size.bit_length() - 1)]

    clip_flips, frame_flips = flips(clip, clips), flips(frame, frames)

    def to_others(action):
        if small:
            for b in reversed(range(frames)):
                to_frame = sum((d for i, d in enumerate(frame_flips) if b >> i & 1), frame)
                for a in reversed(range(clips)):
                    if a or b:
                        action((sum((d for i, d in enumerate(clip_flips) if a >> i & 1), clip), to_frame))
            return
        for a in range(clips):
            to_clip = lax.rem(clip + a, clips)

            def step(b, carry):
                action((to_clip, lax.rem(frame + b, frames)))
                return carry

            lax.fori_loop(0 if a else 1, frames, step, 0)

    for j in range(wide_tiles):
        lanes = pl.ds(LANES * j, LANES)
        pltpu.make_async_copy(x_hbm.at[:, :, lanes], xs.at[j], local_sem.at[0]).start()
    if own_gather:
        part_r = wr_hbm.shape[0]
        part_s = ws_hbm.shape[1]
        part_e = we_hbm.shape[0]
        own_r = wr.at[pl.ds(pl.multiple_of(frame * part_r, part_r), part_r)]
        own_s = ws.at[:, pl.ds(pl.multiple_of(frame * part_s, part_s), part_s)]
        own_e = we.at[pl.ds(pl.multiple_of(frame * part_e, part_e), part_e)]
    else:
        own_r, own_s, own_e = wr, ws, we
    own_copies = [
        pltpu.make_async_copy(wr_hbm, own_r, local_sem.at[2]),
        pltpu.make_async_copy(ws_hbm, own_s, local_sem.at[3]),
        pltpu.make_async_copy(we_hbm, own_e, local_sem.at[4]),
    ]
    for copy in own_copies:
        copy.start()
    for j in range(wide_tiles):
        lanes = pl.ds(LANES * j, LANES)
        pltpu.make_async_copy(ct_hbm.at[:, :, lanes], cs.at[j], local_sem.at[1]).start()

    def copies_in(staged, index):
        return pltpu.make_async_copy(staged, staged, local_sem.at[index])

    def to_rows(staged, native, index):
        return pltpu.make_async_copy(staged.reshape(wide_tiles, rows, LANES), native, local_sem.at[index])

    barrier = pltpu.get_barrier_semaphore()

    to_others(lambda target: pl.semaphore_signal(barrier, inc=1, device_id=target, device_id_type=MESH))

    row_id = lax.broadcasted_iota(jnp.int32, (rows, LANES), 0)
    pixel = row_id >> 1
    slot = row_id & 1
    line = (pixel * 3277) >> 16
    col = pixel - line * side
    extent = [jnp.where(bucket_ref[f] == 0, SMALL_SIDE, side) for f in range(2)]
    limit = [jnp.where(count_ref[0] > f, extent[f], 0) for f in range(2)]
    bound = jnp.where(slot == 0, limit[0], limit[1])
    live = ((line < bound) & (col < bound)).astype(F32)
    mask[...] = live
    left_ok[...] = (col >= 1).astype(F32)
    right_ok[...] = (col <= side - 2).astype(F32)

    par[frame] = jnp.zeros((8, LANES), F32)
    for i, ref in enumerate((g1_ref, b1_ref, g2_ref, b2_ref, g3_ref, b3_ref)):
        width = ref.shape[0]
        par[frame, i : i + 1, 0:width] = ref[...].astype(F32).reshape(1, width)
    counts[me] = jnp.sum(live, axis=0, keepdims=True)

    copies_in(xs, 0).wait()
    to_rows(xs, x_rows, 0).start()
    to_rows(xs, x_rows, 0).wait()

    def block_at(i):
        return pl.ds(pl.multiple_of(i * BLOCK, BLOCK), BLOCK)

    def mask_in(i, carry):
        at = block_at(i)
        m = mask[at, :].astype(BF16)
        for j in range(wide_tiles):
            xm[at, LANES * j : LANES * (j + 1)] = x_rows[j, at, :] * m
        return carry

    lax.fori_loop(0, blocks, mask_in, 0)
    edge = jnp.zeros((3, pad, narrow), F32)
    spad[:, 0:pad, :] = edge
    spad[:, pad + rows : 2 * pad + rows, :] = edge
    turned = xm[...].T
    if own_gather:
        piece = part_r // 2
        for f in range(2 * frames):
            spot = (f % 2) * frames + f // 2
            xt[piece * spot : piece * (spot + 1), :] = turned[piece * f : piece * (f + 1)]
    else:
        xt[...] = turned
    for copy in own_copies:
        copy.wait()

    pl.semaphore_wait(barrier, devices - 1)

    def gather_to_all(buf, index):
        def send(target):
            pltpu.make_async_remote_copy(
                src_ref=buf.at[me],
                dst_ref=buf.at[me],
                send_sem=st_send.at[0],
                recv_sem=st_recv.at[index],
                device_id=target,
                device_id_type=MESH,
            ).start()

        to_others(send)

    def arrived(buf, index):
        most = buf.at[pl.ds(0, devices - 1)]
        pltpu.make_async_copy(most, most, st_recv.at[index]).wait()
        return jnp.sum(buf[...].astype(F32), axis=0)

    across = lax.rem(frame, 2)
    along = lax.div(frame, 2)
    depth = frames // 2
    x_peer = (clip, along * 2 + 1 - across)

    def owner_at(d, side_x):
        return lax.rem(along - d + depth, depth) * 2 + side_x

    if own_gather:

        kinds = ((wr, 0, part_r), (ws, 1, part_s), (we, 0, part_e))

        def piece_of(index, owner, columns=None):
            ref, axis, part = kinds[index]
            at = pl.ds(pl.multiple_of(owner * part + core * (part // 2), part // 2), part // 2)
            if axis == 0:
                return ref.at[at]
            return ref.at[:, at] if columns is None else ref.at[:, at, columns]

        def own_columns(index):
            if index != 1:
                return None
            cut = narrow // lines
            return pl.ds(pl.multiple_of(line_me * cut, LANES), cut)

        def weight_copy(index, sem, owner, target, columns=None):
            part = piece_of(index, owner, columns)
            return pltpu.make_async_remote_copy(
                src_ref=part,
                dst_ref=part,
                send_sem=wsend.at[index],
                recv_sem=wrecv.at[index, sem],
                device_id=target,
                device_id_type=MESH,
            )

        def blocks_of(index, count, wide=True):
            ref, axis, part = kinds[index]
            size = pl.ds(0, count * (part // 2))
            if axis == 0:
                return ref.at[size]
            return ref.at[:, size] if wide else ref.at[:, size, pl.ds(0, narrow // lines)]

        def blocks_wait(sem, view):
            pltpu.make_async_copy(view, view, sem).wait()

        def along_z(index):
            for d in range(1, depth):
                target = (clip, lax.rem(along + d, depth) * 2 + across)
                weight_copy(index, d, frame, target, own_columns(index)).start()

        def along_x(index, d):
            columns = own_columns(index)
            if d:
                weight_copy(index, d, owner_at(d, across), x_peer, columns).wait_recv()
            weight_copy(index, depth + d, owner_at(d, across), x_peer, columns).start()

        def along_y(d):
            weight_copy(1, 2 * depth + 1, owner_at(d, across), y_peer, own_columns(1)).start()

        def along_y_late(d):
            owner = owner_at(d, 1 - across)
            weight_copy(1, depth + d, owner, partner, own_columns(1)).wait_recv()
            weight_copy(1, 2 * depth + 2, owner, y_peer, own_columns(1)).start()

        def y_to_core():
            blocks_wait(wrecv.at[1, 2 * depth + 1], blocks_of(1, depth - 1, False))
            for d in range(1, depth):
                to_core(1, d)
            blocks_wait(wrecv.at[1, 2 * depth + 2], blocks_of(1, depth, False))
            for d in range(depth):
                weight_copy(1, 2 * depth, owner_at(d, 1 - across), partner).start()

        def to_core(index, d):
            weight_copy(index, 2 * depth, owner_at(d, across), partner).start()

        def to_core_late(index, d):
            owner = owner_at(d, 1 - across)
            weight_copy(index, depth + d, owner, partner).wait_recv()
            weight_copy(index, 2 * depth, owner, partner).start()

        def weight_ready(index):
            blocks_wait(wrecv.at[index, 2 * depth], blocks_of(index, 2 * depth - 1))

        def weight_sent(index):
            blocks_wait(wsend.at[index], blocks_of(index, 4 * depth - 2))

    else:

        def nothing(*args):
            pass

        along_z = along_x = along_y = along_y_late = y_to_core = nothing
        to_core = to_core_late = weight_ready = weight_sent = nothing

    def send_params():
        def send(b, carry):
            pltpu.make_async_remote_copy(
                src_ref=par.at[frame],
                dst_ref=par.at[frame],
                send_sem=st_send.at[1],
                recv_sem=st_recv.at[0],
                device_id=(clip, lax.rem(frame + b, frames)),
                device_id_type=MESH,
            ).start()
            return carry

        lax.fori_loop(1, frames, send, 0)

    along_z(0)
    along_x(0, 0)
    along_z(1)
    along_x(1, 0)
    gather_to_all(counts, 7)
    send_params()
    for d in range(1, depth):
        along_x(0, d)
        to_core(0, d)
    along_x(1, 1)
    along_y(1)
    for d in range(depth):
        to_core_late(0, d)

    weight_ready(0)

    def send_sums(buf, index, first, second):
        tiles = first.shape[1] // LANES
        first = jnp.sum(first, axis=0, keepdims=True)
        second = jnp.sum(second, axis=0, keepdims=True)
        for i in range(tiles):
            buf[me, i : i + 1, :] = first[:, LANES * i : LANES * (i + 1)]
            buf[me, tiles + i : tiles + i + 1, :] = second[:, LANES * i : LANES * (i + 1)]
        gather_to_all(buf, index)

    def get_sums(buf, index):
        total = arrived(buf, index)
        tiles = total.shape[0] // 2
        return rows_to_vec(total, 0, tiles), rows_to_vec(total, tiles, tiles)

    def moments(buf, index, inv):
        total, squares = get_sums(buf, index)
        mean = total * inv
        var = squares * inv - mean * mean
        return mean, lax.rsqrt(var + EPS)

    zero_n = jnp.zeros((8, narrow), F32)


    def unit_copy(unit, stage, src, dst, target):
        return pltpu.make_async_remote_copy(
            src_ref=src,
            dst_ref=dst,
            send_sem=rs_send.at[unit],
            recv_sem=rs_recv.at[unit, stage],
            device_id=target,
            device_id_type=MESH,
        )

    def columns(line, cut):
        return pl.ds(pl.multiple_of(line * cut, LANES), cut)

    def cores(unit):
        full, pair = full_refs[unit], pair_refs[unit]
        half = pair.shape[1]
        view = full.reshape(frames, 2 * half, full.shape[1])
        theirs = pl.ds(pl.multiple_of((1 - core) * half, half), half)
        return unit_copy(unit, 0, view.at[:, theirs], pair, partner)

    def near_copy(unit):
        pair, mid = pair_refs[unit], mid_refs[unit]
        half, width = pair.shape[1], pair.shape[2]
        if NEAR[unit] == "x":
            return unit_copy(unit, 1, pair.reshape(depth, 2, half, width).at[:, 1 - across], mid, x_peer)
        return unit_copy(unit, 1, pair.at[:, :, columns(1 - line_me, width // lines)], mid, y_peer)

    def near(unit):
        full, pair = full_refs[unit], pair_refs[unit]
        cores(unit).wait_recv()
        half = pair.shape[1]
        mine = pl.ds(pl.multiple_of(core * half, half), half)
        view = full.reshape(frames, 2 * half, full.shape[1])

        def add(f, carry):
            pair[f] = (pair[f].astype(F32) + view[f, mine, :].astype(F32)).astype(BF16)
            return carry

        lax.fori_loop(0, frames, add, 0)
        if NEAR[unit]:
            near_copy(unit).start()

    def far(unit):
        pair, mid, got = pair_refs[unit], mid_refs[unit], got_refs[unit]
        cut = pair.shape[2] // lines
        if NEAR[unit]:
            near_copy(unit).wait_recv()

        def add(k, carry):
            own = pair[2 * k + across] if NEAR[unit] == "x" else pair[k, :, columns(line_me, cut)]
            mid[k] = (mid[k].astype(F32) + own.astype(F32)).astype(BF16)
            return carry

        if NEAR[unit]:
            lax.fori_loop(0, mid.shape[0], add, 0)
        if not NEAR[unit]:
            slot_me = line_me * frames + frame
            got[slot_me] = pair[frame, :, columns(line_me, cut)]

            def send(k, carry):
                line = lax.rem(line_me + lax.div(k, frames), lines)
                owner = lax.rem(frame + lax.rem(k, frames), frames)
                src = pair.at[owner, :, columns(line, cut)]
                unit_copy(unit, 2, src, got.at[slot_me], (line * 2 + core, owner)).start()
                return carry

        elif NEAR[unit] == "x":
            slot_me = line_me * depth + along
            got[slot_me] = mid[along, :, columns(line_me, cut)]

            def send(k, carry):
                line = lax.rem(line_me + lax.div(k, depth), lines)
                deep = lax.rem(along + lax.rem(k, depth), depth)
                src = mid.at[deep, :, columns(line, cut)]
                unit_copy(unit, 2, src, got.at[slot_me], (line * 2 + core, deep * 2 + across)).start()
                return carry

        else:
            got[frame] = mid[frame]

            def send(k, carry):
                owner = lax.rem(frame + k, frames)
                unit_copy(unit, 2, mid.at[owner], got.at[frame], (clip, owner)).start()
                return carry

        lax.fori_loop(1, got.shape[0], send, 0)

    def owners(unit):
        got, fin = got_refs[unit], fin_refs[unit]
        half, cut = got.shape[1], got.shape[2]
        most = got.at[pl.ds(0, got.shape[0] - 1)]
        unit_copy(unit, 2, most, most, partner).wait_recv()
        spot = fin.at[pl.ds(pl.multiple_of(core * half, half), half), columns(line_me, cut)]
        spot[...] = jnp.sum(got[...].astype(F32), axis=0).astype(BF16)

        def send(k, carry):
            unit_copy(unit, 3, spot, spot, (lax.rem(clip + k, clips), frame)).start()
            return carry

        lax.fori_loop(1, clips, send, 0)

    def finished(unit):
        most = got_refs[unit].at[pl.ds(0, clips - 1)]
        unit_copy(unit, 3, most, most, partner).wait_recv()
        return fin_refs[unit]

    def sent(unit):
        pair, got = pair_refs[unit], got_refs[unit]
        unit_copy(unit, 0, pair, pair, partner).wait_send()
        if NEAR[unit]:
            near_copy(unit).wait_send()
        for count in (got.shape[0] - 1, clips - 1):
            most = got.at[pl.ds(0, count)]
            unit_copy(unit, 2, most, most, partner).wait_send()

    big = rows // 2

    def conv_one(i, carry):
        at = pl.ds(pl.multiple_of(i * big, big), big)
        v = dot(xm[at, :], wr[...])
        pre1[at, :] = v
        return carry[0] + part_sum(v), carry[1] + part_sum(v * v)

    sums = lax.fori_loop(0, 2, conv_one, (zero_n, zero_n))
    send_sums(st1, 1, *sums)
    for d in range(2, depth):
        along_x(1, d)
        along_y(d)
    along_z(2)
    along_x(2, 0)
    for d in range(depth):
        along_y_late(d)
    y_to_core()
    most = par.at[pl.ds(0, frames - 1)]
    pltpu.make_async_copy(most, most, st_recv.at[0]).wait()
    part_n = g1_ref.shape[0]
    part_w = g3_ref.shape[0]
    acc_n = [jnp.zeros((8, LANES), F32) for _ in range(nar_tiles)]
    acc_w = [jnp.zeros((8, LANES), F32) for _ in range(wide_tiles)]
    for f in range(frames):
        tile = par[f]
        spot = f * part_n
        shift = spot % LANES
        acc_n[spot // LANES] += pltpu.roll(tile, shift, 1) if shift else tile
        spot = f * part_w
        shift = spot % LANES
        acc_w[spot // LANES] += pltpu.roll(tile, shift, 1) if shift else tile
    gain1, bias1, gain2, bias2 = [jnp.concatenate([a[i : i + 1] for a in acc_n], axis=1) for i in range(4)]
    gain3, bias3 = [jnp.concatenate([a[i : i + 1] for a in acc_w], axis=1) for i in (4, 5)]
    inv_count = 1.0 / arrived(counts, 7)
    inv_n = jnp.concatenate([inv_count] * nar_tiles, axis=1)
    inv_w = jnp.concatenate([inv_count] * wide_tiles, axis=1)

    mean1, inv1 = moments(st1, 1, inv_n)
    scale1 = inv1 * gain1
    offset1 = bias1 - mean1 * scale1

    def both(v):
        return jnp.concatenate([v] * nar_tiles, axis=1)

    def act_one(i, carry):
        at = block_at(i)
        z = pre1[at, :] * scale1 + offset1
        s = sigmoid(z)
        m = both(mask[at, :])
        ms = m * s
        spad[1, pl.ds(pl.multiple_of(i * BLOCK + pad, 8), BLOCK), :] = ms * z
        slope1[at, :] = ms * (1.0 + z * (1.0 - s))
        return carry

    lax.fori_loop(0, blocks, act_one, 0)

    def spread():
        def shifted(i, carry):
            at = block_at(i)
            v = spad[1, pl.ds(pl.multiple_of(i * BLOCK + pad - 8, 8), BLOCK + 16), :]
            here = pl.ds(pl.multiple_of(i * BLOCK + pad, 8), BLOCK)
            spad[0, here, :] = pltpu.roll(v, 2, 0)[8 : 8 + BLOCK] * both(left_ok[at, :])
            spad[2, here, :] = pltpu.roll(v, BLOCK + 14, 0)[8 : 8 + BLOCK] * both(right_ok[at, :])
            return carry

        lax.fori_loop(0, blocks, shifted, 0)

    def gather_nine(flip):
        def step(i, carry):
            at = block_at(i)
            for tap in range(9):
                row_off, col_off = (tap // 3, tap % 3) if not flip else (2 - tap // 3, 2 - tap % 3)
                src = pl.ds(pl.multiple_of(i * BLOCK + pad * row_off, 8), BLOCK)
                nine[at, narrow * tap : narrow * (tap + 1)] = spad[col_off, src, :].astype(BF16)
            return carry

        lax.fori_loop(0, blocks, step, 0)

    spread()
    gather_nine(False)
    weight_ready(1)
    for d in range(1, depth):
        along_x(2, d)
        to_core(2, d)

    def conv_two(i, carry):
        at = pl.ds(pl.multiple_of(i * big, big), big)
        v = dot(nine[at, :], ws[...].reshape(9 * narrow, narrow))
        pre2[at, :] = v
        mv = both(mask[at, :]) * v
        return carry[0] + part_sum(mv), carry[1] + part_sum(mv * v)

    sums = lax.fori_loop(0, 2, conv_two, (zero_n, zero_n))
    send_sums(st2, 2, *sums)
    wrt[...] = wr[...].T
    a1t[...] = spad[1, pad : pad + rows, :].astype(BF16).T
    for d in range(depth):
        to_core_late(2, d)

    mean2, inv2 = moments(st2, 2, inv_n)
    scale2 = inv2 * gain2
    offset2 = bias2 - mean2 * scale2

    def act_two(i, carry):
        at = block_at(i)
        z = pre2[at, :] * scale2 + offset2
        s = sigmoid(z)
        ms = both(mask[at, :]) * s
        a = (ms * z).astype(BF16)
        act2[at, :] = a
        slope2[at, :] = ms * (1.0 + z * (1.0 - s))
        return carry + part_sum(a.astype(F32))

    act_sum = lax.fori_loop(0, blocks, act_two, zero_n)

    weight_ready(2)
    zero_w = jnp.zeros((8, channels), F32)

    wide = big

    def conv_three(i, carry):
        at = pl.ds(pl.multiple_of(i * wide, wide), wide)
        v = dot(act2[at, :], we[...])
        pre3[at, :] = v
        return carry + part_sum(v * v)

    squares = lax.fori_loop(0, rows // wide, conv_three, zero_w)
    st3[me, :, 0:narrow] = jnp.sum(act_sum, axis=0, keepdims=True)
    st3[me, :, narrow : narrow + channels] = jnp.sum(squares, axis=0, keepdims=True)
    gather_to_all(st3, 3)
    for tap in range(9):
        wst[narrow * tap : narrow * (tap + 1), :] = ws[tap].T
    wet[...] = we[...].T
    a2t[...] = act2[...].T
    copies_in(cs, 1).wait()
    to_rows(cs, ct_rows, 1).start()
    to_rows(cs, ct_rows, 1).wait()
    both_sums = arrived(st3, 3)
    left = both_sums[:, 0:narrow]
    parts = []
    for _ in range(3):
        parts.append(left.astype(BF16).astype(F32))
        left = left - parts[-1]
    exact = jnp.concatenate(parts + [jnp.zeros((5, narrow), F32)], axis=0).astype(BF16)
    mean3 = jnp.sum(dot(exact, we[...]), axis=0, keepdims=True) * inv_w
    inv3 = lax.rsqrt(both_sums[:, narrow:] * inv_w - mean3 * mean3 + EPS)
    scale3 = inv3 * gain3
    offset3 = bias3 - mean3 * scale3

    def from_rows(ref, index):
        return pltpu.make_async_copy(out_rows, ref.reshape(wide_tiles, rows, LANES), out_sem.at[index])

    def finish(i, carry):
        at = block_at(i)
        m = mask[at, :]
        first, second = [], []
        for j in range(wide_tiles):
            lanes = slice(LANES * j, LANES * (j + 1))
            p = pre3[at, lanes]
            t = p * scale3[:, lanes] + offset3[:, lanes] + xm[at, lanes].astype(F32)
            s = sigmoid(t)
            ms = m * s
            o = ms * t
            out_rows[j, at, :] = o.astype(BF16)
            g = ct_rows[j, at, :].astype(F32) * (ms + o * (1.0 - s))
            gt[at, lanes] = g
            first.append(part_sum(g))
            second.append(part_sum(g * p))
        return carry[0] + jnp.concatenate(first, axis=1), carry[1] + jnp.concatenate(second, axis=1)

    shift_own, slope_own = lax.fori_loop(0, blocks, finish, (zero_w, zero_w))
    shift_own = jnp.sum(shift_own, axis=0, keepdims=True)
    slope_own = (jnp.sum(slope_own, axis=0, keepdims=True) - mean3 * shift_own) * inv3
    pieces = [v[:, LANES * j : LANES * (j + 1)] for v in (shift_own, slope_own) for j in range(wide_tiles)]
    st4[me] = jnp.concatenate(pieces, axis=0).astype(BF16)
    gather_to_all(st4, 4)
    from_rows(out_ref, 0).start()
    shift3, slope_gain3 = get_sums(st4, 4)

    def back_terms(scale, inv, mean, shift_sum, gain_sum, inv_cnt):
        along = scale * inv * gain_sum * inv_cnt
        return along, scale * shift_sum * inv_cnt - mean * along

    along3, flat3 = back_terms(scale3, inv3, mean3, shift3, slope_gain3, inv_w)

    def back_three(i, carry):
        at = block_at(i)
        m = mask[at, :]
        for j in range(wide_tiles):
            lanes = slice(LANES * j, LANES * (j + 1))
            g = gt[at, lanes] * scale3[:, lanes] - pre3[at, lanes] * along3[:, lanes] - m * flat3[:, lanes]
            gp3[at, lanes] = g.astype(BF16)
        return carry

    lax.fori_loop(0, blocks, back_three, 0)

    d = dot(gp3[...], wet[...]) * slope2[...]
    dz[...] = d
    send_sums(st5, 5, part_sum(d), part_sum(d * ((pre2[...] - mean2) * inv2)))

    def grad_expand(i, carry):
        lanes = pl.ds(pl.multiple_of(i * 256, 256), 256)
        ge_ref[:, lanes] = dot(a2t[...], gp3[:, lanes]).astype(BF16)
        return carry

    lax.fori_loop(0, channels // 256, grad_expand, 0)
    if own_gather:
        cores(5).start()
        near(5)

    shift2, slope_gain2 = get_sums(st5, 5)
    along2, flat2 = back_terms(scale2, inv2, mean2, shift2, slope_gain2, inv_n)

    def back_two(i, carry):
        at = block_at(i)
        here = pl.ds(pl.multiple_of(i * BLOCK + pad, 8), BLOCK)
        m = both(mask[at, :])
        spad[1, here, :] = dz[at, :] * scale2 - m * (pre2[at, :] * along2 + flat2)
        return carry

    lax.fori_loop(0, blocks, back_two, 0)
    spread()
    gather_nine(True)

    def grad_spatial(row):
        wide_row = 3 * narrow
        gs_refs[row][...] = dot(a1t[...], nine[:, wide_row * row : wide_row * (row + 1)]).astype(BF16)
        if own_gather:
            cores(2 + row).start()

    grad_spatial(0)

    def back_spatial(i, carry):
        at = pl.ds(pl.multiple_of(i * big, big), big)
        d = dot(nine[at, :], wst[...]) * slope1[at, :]
        dz[at, :] = d
        return carry[0] + part_sum(d), carry[1] + part_sum(d * ((pre1[at, :] - mean1) * inv1))

    sums = lax.fori_loop(0, 2, back_spatial, (zero_n, zero_n))
    send_sums(st6, 6, *sums)
    if own_gather:
        near(2)
    grad_spatial(1)
    grad_spatial(2)
    if own_gather:
        near(3)
        near(4)
        far(5)

    shift1, slope_gain1 = get_sums(st6, 6)
    along1, flat1 = back_terms(scale1, inv1, mean1, shift1, slope_gain1, inv_n)

    def back_one(i, carry):
        at = block_at(i)
        g = dz[at, :] * scale1 - both(mask[at, :]) * (pre1[at, :] * along1 + flat1)
        gp1[at, :] = g.astype(BF16)
        return carry

    lax.fori_loop(0, blocks, back_one, 0)

    for i in range(2):
        height = channels // 2
        gr_refs[i][...] = dot(xt[height * i : height * (i + 1), :], gp1[...]).astype(BF16)
        if own_gather:
            cores(i).start()
    if own_gather:
        far(2)
        near(0)
        near(1)
    from_rows(out_ref, 0).wait()

    def grad_in(i, carry):
        at = pl.ds(pl.multiple_of(i * wide, wide), wide)
        m = mask[at, :]
        back = dot(gp1[at, :], wrt[...])
        for j in range(wide_tiles):
            lanes = slice(LANES * j, LANES * (j + 1))
            out_rows[j, at, :] = (m * back[:, lanes] + gt[at, lanes]).astype(BF16)
        return carry

    lax.fori_loop(0, rows // wide, grad_in, 0)
    if own_gather:
        far(3)
        far(4)
    from_rows(gin_ref, 1).start()

    def own_part(ref, v):
        width = ref.shape[0]
        spot = frame * width
        tile = jnp.zeros((1, LANES), F32)
        for t in range(v.shape[1] // LANES):
            tile = jnp.where(lax.div(spot, LANES) == t, v[:, LANES * t : LANES * (t + 1)], tile)
        tile = pltpu.roll(jnp.concatenate([tile] * 8, axis=0), lax.rem(LANES - lax.rem(spot, LANES), LANES), 1)
        ref[...] = tile[0, 0:width]

    own_part(vec1_gain, slope_gain1)
    own_part(vec1_shift, shift1)
    own_part(vec2_gain, slope_gain2)
    own_part(vec2_shift, shift2)
    own_part(vec3_gain, slope_gain3)
    own_part(vec3_shift, shift3)

    if own_gather:
        owners(5)
        far(0)
        far(1)
        for unit in (2, 3, 4, 0, 1):
            owners(unit)
        ge_out[...] = finished(5)[...].astype(F32)
        for row in range(3):
            fin = finished(2 + row)
            for c in range(3):
                gs_out[3 * row + c] = fin[:, narrow * c : narrow * (c + 1)].astype(F32)
        for i in range(2):
            gr_out[piece * i : piece * (i + 1), :] = finished(i)[...].astype(F32)
    else:
        for i in range(2):
            gr_out[channels // 2 * i : channels // 2 * (i + 1), :] = gr_refs[i][...]
        for row in range(3):
            gs_out[:, 3 * narrow * row : 3 * narrow * (row + 1)] = gs_refs[row][...]
        ge_out[...] = ge_ref[...]
    for index in range(3):
        weight_sent(index)
    if own_gather:
        for unit in range(units):
            sent(unit)
    for buf in (counts, st1, st2, st3, st4, st5, st6):
        most = buf.at[pl.ds(0, devices - 1)]
        pltpu.make_async_copy(most, most, st_send.at[0]).wait()
    most = par.at[pl.ds(0, frames - 1)]
    pltpu.make_async_copy(most, most, st_send.at[1]).wait()
    from_rows(gin_ref, 1).wait()


def deliver_kernel(count, *refs):
    sources, targets, sems = refs[:count], refs[count : 2 * count], refs[2 * count]
    for i in range(2):
        for j in range(sources[i].shape[0]):
            part = targets[i].at[:, :, LANES * j : LANES * (j + 1)]
            pltpu.make_async_copy(sources[i].at[j], part, sems.at[i]).start()
    for i in range(2, count):
        pltpu.make_async_copy(sources[i], targets[i], sems.at[i]).start()
    for i in range(count):
        pltpu.make_async_copy(sources[i], sources[i], sems.at[i]).wait()


def deliver(arrays, big):
    count = len(arrays)
    shapes = [big, big] + [jax.ShapeDtypeStruct(a.shape, a.dtype) for a in arrays[2:]]
    return pl.pallas_call(
        functools.partial(deliver_kernel, count),
        out_shape=tuple(shapes),
        in_specs=[pl.BlockSpec(memory_space=pltpu.VMEM)] * count,
        out_specs=(pl.BlockSpec(memory_space=pl.ANY),) * count,
        scratch_shapes=[pltpu.SemaphoreType.DMA((count,))],
        compiler_params=pltpu.CompilerParams(vmem_limit_bytes=1024 * 1024),
    )(*arrays)


def on_device(
    dims,
    x_in,
    cotangent,
    w_reduce,
    w_spatial,
    w_expand,
    gain_one,
    shift_one,
    gain_two,
    shift_two,
    gain_three,
    shift_three,
    bucket,
    frame_count,
):
    clips, frames = dims
    slots, side, _, channels = x_in.shape
    narrow = w_reduce.shape[1]
    pixels = side * side
    rows = pixels * slots
    tiles = channels // LANES
    devices = clips * frames
    own_gather = clips == 4 and all(n % 32 == 0 for n in (w_reduce.shape[0], w_spatial.shape[2], w_expand.shape[0]))
    w_spatial = w_spatial.reshape(9, -1, narrow)
    if not own_gather:
        w_reduce = lax.all_gather(w_reduce, "frame", axis=0, tiled=True)
        w_spatial = lax.all_gather(w_spatial, "frame", axis=1, tiled=True)
        w_expand = lax.all_gather(w_expand, "frame", axis=0, tiled=True)

    def by_pixel(v):
        return jnp.transpose(v, (1, 2, 0, 3)).reshape(pixels, slots, channels)

    any_spec = pl.BlockSpec(memory_space=pl.ANY)
    vmem = pl.BlockSpec(memory_space=pltpu.VMEM)
    smem = pl.BlockSpec(memory_space=pltpu.SMEM)
    big = jax.ShapeDtypeStruct((pixels, slots, channels), BF16)
    staged = pltpu.VMEM((tiles, pixels, slots, LANES), BF16)
    native = pltpu.VMEM((tiles, rows, LANES), BF16)
    narrow_f32 = pltpu.VMEM((rows, narrow), F32)
    wide_f32 = pltpu.VMEM((rows, channels), F32)
    lanes_f32 = pltpu.VMEM((rows, LANES), F32)

    def stats(count):
        return pltpu.VMEM((devices, count, LANES), F32)

    if own_gather:
        grad_shapes = (
            pltpu.VMEM((channels // frames, narrow), F32),
            pltpu.VMEM((9, narrow // frames, narrow), F32),
            pltpu.VMEM((narrow // frames, channels), F32),
        )
    else:
        grad_shapes = (
            jax.ShapeDtypeStruct((channels, narrow), BF16),
            jax.ShapeDtypeStruct((narrow, 9 * narrow), BF16),
            jax.ShapeDtypeStruct((narrow, channels), BF16),
        )
    wholes = (*(((channels // 2, narrow),) * 2), *(((narrow, 3 * narrow),) * 3), (narrow, channels))
    lines = clips // 2
    unit_scratch = [pltpu.VMEM(shape, BF16) for shape in wholes]
    if own_gather:
        cuts = [(height // frames // 2, width) for height, width in wholes]
        unit_scratch += [pltpu.VMEM((frames, half, width), BF16) for half, width in cuts]
        unit_scratch += [
            pltpu.VMEM((frames // 2, half, width) if hop == "x" else (frames, half, width // lines), BF16)
            for (half, width), hop in zip(cuts, NEAR)
        ]
        unit_scratch += [
            pltpu.VMEM((frames if hop else frames * lines, half, width // lines), BF16)
            for (half, width), hop in zip(cuts, NEAR)
        ]
        unit_scratch += [pltpu.VMEM((2 * half, width), BF16) for half, width in cuts]

    results = pl.pallas_call(
        functools.partial(block_kernel, (clips, frames, side, own_gather)),
        out_shape=(
            staged,
            staged,
            *grad_shapes,
            *(pltpu.VMEM((narrow // frames,), F32),) * 4,
            *(pltpu.VMEM((channels // frames,), F32),) * 2,
        ),
        in_specs=[any_spec] * 5 + [vmem] * 6 + [smem] * 2,
        out_specs=(vmem,) * 11,
        scratch_shapes=[
            staged,
            staged,
            native,
            native,
            native,
            pltpu.VMEM((rows, channels), BF16),
            pltpu.VMEM((channels, rows), BF16),
            pltpu.VMEM((narrow, rows), BF16),
            pltpu.VMEM((narrow, rows), BF16),
            lanes_f32,
            lanes_f32,
            lanes_f32,
            pltpu.VMEM((channels, narrow), BF16),
            pltpu.VMEM((9, narrow, narrow), BF16),
            pltpu.VMEM((narrow, channels), BF16),
            pltpu.VMEM((9 * narrow, narrow), BF16),
            pltpu.VMEM((channels, narrow), BF16),
            pltpu.VMEM((narrow, channels), BF16),
            narrow_f32,
            narrow_f32,
            narrow_f32,
            narrow_f32,
            narrow_f32,
            pltpu.VMEM((3, rows + 4 * side, narrow), F32),
            pltpu.VMEM((rows, narrow), BF16),
            pltpu.VMEM((rows, 9 * narrow), BF16),
            wide_f32,
            wide_f32,
            pltpu.VMEM((rows, channels), BF16),
            pltpu.VMEM((rows, narrow), BF16),
            pltpu.VMEM((frames, 8, LANES), F32),
            stats(1),
            stats(2 * narrow // LANES),
            stats(2 * narrow // LANES),
            pltpu.VMEM((devices, 1, narrow + channels), F32),
            pltpu.VMEM((devices, 2 * tiles, LANES), BF16),
            stats(2 * narrow // LANES),
            stats(2 * narrow // LANES),
            pltpu.SemaphoreType.DMA((5,)),
            pltpu.SemaphoreType.DMA((3,)),
            pltpu.SemaphoreType.DMA((3, frames + 3)),
            pltpu.SemaphoreType.DMA((2,)),
            pltpu.SemaphoreType.DMA((8,)),
            pltpu.SemaphoreType.DMA((2,)),
            pltpu.SemaphoreType.DMA((len(NEAR),)),
            pltpu.SemaphoreType.DMA((len(NEAR), 4)),
            *unit_scratch,
        ],
        compiler_params=pltpu.CompilerParams(
            collective_id=0, has_side_effects=True, vmem_limit_bytes=VMEM_BYTES
        ),
    )(
        by_pixel(x_in),
        by_pixel(cotangent),
        w_reduce,
        w_spatial,
        w_expand,
        gain_one,
        shift_one,
        gain_two,
        shift_two,
        gain_three,
        shift_three,
        bucket,
        frame_count,
    )

    def by_frame(v):
        return jnp.transpose(v.reshape(side, side, slots, channels), (2, 0, 1, 3))

    def owned(v):
        part = lax.psum_scatter(v, "frame", scatter_dimension=0, tiled=True)
        return lax.psum(part, "clip").astype(F32)

    if own_gather:
        out, gin, gr, gs, ge, *vectors = deliver(results, big)
    else:
        gr, gs, ge = [owned(v) for v in results[2:5]]
        gs = gs.reshape(-1, 9, narrow).transpose(1, 0, 2)
        out, gin, gr, gs, ge, *vectors = deliver((*results[:2], gr, gs, ge, *results[5:]), big)
    return (by_frame(out), by_frame(gin), gr, gs.reshape(3, 3, -1, narrow), ge, *vectors)


def solution(mesh):
    by_device = P(("clip", "frame"))
    shard = P("frame")
    spatial = P(None, None, "frame", None)
    return jax.shard_map(
        functools.partial(on_device, (mesh.shape["clip"], mesh.shape["frame"])),
        mesh=mesh,
        in_specs=(by_device, by_device, shard, spatial) + (shard,) * 7 + (by_device, by_device),
        out_specs=(by_device, by_device, shard, spatial) + (shard,) * 7,
        check_vma=False,
    )
```

```python
import functools

import jax
import jax.numpy as jnp
from jax import lax
from jax.experimental import pallas as pl
from jax.experimental.pallas import tpu as pltpu
from jax.sharding import PartitionSpec as P

SMALL_SIDE = 14
EPS = 1e-05
LANES = 128
BLOCK = 80
VMEM_BYTES = 52 * 1024 * 1024
MESH = pl.DeviceIdType.MESH
NEAR = ("x", "y", "y", "x", "y", "x")
F32 = jnp.float32
BF16 = jnp.bfloat16


def sigmoid(v):
    return 0.5 * jnp.tanh(0.5 * v) + 0.5


def part_sum(v):
    rows, width = v.shape
    return jnp.sum(v.reshape(rows // 8, 8, width), axis=0)


def dot(a, b):
    return jnp.dot(a, b, preferred_element_type=F32)


def rows_to_vec(tile, first, count):
    return jnp.concatenate([tile[first + i : first + i + 1] for i in range(count)], axis=1)


def block_kernel(
    dims,
    x_hbm,
    ct_hbm,
    wr_hbm,
    ws_hbm,
    we_hbm,
    g1_ref,
    b1_ref,
    g2_ref,
    b2_ref,
    g3_ref,
    b3_ref,
    bucket_ref,
    count_ref,
    out_ref,
    gin_ref,
    gr_out,
    gs_out,
    ge_out,
    vec1_gain,
    vec1_shift,
    vec2_gain,
    vec2_shift,
    vec3_gain,
    vec3_shift,
    xs,
    cs,
    x_rows,
    ct_rows,
    out_rows,
    xm,
    xt,
    a1t,
    a2t,
    mask,
    left_ok,
    right_ok,
    wr,
    ws,
    we,
    wst,
    wet,
    wrt,
    pre1,
    slope1,
    pre2,
    slope2,
    dz,
    spad,
    act2,
    nine,
    pre3,
    gt,
    gp3,
    gp1,
    par,
    counts,
    st1,
    st2,
    st3,
    st4,
    st5,
    st6,
    local_sem,
    wsend,
    wrecv,
    st_send,
    st_recv,
    out_sem,
    rs_send,
    rs_recv,
    *unit_refs,
):
    clips, frames, side, own_gather = dims
    units = len(NEAR)
    full_refs, pair_refs, mid_refs, got_refs, fin_refs = [unit_refs[units * i : units * (i + 1)] for i in range(5)]
    gr_refs, gs_refs, ge_ref = full_refs[0:2], full_refs[2:5], full_refs[5]
    devices = clips * frames
    clip = lax.axis_index("clip")
    frame = lax.axis_index("frame")
    me = clip * frames + frame
    core = lax.rem(clip, 2)
    partner = (clip + 1 - 2 * core, frame)
    rows = xm.shape[0]
    channels = xm.shape[1]
    narrow = wr.shape[1]
    wide_tiles = channels // LANES
    nar_tiles = narrow // LANES
    blocks = rows // BLOCK
    pad = 2 * side
    lines = clips // 2
    line_me = lax.div(clip, 2)
    y_peer = (lax.rem(clip + 2, clips), frame)

    small = devices <= 32 and clips & (clips - 1) == 0 and frames & (frames - 1) == 0

    def flips(v, size):
        return [(1 - 2 * lax.rem(lax.div(v, 1 << i), 2)) * (1 << i) for i in range(size.bit_length() - 1)]

    clip_flips, frame_flips = flips(clip, clips), flips(frame, frames)

    def to_others(action):
        if small:
            for b in reversed(range(frames)):
                to_frame = sum((d for i, d in enumerate(frame_flips) if b >> i & 1), frame)
                for a in reversed(range(clips)):
                    if a or b:
                        action((sum((d for i, d in enumerate(clip_flips) if a >> i & 1), clip), to_frame))
            return
        for a in range(clips):
            to_clip = lax.rem(clip + a, clips)

            def step(b, carry):
                action((to_clip, lax.rem(frame + b, frames)))
                return carry

            lax.fori_loop(0 if a else 1, frames, step, 0)

    for j in range(wide_tiles):
        lanes = pl.ds(LANES * j, LANES)
        pltpu.make_async_copy(x_hbm.at[:, :, lanes], xs.at[j], local_sem.at[0]).start()
    if own_gather:
        part_r = wr_hbm.shape[0]
        part_s = ws_hbm.shape[1]
        part_e = we_hbm.shape[0]
        own_r = wr.at[pl.ds(pl.multiple_of(frame * part_r, part_r), part_r)]
        own_s = ws.at[:, pl.ds(pl.multiple_of(frame * part_s, part_s), part_s)]
        own_e = we.at[pl.ds(pl.multiple_of(frame * part_e, part_e), part_e)]
    else:
        own_r, own_s, own_e = wr, ws, we
    own_copies = [
        pltpu.make_async_copy(wr_hbm, own_r, local_sem.at[2]),
        pltpu.make_async_copy(ws_hbm, own_s, local_sem.at[3]),
        pltpu.make_async_copy(we_hbm, own_e, local_sem.at[4]),
    ]
    for copy in own_copies:
        copy.start()
    for j in range(wide_tiles):
        lanes = pl.ds(LANES * j, LANES)
        pltpu.make_async_copy(ct_hbm.at[:, :, lanes], cs.at[j], local_sem.at[1]).start()

    def copies_in(staged, index):
        return pltpu.make_async_copy(staged, staged, local_sem.at[index])

    def to_rows(staged, native, index):
        return pltpu.make_async_copy(staged.reshape(wide_tiles, rows, LANES), native, local_sem.at[index])

    barrier = pltpu.get_barrier_semaphore()

    to_others(lambda target: pl.semaphore_signal(barrier, inc=1, device_id=target, device_id_type=MESH))

    row_id = lax.broadcasted_iota(jnp.int32, (rows, LANES), 0)
    pixel = row_id >> 1
    slot = row_id & 1
    line = (pixel * 3277) >> 16
    col = pixel - line * side
    extent = [jnp.where(bucket_ref[f] == 0, SMALL_SIDE, side) for f in range(2)]
    limit = [jnp.where(count_ref[0] > f, extent[f], 0) for f in range(2)]
    bound = jnp.where(slot == 0, limit[0], limit[1])
    live = ((line < bound) & (col < bound)).astype(F32)
    mask[...] = live
    left_ok[...] = (col >= 1).astype(F32)
    right_ok[...] = (col <= side - 2).astype(F32)

    par[frame] = jnp.zeros((8, LANES), F32)
    for i, ref in enumerate((g1_ref, b1_ref, g2_ref, b2_ref, g3_ref, b3_ref)):
        width = ref.shape[0]
        par[frame, i : i + 1, 0:width] = ref[...].astype(F32).reshape(1, width)
    counts[me] = jnp.sum(live, axis=0, keepdims=True)

    copies_in(xs, 0).wait()
    to_rows(xs, x_rows, 0).start()
    to_rows(xs, x_rows, 0).wait()

    def block_at(i):
        return pl.ds(pl.multiple_of(i * BLOCK, BLOCK), BLOCK)

    def mask_in(i, carry):
        at = block_at(i)
        m = mask[at, :].astype(BF16)
        for j in range(wide_tiles):
            xm[at, LANES * j : LANES * (j + 1)] = x_rows[j, at, :] * m
        return carry

    lax.fori_loop(0, blocks, mask_in, 0)
    edge = jnp.zeros((3, pad, narrow), F32)
    spad[:, 0:pad, :] = edge
    spad[:, pad + rows : 2 * pad + rows, :] = edge
    turned = xm[...].T
    if own_gather:
        piece = part_r // 2
        for f in range(2 * frames):
            spot = (f % 2) * frames + f // 2
            xt[piece * spot : piece * (spot + 1), :] = turned[piece * f : piece * (f + 1)]
    else:
        xt[...] = turned
    for copy in own_copies:
        copy.wait()

    pl.semaphore_wait(barrier, devices - 1)

    def gather_to_all(buf, index):
        def send(target):
            pltpu.make_async_remote_copy(
                src_ref=buf.at[me],
                dst_ref=buf.at[me],
                send_sem=st_send.at[0],
                recv_sem=st_recv.at[index],
                device_id=target,
                device_id_type=MESH,
            ).start()

        to_others(send)

    def arrived(buf, index):
        most = buf.at[pl.ds(0, devices - 1)]
        pltpu.make_async_copy(most, most, st_recv.at[index]).wait()
        return jnp.sum(buf[...].astype(F32), axis=0)

    across = lax.rem(frame, 2)
    along = lax.div(frame, 2)
    depth = frames // 2
    x_peer = (clip, along * 2 + 1 - across)
    xy_peer = (lax.rem(clip + 2, clips), along * 2 + 1 - across)

    def owner_at(d, side_x):
        return lax.rem(along - d + depth, depth) * 2 + side_x

    if own_gather:

        kinds = ((wr, 0, part_r), (ws, 1, part_s), (we, 0, part_e))

        def piece_of(index, owner, columns=None):
            ref, axis, part = kinds[index]
            at = pl.ds(pl.multiple_of(owner * part + core * (part // 2), part // 2), part // 2)
            if axis == 0:
                return ref.at[at]
            return ref.at[:, at] if columns is None else ref.at[:, at, columns]

        def own_columns(index):
            if index != 1:
                return None
            cut = narrow // lines
            return pl.ds(pl.multiple_of(line_me * cut, LANES), cut)

        def weight_copy(index, sem, owner, target, columns=None):
            part = piece_of(index, owner, columns)
            return pltpu.make_async_remote_copy(
                src_ref=part,
                dst_ref=part,
                send_sem=wsend.at[index],
                recv_sem=wrecv.at[index, sem],
                device_id=target,
                device_id_type=MESH,
            )

        def blocks_of(index, count, wide=True):
            ref, axis, part = kinds[index]
            size = pl.ds(0, count * (part // 2))
            if axis == 0:
                return ref.at[size]
            return ref.at[:, size] if wide else ref.at[:, size, pl.ds(0, narrow // lines)]

        def blocks_wait(sem, view):
            pltpu.make_async_copy(view, view, sem).wait()

        def along_z(index):
            for d in range(1, depth):
                target = (clip, lax.rem(along + d, depth) * 2 + across)
                weight_copy(index, d, frame, target, own_columns(index)).start()

        def along_x(index, d):
            columns = own_columns(index)
            if d:
                weight_copy(index, d, owner_at(d, across), x_peer, columns).wait_recv()
            weight_copy(index, depth + d, owner_at(d, across), x_peer, columns).start()

        def along_y(d):
            weight_copy(1, 2 * depth + 1, owner_at(d, across), y_peer, own_columns(1)).start()

        def along_xy(d):
            weight_copy(1, 2 * depth + 2, owner_at(d, across), xy_peer, own_columns(1)).start()

        def y_to_core():
            blocks_wait(wrecv.at[1, 2 * depth + 1], blocks_of(1, depth - 1, False))
            for d in range(1, depth):
                to_core(1, d)
            for d in range(depth):
                weight_copy(1, depth + d, owner_at(d, 1 - across), partner, own_columns(1)).wait_recv()
            blocks_wait(wrecv.at[1, 2 * depth + 2], blocks_of(1, depth, False))
            for d in range(depth):
                weight_copy(1, 2 * depth, owner_at(d, 1 - across), partner).start()

        def to_core(index, d):
            weight_copy(index, 2 * depth, owner_at(d, across), partner).start()

        def to_core_late(index, d):
            owner = owner_at(d, 1 - across)
            weight_copy(index, depth + d, owner, partner).wait_recv()
            weight_copy(index, 2 * depth, owner, partner).start()

        def weight_ready(index):
            blocks_wait(wrecv.at[index, 2 * depth], blocks_of(index, 2 * depth - 1))

        def weight_sent(index):
            blocks_wait(wsend.at[index], blocks_of(index, 4 * depth - 2))

    else:

        def nothing(*args):
            pass

        along_z = along_x = along_y = along_xy = y_to_core = nothing
        to_core = to_core_late = weight_ready = weight_sent = nothing

    def send_params():
        def send(b, carry):
            pltpu.make_async_remote_copy(
                src_ref=par.at[frame],
                dst_ref=par.at[frame],
                send_sem=st_send.at[1],
                recv_sem=st_recv.at[0],
                device_id=(clip, lax.rem(frame + b, frames)),
                device_id_type=MESH,
            ).start()
            return carry

        lax.fori_loop(1, frames, send, 0)

    along_z(0)
    along_x(0, 0)
    along_z(1)
    along_x(1, 0)
    along_xy(0)
    gather_to_all(counts, 7)
    send_params()
    for d in range(1, depth):
        along_x(0, d)
        to_core(0, d)
    along_x(1, 1)
    along_xy(1)
    along_y(1)
    for d in range(depth):
        to_core_late(0, d)

    for d in range(2, depth):
        along_x(1, d)
        along_xy(d)
        along_y(d)

    weight_ready(0)

    def send_sums(buf, index, first, second):
        tiles = first.shape[1] // LANES
        first = jnp.sum(first, axis=0, keepdims=True)
        second = jnp.sum(second, axis=0, keepdims=True)
        for i in range(tiles):
            buf[me, i : i + 1, :] = first[:, LANES * i : LANES * (i + 1)]
            buf[me, tiles + i : tiles + i + 1, :] = second[:, LANES * i : LANES * (i + 1)]
        gather_to_all(buf, index)

    def get_sums(buf, index):
        total = arrived(buf, index)
        tiles = total.shape[0] // 2
        return rows_to_vec(total, 0, tiles), rows_to_vec(total, tiles, tiles)

    def moments(buf, index, inv):
        total, squares = get_sums(buf, index)
        mean = total * inv
        var = squares * inv - mean * mean
        return mean, lax.rsqrt(var + EPS)

    zero_n = jnp.zeros((8, narrow), F32)


    def unit_copy(unit, stage, src, dst, target):
        return pltpu.make_async_remote_copy(
            src_ref=src,
            dst_ref=dst,
            send_sem=rs_send.at[unit],
            recv_sem=rs_recv.at[unit, stage],
            device_id=target,
            device_id_type=MESH,
        )

    def columns(line, cut):
        return pl.ds(pl.multiple_of(line * cut, LANES), cut)

    def cores(unit):
        full, pair = full_refs[unit], pair_refs[unit]
        half = pair.shape[1]
        view = full.reshape(frames, 2 * half, full.shape[1])
        theirs = pl.ds(pl.multiple_of((1 - core) * half, half), half)
        return unit_copy(unit, 0, view.at[:, theirs], pair, partner)

    def near_copy(unit):
        pair, mid = pair_refs[unit], mid_refs[unit]
        half, width = pair.shape[1], pair.shape[2]
        if NEAR[unit] == "x":
            return unit_copy(unit, 1, pair.reshape(depth, 2, half, width).at[:, 1 - across], mid, x_peer)
        return unit_copy(unit, 1, pair.at[:, :, columns(1 - line_me, width // lines)], mid, y_peer)

    def near(unit):
        full, pair = full_refs[unit], pair_refs[unit]
        cores(unit).wait_recv()
        half = pair.shape[1]
        mine = pl.ds(pl.multiple_of(core * half, half), half)
        view = full.reshape(frames, 2 * half, full.shape[1])

        def add(f, carry):
            pair[f] = (pair[f].astype(F32) + view[f, mine, :].astype(F32)).astype(BF16)
            return carry

        lax.fori_loop(0, frames, add, 0)
        if NEAR[unit]:
            near_copy(unit).start()

    def far(unit):
        pair, mid, got = pair_refs[unit], mid_refs[unit], got_refs[unit]
        cut = pair.shape[2] // lines
        if NEAR[unit]:
            near_copy(unit).wait_recv()

        def add(k, carry):
            own = pair[2 * k + across] if NEAR[unit] == "x" else pair[k, :, columns(line_me, cut)]
            mid[k] = (mid[k].astype(F32) + own.astype(F32)).astype(BF16)
            return carry

        if NEAR[unit]:
            lax.fori_loop(0, mid.shape[0], add, 0)
        if not NEAR[unit]:
            slot_me = line_me * frames + frame
            got[slot_me] = pair[frame, :, columns(line_me, cut)]

            def send(k, carry):
                line = lax.rem(line_me + lax.div(k, frames), lines)
                owner = lax.rem(frame + lax.rem(k, frames), frames)
                src = pair.at[owner, :, columns(line, cut)]
                unit_copy(unit, 2, src, got.at[slot_me], (line * 2 + core, owner)).start()
                return carry

        elif NEAR[unit] == "x":
            slot_me = line_me * depth + along
            got[slot_me] = mid[along, :, columns(line_me, cut)]

            def send(k, carry):
                line = lax.rem(line_me + lax.div(k, depth), lines)
                deep = lax.rem(along + lax.rem(k, depth), depth)
                src = mid.at[deep, :, columns(line, cut)]
                unit_copy(unit, 2, src, got.at[slot_me], (line * 2 + core, deep * 2 + across)).start()
                return carry

        else:
            got[frame] = mid[frame]

            def send(k, carry):
                owner = lax.rem(frame + k, frames)
                unit_copy(unit, 2, mid.at[owner], got.at[frame], (clip, owner)).start()
                return carry

        lax.fori_loop(1, got.shape[0], send, 0)

    def owners(unit):
        got, fin = got_refs[unit], fin_refs[unit]
        half, cut = got.shape[1], got.shape[2]
        most = got.at[pl.ds(0, got.shape[0] - 1)]
        unit_copy(unit, 2, most, most, partner).wait_recv()
        spot = fin.at[pl.ds(pl.multiple_of(core * half, half), half), columns(line_me, cut)]
        spot[...] = jnp.sum(got[...].astype(F32), axis=0).astype(BF16)

        def send(k, carry):
            unit_copy(unit, 3, spot, spot, (lax.rem(clip + k, clips), frame)).start()
            return carry

        lax.fori_loop(1, clips, send, 0)

    def finished(unit):
        most = got_refs[unit].at[pl.ds(0, clips - 1)]
        unit_copy(unit, 3, most, most, partner).wait_recv()
        return fin_refs[unit]

    def sent(unit):
        pair, got = pair_refs[unit], got_refs[unit]
        unit_copy(unit, 0, pair, pair, partner).wait_send()
        if NEAR[unit]:
            near_copy(unit).wait_send()
        for count in (got.shape[0] - 1, clips - 1):
            most = got.at[pl.ds(0, count)]
            unit_copy(unit, 2, most, most, partner).wait_send()

    big = rows // 2

    def conv_one(i, carry):
        at = pl.ds(pl.multiple_of(i * big, big), big)
        v = dot(xm[at, :], wr[...])
        pre1[at, :] = v
        return carry[0] + part_sum(v), carry[1] + part_sum(v * v)

    sums = lax.fori_loop(0, 2, conv_one, (zero_n, zero_n))
    send_sums(st1, 1, *sums)
    along_z(2)
    along_x(2, 0)
    y_to_core()
    most = par.at[pl.ds(0, frames - 1)]
    pltpu.make_async_copy(most, most, st_recv.at[0]).wait()
    part_n = g1_ref.shape[0]
    part_w = g3_ref.shape[0]
    acc_n = [jnp.zeros((8, LANES), F32) for _ in range(nar_tiles)]
    acc_w = [jnp.zeros((8, LANES), F32) for _ in range(wide_tiles)]
    for f in range(frames):
        tile = par[f]
        spot = f * part_n
        shift = spot % LANES
        acc_n[spot // LANES] += pltpu.roll(tile, shift, 1) if shift else tile
        spot = f * part_w
        shift = spot % LANES
        acc_w[spot // LANES] += pltpu.roll(tile, shift, 1) if shift else tile
    gain1, bias1, gain2, bias2 = [jnp.concatenate([a[i : i + 1] for a in acc_n], axis=1) for i in range(4)]
    gain3, bias3 = [jnp.concatenate([a[i : i + 1] for a in acc_w], axis=1) for i in (4, 5)]
    inv_count = 1.0 / arrived(counts, 7)
    inv_n = jnp.concatenate([inv_count] * nar_tiles, axis=1)
    inv_w = jnp.concatenate([inv_count] * wide_tiles, axis=1)

    mean1, inv1 = moments(st1, 1, inv_n)
    scale1 = inv1 * gain1
    offset1 = bias1 - mean1 * scale1

    def both(v):
        return jnp.concatenate([v] * nar_tiles, axis=1)

    def act_one(i, carry):
        at = block_at(i)
        z = pre1[at, :] * scale1 + offset1
        s = sigmoid(z)
        m = both(mask[at, :])
        ms = m * s
        spad[1, pl.ds(pl.multiple_of(i * BLOCK + pad, 8), BLOCK), :] = ms * z
        slope1[at, :] = ms * (1.0 + z * (1.0 - s))
        return carry

    lax.fori_loop(0, blocks, act_one, 0)

    def spread():
        def shifted(i, carry):
            at = block_at(i)
            v = spad[1, pl.ds(pl.multiple_of(i * BLOCK + pad - 8, 8), BLOCK + 16), :]
            here = pl.ds(pl.multiple_of(i * BLOCK + pad, 8), BLOCK)
            spad[0, here, :] = pltpu.roll(v, 2, 0)[8 : 8 + BLOCK] * both(left_ok[at, :])
            spad[2, here, :] = pltpu.roll(v, BLOCK + 14, 0)[8 : 8 + BLOCK] * both(right_ok[at, :])
            return carry

        lax.fori_loop(0, blocks, shifted, 0)

    def gather_nine(flip):
        def step(i, carry):
            at = block_at(i)
            for tap in range(9):
                row_off, col_off = (tap // 3, tap % 3) if not flip else (2 - tap // 3, 2 - tap % 3)
                src = pl.ds(pl.multiple_of(i * BLOCK + pad * row_off, 8), BLOCK)
                nine[at, narrow * tap : narrow * (tap + 1)] = spad[col_off, src, :].astype(BF16)
            return carry

        lax.fori_loop(0, blocks, step, 0)

    spread()
    gather_nine(False)
    weight_ready(1)
    for d in range(1, depth):
        along_x(2, d)
        to_core(2, d)

    def conv_two(i, carry):
        at = pl.ds(pl.multiple_of(i * big, big), big)
        v = dot(nine[at, :], ws[...].reshape(9 * narrow, narrow))
        pre2[at, :] = v
        mv = both(mask[at, :]) * v
        return carry[0] + part_sum(mv), carry[1] + part_sum(mv * v)

    sums = lax.fori_loop(0, 2, conv_two, (zero_n, zero_n))
    send_sums(st2, 2, *sums)
    wrt[...] = wr[...].T
    a1t[...] = spad[1, pad : pad + rows, :].astype(BF16).T
    for d in range(depth):
        to_core_late(2, d)

    mean2, inv2 = moments(st2, 2, inv_n)
    scale2 = inv2 * gain2
    offset2 = bias2 - mean2 * scale2

    def act_two(i, carry):
        at = block_at(i)
        z = pre2[at, :] * scale2 + offset2
        s = sigmoid(z)
        ms = both(mask[at, :]) * s
        a = (ms * z).astype(BF16)
        act2[at, :] = a
        slope2[at, :] = ms * (1.0 + z * (1.0 - s))
        return carry + part_sum(a.astype(F32))

    act_sum = lax.fori_loop(0, blocks, act_two, zero_n)

    weight_ready(2)
    zero_w = jnp.zeros((8, channels), F32)

    wide = big

    def conv_three(i, carry):
        at = pl.ds(pl.multiple_of(i * wide, wide), wide)
        v = dot(act2[at, :], we[...])
        pre3[at, :] = v
        return carry + part_sum(v * v)

    squares = lax.fori_loop(0, rows // wide, conv_three, zero_w)
    st3[me, :, 0:narrow] = jnp.sum(act_sum, axis=0, keepdims=True)
    st3[me, :, narrow : narrow + channels] = jnp.sum(squares, axis=0, keepdims=True)
    gather_to_all(st3, 3)
    for tap in range(9):
        wst[narrow * tap : narrow * (tap + 1), :] = ws[tap].T
    wet[...] = we[...].T
    a2t[...] = act2[...].T
    copies_in(cs, 1).wait()
    to_rows(cs, ct_rows, 1).start()
    to_rows(cs, ct_rows, 1).wait()
    both_sums = arrived(st3, 3)
    left = both_sums[:, 0:narrow]
    parts = []
    for _ in range(3):
        parts.append(left.astype(BF16).astype(F32))
        left = left - parts[-1]
    exact = jnp.concatenate(parts + [jnp.zeros((5, narrow), F32)], axis=0).astype(BF16)
    mean3 = jnp.sum(dot(exact, we[...]), axis=0, keepdims=True) * inv_w
    inv3 = lax.rsqrt(both_sums[:, narrow:] * inv_w - mean3 * mean3 + EPS)
    scale3 = inv3 * gain3
    offset3 = bias3 - mean3 * scale3

    def from_rows(ref, index):
        return pltpu.make_async_copy(out_rows, ref.reshape(wide_tiles, rows, LANES), out_sem.at[index])

    def finish(i, carry):
        at = block_at(i)
        m = mask[at, :]
        first, second = [], []
        for j in range(wide_tiles):
            lanes = slice(LANES * j, LANES * (j + 1))
            p = pre3[at, lanes]
            t = p * scale3[:, lanes] + offset3[:, lanes] + xm[at, lanes].astype(F32)
            s = sigmoid(t)
            ms = m * s
            o = ms * t
            out_rows[j, at, :] = o.astype(BF16)
            g = ct_rows[j, at, :].astype(F32) * (ms + o * (1.0 - s))
            gt[at, lanes] = g
            first.append(part_sum(g))
            second.append(part_sum(g * p))
        return carry[0] + jnp.concatenate(first, axis=1), carry[1] + jnp.concatenate(second, axis=1)

    shift_own, slope_own = lax.fori_loop(0, blocks, finish, (zero_w, zero_w))
    shift_own = jnp.sum(shift_own, axis=0, keepdims=True)
    slope_own = (jnp.sum(slope_own, axis=0, keepdims=True) - mean3 * shift_own) * inv3
    pieces = [v[:, LANES * j : LANES * (j + 1)] for v in (shift_own, slope_own) for j in range(wide_tiles)]
    st4[me] = jnp.concatenate(pieces, axis=0).astype(BF16)
    gather_to_all(st4, 4)
    from_rows(out_ref, 0).start()
    shift3, slope_gain3 = get_sums(st4, 4)

    def back_terms(scale, inv, mean, shift_sum, gain_sum, inv_cnt):
        along = scale * inv * gain_sum * inv_cnt
        return along, scale * shift_sum * inv_cnt - mean * along

    along3, flat3 = back_terms(scale3, inv3, mean3, shift3, slope_gain3, inv_w)

    def back_three(i, carry):
        at = pl.ds(pl.multiple_of(i * big, big), big)
        m = mask[at, :]
        tiles = []
        for j in range(wide_tiles):
            lanes = slice(LANES * j, LANES * (j + 1))
            g = gt[at, lanes] * scale3[:, lanes] - pre3[at, lanes] * along3[:, lanes] - m * flat3[:, lanes]
            tiles.append(g.astype(BF16))
            gp3[at, lanes] = tiles[-1]
        d = dot(jnp.concatenate(tiles, axis=1), wet[...]) * slope2[at, :]
        dz[at, :] = d
        return carry[0] + part_sum(d), carry[1] + part_sum(d * ((pre2[at, :] - mean2) * inv2))

    sums = lax.fori_loop(0, 2, back_three, (zero_n, zero_n))
    send_sums(st5, 5, *sums)

    def grad_expand(i, carry):
        lanes = pl.ds(pl.multiple_of(i * 256, 256), 256)
        ge_ref[:, lanes] = dot(a2t[...], gp3[:, lanes]).astype(BF16)
        return carry

    lax.fori_loop(0, channels // 256, grad_expand, 0)
    if own_gather:
        cores(5).start()
        near(5)

    shift2, slope_gain2 = get_sums(st5, 5)
    along2, flat2 = back_terms(scale2, inv2, mean2, shift2, slope_gain2, inv_n)

    def back_two(i, carry):
        at = block_at(i)
        here = pl.ds(pl.multiple_of(i * BLOCK + pad, 8), BLOCK)
        m = both(mask[at, :])
        spad[1, here, :] = dz[at, :] * scale2 - m * (pre2[at, :] * along2 + flat2)
        return carry

    lax.fori_loop(0, blocks, back_two, 0)
    spread()
    gather_nine(True)

    def grad_spatial(row):
        wide_row = 3 * narrow
        gs_refs[row][...] = dot(a1t[...], nine[:, wide_row * row : wide_row * (row + 1)]).astype(BF16)
        if own_gather:
            cores(2 + row).start()

    grad_spatial(0)

    def back_spatial(i, carry):
        at = pl.ds(pl.multiple_of(i * big, big), big)
        d = dot(nine[at, :], wst[...]) * slope1[at, :]
        dz[at, :] = d
        return carry[0] + part_sum(d), carry[1] + part_sum(d * ((pre1[at, :] - mean1) * inv1))

    sums = lax.fori_loop(0, 2, back_spatial, (zero_n, zero_n))
    send_sums(st6, 6, *sums)
    if own_gather:
        near(2)
    grad_spatial(1)
    grad_spatial(2)
    if own_gather:
        near(3)
        near(4)
        far(5)

    shift1, slope_gain1 = get_sums(st6, 6)
    along1, flat1 = back_terms(scale1, inv1, mean1, shift1, slope_gain1, inv_n)

    def back_one(i, carry):
        at = block_at(i)
        g = dz[at, :] * scale1 - both(mask[at, :]) * (pre1[at, :] * along1 + flat1)
        gp1[at, :] = g.astype(BF16)
        return carry

    lax.fori_loop(0, blocks, back_one, 0)

    for i in range(2):
        height = channels // 2
        gr_refs[i][...] = dot(xt[height * i : height * (i + 1), :], gp1[...]).astype(BF16)
        if own_gather:
            cores(i).start()
    if own_gather:
        far(2)
        near(0)
        near(1)
    from_rows(out_ref, 0).wait()

    def grad_in(i, carry):
        at = pl.ds(pl.multiple_of(i * wide, wide), wide)
        m = mask[at, :]
        back = dot(gp1[at, :], wrt[...])
        for j in range(wide_tiles):
            lanes = slice(LANES * j, LANES * (j + 1))
            out_rows[j, at, :] = (m * back[:, lanes] + gt[at, lanes]).astype(BF16)
        return carry

    lax.fori_loop(0, rows // wide, grad_in, 0)
    if own_gather:
        far(3)
        far(4)
    from_rows(gin_ref, 1).start()

    def own_part(ref, v):
        width = ref.shape[0]
        spot = frame * width
        tile = jnp.zeros((1, LANES), F32)
        for t in range(v.shape[1] // LANES):
            tile = jnp.where(lax.div(spot, LANES) == t, v[:, LANES * t : LANES * (t + 1)], tile)
        tile = pltpu.roll(jnp.concatenate([tile] * 8, axis=0), lax.rem(LANES - lax.rem(spot, LANES), LANES), 1)
        ref[...] = tile[0, 0:width]

    own_part(vec1_gain, slope_gain1)
    own_part(vec1_shift, shift1)
    own_part(vec2_gain, slope_gain2)
    own_part(vec2_shift, shift2)
    own_part(vec3_gain, slope_gain3)
    own_part(vec3_shift, shift3)

    if own_gather:
        owners(5)
        far(0)
        far(1)
        for unit in (2, 3, 4, 0, 1):
            owners(unit)
        ge_out[...] = finished(5)[...].astype(F32)
        for row in range(3):
            fin = finished(2 + row)
            for c in range(3):
                gs_out[3 * row + c] = fin[:, narrow * c : narrow * (c + 1)].astype(F32)
        for i in range(2):
            gr_out[piece * i : piece * (i + 1), :] = finished(i)[...].astype(F32)
    else:
        for i in range(2):
            gr_out[channels // 2 * i : channels // 2 * (i + 1), :] = gr_refs[i][...]
        for row in range(3):
            gs_out[:, 3 * narrow * row : 3 * narrow * (row + 1)] = gs_refs[row][...]
        ge_out[...] = ge_ref[...]
    for index in range(3):
        weight_sent(index)
    if own_gather:
        for unit in range(units):
            sent(unit)
    for buf in (counts, st1, st2, st3, st4, st5, st6):
        most = buf.at[pl.ds(0, devices - 1)]
        pltpu.make_async_copy(most, most, st_send.at[0]).wait()
    most = par.at[pl.ds(0, frames - 1)]
    pltpu.make_async_copy(most, most, st_send.at[1]).wait()
    from_rows(gin_ref, 1).wait()


def deliver_kernel(count, *refs):
    sources, targets, sems = refs[:count], refs[count : 2 * count], refs[2 * count]
    for i in range(2):
        for j in range(sources[i].shape[0]):
            part = targets[i].at[:, :, LANES * j : LANES * (j + 1)]
            pltpu.make_async_copy(sources[i].at[j], part, sems.at[i]).start()
    for i in range(2, count):
        pltpu.make_async_copy(sources[i], targets[i], sems.at[i]).start()
    for i in range(count):
        pltpu.make_async_copy(sources[i], sources[i], sems.at[i]).wait()


def deliver(arrays, big):
    count = len(arrays)
    shapes = [big, big] + [jax.ShapeDtypeStruct(a.shape, a.dtype) for a in arrays[2:]]
    return pl.pallas_call(
        functools.partial(deliver_kernel, count),
        out_shape=tuple(shapes),
        in_specs=[pl.BlockSpec(memory_space=pltpu.VMEM)] * count,
        out_specs=(pl.BlockSpec(memory_space=pl.ANY),) * count,
        scratch_shapes=[pltpu.SemaphoreType.DMA((count,))],
        compiler_params=pltpu.CompilerParams(vmem_limit_bytes=1024 * 1024),
    )(*arrays)


def on_device(
    dims,
    x_in,
    cotangent,
    w_reduce,
    w_spatial,
    w_expand,
    gain_one,
    shift_one,
    gain_two,
    shift_two,
    gain_three,
    shift_three,
    bucket,
    frame_count,
):
    clips, frames = dims
    slots, side, _, channels = x_in.shape
    narrow = w_reduce.shape[1]
    pixels = side * side
    rows = pixels * slots
    tiles = channels // LANES
    devices = clips * frames
    own_gather = clips == 4 and all(n % 32 == 0 for n in (w_reduce.shape[0], w_spatial.shape[2], w_expand.shape[0]))
    w_spatial = w_spatial.reshape(9, -1, narrow)
    if not own_gather:
        w_reduce = lax.all_gather(w_reduce, "frame", axis=0, tiled=True)
        w_spatial = lax.all_gather(w_spatial, "frame", axis=1, tiled=True)
        w_expand = lax.all_gather(w_expand, "frame", axis=0, tiled=True)

    def by_pixel(v):
        return jnp.transpose(v, (1, 2, 0, 3)).reshape(pixels, slots, channels)

    any_spec = pl.BlockSpec(memory_space=pl.ANY)
    vmem = pl.BlockSpec(memory_space=pltpu.VMEM)
    smem = pl.BlockSpec(memory_space=pltpu.SMEM)
    big = jax.ShapeDtypeStruct((pixels, slots, channels), BF16)
    staged = pltpu.VMEM((tiles, pixels, slots, LANES), BF16)
    native = pltpu.VMEM((tiles, rows, LANES), BF16)
    narrow_f32 = pltpu.VMEM((rows, narrow), F32)
    wide_f32 = pltpu.VMEM((rows, channels), F32)
    lanes_f32 = pltpu.VMEM((rows, LANES), F32)

    def stats(count):
        return pltpu.VMEM((devices, count, LANES), F32)

    if own_gather:
        grad_shapes = (
            pltpu.VMEM((channels // frames, narrow), F32),
            pltpu.VMEM((9, narrow // frames, narrow), F32),
            pltpu.VMEM((narrow // frames, channels), F32),
        )
    else:
        grad_shapes = (
            jax.ShapeDtypeStruct((channels, narrow), BF16),
            jax.ShapeDtypeStruct((narrow, 9 * narrow), BF16),
            jax.ShapeDtypeStruct((narrow, channels), BF16),
        )
    wholes = (*(((channels // 2, narrow),) * 2), *(((narrow, 3 * narrow),) * 3), (narrow, channels))
    lines = clips // 2
    unit_scratch = [pltpu.VMEM(shape, BF16) for shape in wholes]
    if own_gather:
        cuts = [(height // frames // 2, width) for height, width in wholes]
        unit_scratch += [pltpu.VMEM((frames, half, width), BF16) for half, width in cuts]
        unit_scratch += [
            pltpu.VMEM((frames // 2, half, width) if hop == "x" else (frames, half, width // lines), BF16)
            for (half, width), hop in zip(cuts, NEAR)
        ]
        unit_scratch += [
            pltpu.VMEM((frames if hop else frames * lines, half, width // lines), BF16)
            for (half, width), hop in zip(cuts, NEAR)
        ]
        unit_scratch += [pltpu.VMEM((2 * half, width), BF16) for half, width in cuts]

    results = pl.pallas_call(
        functools.partial(block_kernel, (clips, frames, side, own_gather)),
        out_shape=(
            staged,
            staged,
            *grad_shapes,
            *(pltpu.VMEM((narrow // frames,), F32),) * 4,
            *(pltpu.VMEM((channels // frames,), F32),) * 2,
        ),
        in_specs=[any_spec] * 5 + [vmem] * 6 + [smem] * 2,
        out_specs=(vmem,) * 11,
        scratch_shapes=[
            staged,
            staged,
            native,
            native,
            native,
            pltpu.VMEM((rows, channels), BF16),
            pltpu.VMEM((channels, rows), BF16),
            pltpu.VMEM((narrow, rows), BF16),
            pltpu.VMEM((narrow, rows), BF16),
            lanes_f32,
            lanes_f32,
            lanes_f32,
            pltpu.VMEM((channels, narrow), BF16),
            pltpu.VMEM((9, narrow, narrow), BF16),
            pltpu.VMEM((narrow, channels), BF16),
            pltpu.VMEM((9 * narrow, narrow), BF16),
            pltpu.VMEM((channels, narrow), BF16),
            pltpu.VMEM((narrow, channels), BF16),
            narrow_f32,
            narrow_f32,
            narrow_f32,
            narrow_f32,
            narrow_f32,
            pltpu.VMEM((3, rows + 4 * side, narrow), F32),
            pltpu.VMEM((rows, narrow), BF16),
            pltpu.VMEM((rows, 9 * narrow), BF16),
            wide_f32,
            wide_f32,
            pltpu.VMEM((rows, channels), BF16),
            pltpu.VMEM((rows, narrow), BF16),
            pltpu.VMEM((frames, 8, LANES), F32),
            stats(1),
            stats(2 * narrow // LANES),
            stats(2 * narrow // LANES),
            pltpu.VMEM((devices, 1, narrow + channels), F32),
            pltpu.VMEM((devices, 2 * tiles, LANES), BF16),
            stats(2 * narrow // LANES),
            stats(2 * narrow // LANES),
            pltpu.SemaphoreType.DMA((5,)),
            pltpu.SemaphoreType.DMA((3,)),
            pltpu.SemaphoreType.DMA((3, frames + 3)),
            pltpu.SemaphoreType.DMA((2,)),
            pltpu.SemaphoreType.DMA((8,)),
            pltpu.SemaphoreType.DMA((2,)),
            pltpu.SemaphoreType.DMA((len(NEAR),)),
            pltpu.SemaphoreType.DMA((len(NEAR), 4)),
            *unit_scratch,
        ],
        compiler_params=pltpu.CompilerParams(
            collective_id=0, has_side_effects=True, vmem_limit_bytes=VMEM_BYTES
        ),
    )(
        by_pixel(x_in),
        by_pixel(cotangent),
        w_reduce,
        w_spatial,
        w_expand,
        gain_one,
        shift_one,
        gain_two,
        shift_two,
        gain_three,
        shift_three,
        bucket,
        frame_count,
    )

    def by_frame(v):
        return jnp.transpose(v.reshape(side, side, slots, channels), (2, 0, 1, 3))

    def owned(v):
        part = lax.psum_scatter(v, "frame", scatter_dimension=0, tiled=True)
        return lax.psum(part, "clip").astype(F32)

    if own_gather:
        out, gin, gr, gs, ge, *vectors = deliver(results, big)
    else:
        gr, gs, ge = [owned(v) for v in results[2:5]]
        gs = gs.reshape(-1, 9, narrow).transpose(1, 0, 2)
        out, gin, gr, gs, ge, *vectors = deliver((*results[:2], gr, gs, ge, *results[5:]), big)
    return (by_frame(out), by_frame(gin), gr, gs.reshape(3, 3, -1, narrow), ge, *vectors)


def solution(mesh):
    by_device = P(("clip", "frame"))
    shard = P("frame")
    spatial = P(None, None, "frame", None)
    return jax.shard_map(
        functools.partial(on_device, (mesh.shape["clip"], mesh.shape["frame"])),
        mesh=mesh,
        in_specs=(by_device, by_device, shard, spatial) + (shard,) * 7 + (by_device, by_device),
        out_specs=(by_device, by_device, shard, spatial) + (shard,) * 7,
        check_vma=False,
    )
```

```python
import functools

import jax
import jax.numpy as jnp
from jax import lax
from jax.experimental import pallas as pl
from jax.experimental.pallas import tpu as pltpu
from jax.sharding import PartitionSpec as P

SMALL_SIDE = 14
EPS = 1e-05
LANES = 128
BLOCK = 80
VMEM_BYTES = 52 * 1024 * 1024
MESH = pl.DeviceIdType.MESH
NEAR = ("x", "y", "y", "x", "y", "x")
F32 = jnp.float32
BF16 = jnp.bfloat16


def sigmoid(v):
    return 0.5 * jnp.tanh(0.5 * v) + 0.5


def part_sum(v):
    rows, width = v.shape
    return jnp.sum(v.reshape(rows // 8, 8, width), axis=0)


def dot(a, b):
    return jnp.dot(a, b, preferred_element_type=F32)


def rows_to_vec(tile, first, count):
    return jnp.concatenate([tile[first + i : first + i + 1] for i in range(count)], axis=1)


def block_kernel(
    dims,
    x_hbm,
    ct_hbm,
    wr_hbm,
    ws_hbm,
    we_hbm,
    g1_ref,
    b1_ref,
    g2_ref,
    b2_ref,
    g3_ref,
    b3_ref,
    bucket_ref,
    count_ref,
    out_ref,
    gin_ref,
    gr_out,
    gs_out,
    ge_out,
    vec1_gain,
    vec1_shift,
    vec2_gain,
    vec2_shift,
    vec3_gain,
    vec3_shift,
    xs,
    cs,
    x_rows,
    ct_rows,
    out_rows,
    xm,
    xt,
    a1t,
    a2t,
    mask,
    left_ok,
    right_ok,
    wr,
    ws,
    we,
    wst,
    wet,
    wrt,
    pre1,
    slope1,
    pre2,
    slope2,
    dz,
    spad,
    act2,
    still,
    moved,
    pre3,
    gt,
    gp3,
    gp1,
    par,
    counts,
    st1,
    st2,
    st3,
    st4,
    st5,
    st6,
    local_sem,
    wsend,
    wrecv,
    st_send,
    st_recv,
    out_sem,
    rs_send,
    rs_recv,
    *unit_refs,
):
    clips, frames, side, own_gather = dims
    units = len(NEAR)
    full_refs, pair_refs, mid_refs, got_refs, fin_refs = [unit_refs[units * i : units * (i + 1)] for i in range(5)]
    gr_refs, gs_refs, ge_ref = full_refs[0:2], full_refs[2:5], full_refs[5]
    devices = clips * frames
    clip = lax.axis_index("clip")
    frame = lax.axis_index("frame")
    me = clip * frames + frame
    core = lax.rem(clip, 2)
    partner = (clip + 1 - 2 * core, frame)
    rows = xm.shape[0]
    channels = xm.shape[1]
    narrow = wr.shape[1]
    wide_tiles = channels // LANES
    nar_tiles = narrow // LANES
    blocks = rows // BLOCK
    step_rows = 2 * side
    pad = step_rows + 8
    lines = clips // 2
    line_me = lax.div(clip, 2)
    y_peer = (lax.rem(clip + 2, clips), frame)

    small = devices <= 32 and clips & (clips - 1) == 0 and frames & (frames - 1) == 0

    def flips(v, size):
        return [(1 - 2 * lax.rem(lax.div(v, 1 << i), 2)) * (1 << i) for i in range(size.bit_length() - 1)]

    clip_flips, frame_flips = flips(clip, clips), flips(frame, frames)

    def to_others(action):
        if small:
            for b in reversed(range(frames)):
                to_frame = sum((d for i, d in enumerate(frame_flips) if b >> i & 1), frame)
                for a in reversed(range(clips)):
                    if a or b:
                        action((sum((d for i, d in enumerate(clip_flips) if a >> i & 1), clip), to_frame))
            return
        for a in range(clips):
            to_clip = lax.rem(clip + a, clips)

            def step(b, carry):
                action((to_clip, lax.rem(frame + b, frames)))
                return carry

            lax.fori_loop(0 if a else 1, frames, step, 0)

    for j in range(wide_tiles):
        lanes = pl.ds(LANES * j, LANES)
        pltpu.make_async_copy(x_hbm.at[:, :, lanes], xs.at[j], local_sem.at[0]).start()
    if own_gather:
        part_r = wr_hbm.shape[0]
        part_s = ws_hbm.shape[1]
        part_e = we_hbm.shape[0]
        own_r = wr.at[pl.ds(pl.multiple_of(frame * part_r, part_r), part_r)]
        own_s = ws.at[:, pl.ds(pl.multiple_of(frame * part_s, part_s), part_s)]
        own_e = we.at[pl.ds(pl.multiple_of(frame * part_e, part_e), part_e)]
    else:
        own_r, own_s, own_e = wr, ws, we
    own_copies = [
        pltpu.make_async_copy(wr_hbm, own_r, local_sem.at[2]),
        pltpu.make_async_copy(ws_hbm, own_s, local_sem.at[3]),
        pltpu.make_async_copy(we_hbm, own_e, local_sem.at[4]),
    ]
    for copy in own_copies:
        copy.start()
    for j in range(wide_tiles):
        lanes = pl.ds(LANES * j, LANES)
        pltpu.make_async_copy(ct_hbm.at[:, :, lanes], cs.at[j], local_sem.at[1]).start()

    def copies_in(staged, index):
        return pltpu.make_async_copy(staged, staged, local_sem.at[index])

    def to_rows(staged, native, index):
        return pltpu.make_async_copy(staged.reshape(wide_tiles, rows, LANES), native, local_sem.at[index])

    barrier = pltpu.get_barrier_semaphore()

    to_others(lambda target: pl.semaphore_signal(barrier, inc=1, device_id=target, device_id_type=MESH))

    row_id = lax.broadcasted_iota(jnp.int32, (rows, LANES), 0)
    pixel = row_id >> 1
    slot = row_id & 1
    line = (pixel * 3277) >> 16
    col = pixel - line * side
    extent = [jnp.where(bucket_ref[f] == 0, SMALL_SIDE, side) for f in range(2)]
    limit = [jnp.where(count_ref[0] > f, extent[f], 0) for f in range(2)]
    bound = jnp.where(slot == 0, limit[0], limit[1])
    live = ((line < bound) & (col < bound)).astype(F32)
    mask[...] = live
    for ref, ok in ((left_ok, col >= 1), (right_ok, col <= side - 2)):
        ref[0:8, :] = jnp.zeros((8, LANES), F32)
        ref[8 : 8 + rows, :] = ok.astype(F32)
        ref[8 + rows : 16 + rows, :] = jnp.zeros((8, LANES), F32)

    par[frame] = jnp.zeros((8, LANES), F32)
    for i, ref in enumerate((g1_ref, b1_ref, g2_ref, b2_ref, g3_ref, b3_ref)):
        width = ref.shape[0]
        par[frame, i : i + 1, 0:width] = ref[...].astype(F32).reshape(1, width)
    counts[me] = jnp.sum(live, axis=0, keepdims=True)

    copies_in(xs, 0).wait()
    to_rows(xs, x_rows, 0).start()
    to_rows(xs, x_rows, 0).wait()

    def block_at(i):
        return pl.ds(pl.multiple_of(i * BLOCK, BLOCK), BLOCK)

    def mask_in(i, carry):
        at = block_at(i)
        m = mask[at, :].astype(BF16)
        for j in range(wide_tiles):
            xm[at, LANES * j : LANES * (j + 1)] = x_rows[j, at, :] * m
        return carry

    lax.fori_loop(0, blocks, mask_in, 0)
    edge = jnp.zeros((pad, narrow), F32)
    spad[0:pad, :] = edge
    spad[pad + rows : 2 * pad + rows, :] = edge
    edge = jnp.zeros((3, step_rows - 8, narrow), BF16)
    moved[:, 0 : step_rows - 8, :] = edge
    moved[:, step_rows + 8 + rows : 2 * step_rows + rows, :] = edge
    turned = xm[...].T
    if own_gather:
        piece = part_r // 2
        for f in range(2 * frames):
            spot = (f % 2) * frames + f // 2
            xt[piece * spot : piece * (spot + 1), :] = turned[piece * f : piece * (f + 1)]
    else:
        xt[...] = turned
    for copy in own_copies:
        copy.wait()

    pl.semaphore_wait(barrier, devices - 1)

    def gather_to_all(buf, index):
        def send(target):
            pltpu.make_async_remote_copy(
                src_ref=buf.at[me],
                dst_ref=buf.at[me],
                send_sem=st_send.at[0],
                recv_sem=st_recv.at[index],
                device_id=target,
                device_id_type=MESH,
            ).start()

        to_others(send)

    def arrived(buf, index):
        most = buf.at[pl.ds(0, devices - 1)]
        pltpu.make_async_copy(most, most, st_recv.at[index]).wait()
        return jnp.sum(buf[...].astype(F32), axis=0)

    across = lax.rem(frame, 2)
    along = lax.div(frame, 2)
    depth = frames // 2
    x_peer = (clip, along * 2 + 1 - across)
    xy_peer = (lax.rem(clip + 2, clips), along * 2 + 1 - across)

    def owner_at(d, side_x):
        return lax.rem(along - d + depth, depth) * 2 + side_x

    if own_gather:

        kinds = ((wr, 0, part_r), (ws, 1, part_s), (we, 0, part_e))

        def piece_of(index, owner, columns=None):
            ref, axis, part = kinds[index]
            at = pl.ds(pl.multiple_of(owner * part + core * (part // 2), part // 2), part // 2)
            if axis == 0:
                return ref.at[at]
            return ref.at[:, at] if columns is None else ref.at[:, at, columns]

        def own_columns(index):
            if index != 1:
                return None
            cut = narrow // lines
            return pl.ds(pl.multiple_of(line_me * cut, LANES), cut)

        def weight_copy(index, sem, owner, target, columns=None):
            part = piece_of(index, owner, columns)
            return pltpu.make_async_remote_copy(
                src_ref=part,
                dst_ref=part,
                send_sem=wsend.at[index],
                recv_sem=wrecv.at[index, sem],
                device_id=target,
                device_id_type=MESH,
            )

        def blocks_of(index, count, wide=True):
            ref, axis, part = kinds[index]
            size = pl.ds(0, count * (part // 2))
            if axis == 0:
                return ref.at[size]
            return ref.at[:, size] if wide else ref.at[:, size, pl.ds(0, narrow // lines)]

        def blocks_wait(sem, view):
            pltpu.make_async_copy(view, view, sem).wait()

        def along_z(index):
            for d in range(1, depth):
                target = (clip, lax.rem(along + d, depth) * 2 + across)
                weight_copy(index, d, frame, target, own_columns(index)).start()

        def along_x(index, d):
            columns = own_columns(index)
            if d:
                weight_copy(index, d, owner_at(d, across), x_peer, columns).wait_recv()
            weight_copy(index, depth + d, owner_at(d, across), x_peer, columns).start()

        def along_y(d):
            weight_copy(1, 2 * depth + 1, owner_at(d, across), y_peer, own_columns(1)).start()

        def along_xy(d):
            weight_copy(1, 2 * depth + 2, owner_at(d, across), xy_peer, own_columns(1)).start()

        def y_to_core():
            blocks_wait(wrecv.at[1, 2 * depth + 1], blocks_of(1, depth - 1, False))
            for d in range(1, depth):
                to_core(1, d)
            for d in range(depth):
                weight_copy(1, depth + d, owner_at(d, 1 - across), partner, own_columns(1)).wait_recv()
            blocks_wait(wrecv.at[1, 2 * depth + 2], blocks_of(1, depth, False))
            for d in range(depth):
                weight_copy(1, 2 * depth, owner_at(d, 1 - across), partner).start()

        def to_core(index, d):
            weight_copy(index, 2 * depth, owner_at(d, across), partner).start()

        def to_core_late(index, d):
            owner = owner_at(d, 1 - across)
            weight_copy(index, depth + d, owner, partner).wait_recv()
            weight_copy(index, 2 * depth, owner, partner).start()

        def weight_ready(index):
            blocks_wait(wrecv.at[index, 2 * depth], blocks_of(index, 2 * depth - 1))

        def weight_sent(index):
            blocks_wait(wsend.at[index], blocks_of(index, 4 * depth - 2))

    else:

        def nothing(*args):
            pass

        along_z = along_x = along_y = along_xy = y_to_core = nothing
        to_core = to_core_late = weight_ready = weight_sent = nothing

    def send_params():
        def send(b, carry):
            pltpu.make_async_remote_copy(
                src_ref=par.at[frame],
                dst_ref=par.at[frame],
                send_sem=st_send.at[1],
                recv_sem=st_recv.at[0],
                device_id=(clip, lax.rem(frame + b, frames)),
                device_id_type=MESH,
            ).start()
            return carry

        lax.fori_loop(1, frames, send, 0)

    along_z(0)
    along_x(0, 0)
    along_z(1)
    along_x(1, 0)
    along_xy(0)
    gather_to_all(counts, 7)
    send_params()
    for d in range(1, depth):
        along_x(0, d)
        to_core(0, d)
    along_x(1, 1)
    along_xy(1)
    along_y(1)
    for d in range(depth):
        to_core_late(0, d)

    for d in range(2, depth):
        along_x(1, d)
        along_xy(d)
        along_y(d)

    weight_ready(0)

    def send_sums(buf, index, first, second):
        tiles = first.shape[1] // LANES
        first = jnp.sum(first, axis=0, keepdims=True)
        second = jnp.sum(second, axis=0, keepdims=True)
        for i in range(tiles):
            buf[me, i : i + 1, :] = first[:, LANES * i : LANES * (i + 1)]
            buf[me, tiles + i : tiles + i + 1, :] = second[:, LANES * i : LANES * (i + 1)]
        gather_to_all(buf, index)

    def get_sums(buf, index):
        total = arrived(buf, index)
        tiles = total.shape[0] // 2
        return rows_to_vec(total, 0, tiles), rows_to_vec(total, tiles, tiles)

    def moments(buf, index, inv):
        total, squares = get_sums(buf, index)
        mean = total * inv
        var = squares * inv - mean * mean
        return mean, lax.rsqrt(var + EPS)

    zero_n = jnp.zeros((8, narrow), F32)


    def unit_copy(unit, stage, src, dst, target):
        return pltpu.make_async_remote_copy(
            src_ref=src,
            dst_ref=dst,
            send_sem=rs_send.at[unit],
            recv_sem=rs_recv.at[unit, stage],
            device_id=target,
            device_id_type=MESH,
        )

    def columns(line, cut):
        return pl.ds(pl.multiple_of(line * cut, LANES), cut)

    def cores(unit):
        full, pair = full_refs[unit], pair_refs[unit]
        half = pair.shape[1]
        view = full.reshape(frames, 2 * half, full.shape[1])
        theirs = pl.ds(pl.multiple_of((1 - core) * half, half), half)
        return unit_copy(unit, 0, view.at[:, theirs], pair, partner)

    def near_copy(unit):
        pair, mid = pair_refs[unit], mid_refs[unit]
        half, width = pair.shape[1], pair.shape[2]
        if NEAR[unit] == "x":
            return unit_copy(unit, 1, pair.reshape(depth, 2, half, width).at[:, 1 - across], mid, x_peer)
        return unit_copy(unit, 1, pair.at[:, :, columns(1 - line_me, width // lines)], mid, y_peer)

    def near(unit):
        full, pair = full_refs[unit], pair_refs[unit]
        cores(unit).wait_recv()
        half = pair.shape[1]
        mine = pl.ds(pl.multiple_of(core * half, half), half)
        view = full.reshape(frames, 2 * half, full.shape[1])

        def add(f, carry):
            pair[f] = (pair[f].astype(F32) + view[f, mine, :].astype(F32)).astype(BF16)
            return carry

        lax.fori_loop(0, frames, add, 0)
        near_copy(unit).start()

    def far(unit):
        pair, mid, got = pair_refs[unit], mid_refs[unit], got_refs[unit]
        cut = pair.shape[2] // lines
        near_copy(unit).wait_recv()

        def add(k, carry):
            own = pair[2 * k + across] if NEAR[unit] == "x" else pair[k, :, columns(line_me, cut)]
            mid[k] = (mid[k].astype(F32) + own.astype(F32)).astype(BF16)
            return carry

        lax.fori_loop(0, mid.shape[0], add, 0)
        if NEAR[unit] == "x":
            slot_me = line_me * depth + along
            got[slot_me] = mid[along, :, columns(line_me, cut)]

            def send(k, carry):
                deep, line = lax.div(k, lines), lax.rem(k, lines)

                @pl.when(jnp.logical_or(deep != along, line != line_me))
                def _():
                    src = mid.at[deep, :, columns(line, cut)]
                    unit_copy(unit, 2, src, got.at[slot_me], (line * 2 + core, deep * 2 + across)).start()

                return carry

        else:
            got[frame] = mid[frame]

            def send(owner, carry):
                @pl.when(owner != frame)
                def _():
                    unit_copy(unit, 2, mid.at[owner], got.at[frame], (clip, owner)).start()

                return carry

        lax.fori_loop(0, got.shape[0], send, 0)

    def owners(unit):
        got, fin = got_refs[unit], fin_refs[unit]
        half, cut = got.shape[1], got.shape[2]
        most = got.at[pl.ds(0, got.shape[0] - 1)]
        unit_copy(unit, 2, most, most, partner).wait_recv()
        spot = fin.at[pl.ds(pl.multiple_of(core * half, half), half), columns(line_me, cut)]
        spot[...] = jnp.sum(got[...].astype(F32), axis=0).astype(BF16)

        def send(k, carry):
            unit_copy(unit, 3, spot, spot, (lax.rem(clip + k, clips), frame)).start()
            return carry

        lax.fori_loop(1, clips, send, 0)

    def finished(unit):
        most = got_refs[unit].at[pl.ds(0, clips - 1)]
        unit_copy(unit, 3, most, most, partner).wait_recv()
        return fin_refs[unit]

    def sent(unit):
        pair, got = pair_refs[unit], got_refs[unit]
        unit_copy(unit, 0, pair, pair, partner).wait_send()
        near_copy(unit).wait_send()
        for count in (got.shape[0] - 1, clips - 1):
            most = got.at[pl.ds(0, count)]
            unit_copy(unit, 2, most, most, partner).wait_send()

    big = rows // 2

    def conv_one(i, carry):
        at = pl.ds(pl.multiple_of(i * big, big), big)
        v = dot(xm[at, :], wr[...])
        pre1[at, :] = v
        return carry[0] + part_sum(v), carry[1] + part_sum(v * v)

    sums = lax.fori_loop(0, 2, conv_one, (zero_n, zero_n))
    send_sums(st1, 1, *sums)
    along_z(2)
    along_x(2, 0)
    y_to_core()
    most = par.at[pl.ds(0, frames - 1)]
    pltpu.make_async_copy(most, most, st_recv.at[0]).wait()
    part_n = g1_ref.shape[0]
    part_w = g3_ref.shape[0]
    acc_n = [jnp.zeros((8, LANES), F32) for _ in range(nar_tiles)]
    acc_w = [jnp.zeros((8, LANES), F32) for _ in range(wide_tiles)]
    for f in range(frames):
        tile = par[f]
        spot = f * part_n
        shift = spot % LANES
        acc_n[spot // LANES] += pltpu.roll(tile, shift, 1) if shift else tile
        spot = f * part_w
        shift = spot % LANES
        acc_w[spot // LANES] += pltpu.roll(tile, shift, 1) if shift else tile
    gain1, bias1, gain2, bias2 = [jnp.concatenate([a[i : i + 1] for a in acc_n], axis=1) for i in range(4)]
    gain3, bias3 = [jnp.concatenate([a[i : i + 1] for a in acc_w], axis=1) for i in (4, 5)]
    inv_count = 1.0 / arrived(counts, 7)
    inv_n = jnp.concatenate([inv_count] * nar_tiles, axis=1)
    inv_w = jnp.concatenate([inv_count] * wide_tiles, axis=1)

    mean1, inv1 = moments(st1, 1, inv_n)
    scale1 = inv1 * gain1
    offset1 = bias1 - mean1 * scale1

    def both(v):
        return jnp.concatenate([v] * nar_tiles, axis=1)

    def act_one(i, carry):
        at = block_at(i)
        z = pre1[at, :] * scale1 + offset1
        s = sigmoid(z)
        m = both(mask[at, :])
        ms = m * s
        spad[pl.ds(pl.multiple_of(i * BLOCK + pad, 16), BLOCK), :] = ms * z
        slope1[at, :] = ms * (1.0 + z * (1.0 - s))
        return carry

    lax.fori_loop(0, blocks, act_one, 0)

    def spread():
        def shifted(i, carry):
            at = block_at(i)
            v = spad[pl.ds(pl.multiple_of(i * BLOCK + pad - 8, 8), BLOCK + 24), :]
            span = pl.ds(pl.multiple_of(i * BLOCK + 8, 8), BLOCK + 8)
            three = (
                pltpu.roll(v, 2, 0)[8 : 16 + BLOCK] * both(left_ok[span, :]),
                v[8 : 16 + BLOCK],
                pltpu.roll(v, BLOCK + 22, 0)[8 : 16 + BLOCK] * both(right_ok[span, :]),
            )
            there = pl.ds(pl.multiple_of(i * BLOCK + pad, 16), BLOCK)
            for j in range(3):
                still[j, at, :] = three[j][0:BLOCK].astype(BF16)
                moved[j, there, :] = three[j][8 : 8 + BLOCK].astype(BF16)
            return carry

        lax.fori_loop(0, blocks, shifted, 0)
        for j in range(3):
            head = jnp.concatenate([jnp.zeros((8, narrow), F32), still[j, 0:16, :].astype(F32)[0:8]], axis=0)
            moved[j, pad - 16 : pad, :] = head.astype(BF16)

    def taps(start, count, chosen, flip):
        parts = []
        for tap in chosen:
            row_off, col_off = (tap // 3, tap % 3) if not flip else (2 - tap // 3, 2 - tap % 3)
            ref = still if row_off == 1 else moved
            first = start if row_off < 2 else start + 2 * step_rows
            parts.append(ref[col_off, pl.ds(pl.multiple_of(first, 16), count), :])
        return jnp.concatenate(parts, axis=1)

    spread()
    weight_ready(1)
    for d in range(1, depth):
        along_x(2, d)
        to_core(2, d)

    def conv_two(i, carry):
        at = pl.ds(pl.multiple_of(i * big, big), big)
        v = dot(taps(i * big, big, range(9), False), ws[...].reshape(9 * narrow, narrow))
        pre2[at, :] = v
        mv = both(mask[at, :]) * v
        return carry[0] + part_sum(mv), carry[1] + part_sum(mv * v)

    sums = lax.fori_loop(0, 2, conv_two, (zero_n, zero_n))
    send_sums(st2, 2, *sums)
    wrt[...] = wr[...].T
    a1t[...] = still[1].T
    for d in range(depth):
        to_core_late(2, d)

    mean2, inv2 = moments(st2, 2, inv_n)
    scale2 = inv2 * gain2
    offset2 = bias2 - mean2 * scale2

    def act_two(i, carry):
        at = block_at(i)
        z = pre2[at, :] * scale2 + offset2
        s = sigmoid(z)
        ms = both(mask[at, :]) * s
        a = (ms * z).astype(BF16)
        act2[at, :] = a
        slope2[at, :] = ms * (1.0 + z * (1.0 - s))
        return carry + part_sum(a.astype(F32))

    act_sum = lax.fori_loop(0, blocks, act_two, zero_n)

    weight_ready(2)
    zero_w = jnp.zeros((8, channels), F32)

    wide = big

    def conv_three(i, carry):
        at = pl.ds(pl.multiple_of(i * wide, wide), wide)
        v = dot(act2[at, :], we[...])
        pre3[at, :] = v
        return carry + part_sum(v * v)

    squares = lax.fori_loop(0, rows // wide, conv_three, zero_w)
    st3[me, :, 0:narrow] = jnp.sum(act_sum, axis=0, keepdims=True)
    st3[me, :, narrow : narrow + channels] = jnp.sum(squares, axis=0, keepdims=True)
    gather_to_all(st3, 3)
    for tap in range(9):
        wst[narrow * tap : narrow * (tap + 1), :] = ws[tap].T
    wet[...] = we[...].T
    a2t[...] = act2[...].T
    copies_in(cs, 1).wait()
    to_rows(cs, ct_rows, 1).start()
    to_rows(cs, ct_rows, 1).wait()
    both_sums = arrived(st3, 3)
    left = both_sums[:, 0:narrow]
    parts = []
    for _ in range(3):
        parts.append(left.astype(BF16).astype(F32))
        left = left - parts[-1]
    exact = jnp.concatenate(parts + [jnp.zeros((5, narrow), F32)], axis=0).astype(BF16)
    mean3 = jnp.sum(dot(exact, we[...]), axis=0, keepdims=True) * inv_w
    inv3 = lax.rsqrt(both_sums[:, narrow:] * inv_w - mean3 * mean3 + EPS)
    scale3 = inv3 * gain3
    offset3 = bias3 - mean3 * scale3

    def from_rows(ref, index):
        return pltpu.make_async_copy(out_rows, ref.reshape(wide_tiles, rows, LANES), out_sem.at[index])

    def finish(i, carry):
        at = block_at(i)
        m = mask[at, :]
        first, second = [], []
        for j in range(wide_tiles):
            lanes = slice(LANES * j, LANES * (j + 1))
            p = pre3[at, lanes]
            t = p * scale3[:, lanes] + offset3[:, lanes] + xm[at, lanes].astype(F32)
            s = sigmoid(t)
            ms = m * s
            o = ms * t
            out_rows[j, at, :] = o.astype(BF16)
            g = ct_rows[j, at, :].astype(F32) * (ms + o * (1.0 - s))
            gt[at, lanes] = g
            first.append(part_sum(g))
            second.append(part_sum(g * p))
        return carry[0] + jnp.concatenate(first, axis=1), carry[1] + jnp.concatenate(second, axis=1)

    shift_own, slope_own = lax.fori_loop(0, blocks, finish, (zero_w, zero_w))
    shift_own = jnp.sum(shift_own, axis=0, keepdims=True)
    slope_own = (jnp.sum(slope_own, axis=0, keepdims=True) - mean3 * shift_own) * inv3
    pieces = [v[:, LANES * j : LANES * (j + 1)] for v in (shift_own, slope_own) for j in range(wide_tiles)]
    st4[me] = jnp.concatenate(pieces, axis=0).astype(BF16)
    gather_to_all(st4, 4)
    from_rows(out_ref, 0).start()
    shift3, slope_gain3 = get_sums(st4, 4)

    def back_terms(scale, inv, mean, shift_sum, gain_sum, inv_cnt):
        along = scale * inv * gain_sum * inv_cnt
        return along, scale * shift_sum * inv_cnt - mean * along

    along3, flat3 = back_terms(scale3, inv3, mean3, shift3, slope_gain3, inv_w)

    def back_three(i, carry):
        at = pl.ds(pl.multiple_of(i * big, big), big)
        m = mask[at, :]
        tiles = []
        for j in range(wide_tiles):
            lanes = slice(LANES * j, LANES * (j + 1))
            g = gt[at, lanes] * scale3[:, lanes] - pre3[at, lanes] * along3[:, lanes] - m * flat3[:, lanes]
            tiles.append(g.astype(BF16))
            gp3[at, lanes] = tiles[-1]
        d = dot(jnp.concatenate(tiles, axis=1), wet[...]) * slope2[at, :]
        dz[at, :] = d
        return carry[0] + part_sum(d), carry[1] + part_sum(d * ((pre2[at, :] - mean2) * inv2))

    sums = lax.fori_loop(0, 2, back_three, (zero_n, zero_n))
    send_sums(st5, 5, *sums)

    def grad_expand(i, carry):
        lanes = pl.ds(pl.multiple_of(i * 256, 256), 256)
        ge_ref[:, lanes] = dot(a2t[...], gp3[:, lanes]).astype(BF16)
        return carry

    lax.fori_loop(0, channels // 256, grad_expand, 0)
    if own_gather:
        cores(5).start()
        near(5)

    shift2, slope_gain2 = get_sums(st5, 5)
    along2, flat2 = back_terms(scale2, inv2, mean2, shift2, slope_gain2, inv_n)

    def back_two(i, carry):
        at = block_at(i)
        here = pl.ds(pl.multiple_of(i * BLOCK + pad, 16), BLOCK)
        m = both(mask[at, :])
        spad[here, :] = dz[at, :] * scale2 - m * (pre2[at, :] * along2 + flat2)
        return carry

    lax.fori_loop(0, blocks, back_two, 0)
    spread()

    def grad_spatial(row):
        gs_refs[row][...] = dot(a1t[...], taps(0, rows, range(3 * row, 3 * row + 3), True)).astype(BF16)
        if own_gather:
            cores(2 + row).start()

    grad_spatial(0)

    def back_spatial(i, carry):
        at = pl.ds(pl.multiple_of(i * big, big), big)
        d = dot(taps(i * big, big, range(9), True), wst[...]) * slope1[at, :]
        dz[at, :] = d
        return carry[0] + part_sum(d), carry[1] + part_sum(d * ((pre1[at, :] - mean1) * inv1))

    sums = lax.fori_loop(0, 2, back_spatial, (zero_n, zero_n))
    send_sums(st6, 6, *sums)
    if own_gather:
        near(2)
    grad_spatial(1)
    grad_spatial(2)
    if own_gather:
        near(3)
        near(4)
        far(5)

    shift1, slope_gain1 = get_sums(st6, 6)
    along1, flat1 = back_terms(scale1, inv1, mean1, shift1, slope_gain1, inv_n)

    def back_one(i, carry):
        at = block_at(i)
        g = dz[at, :] * scale1 - both(mask[at, :]) * (pre1[at, :] * along1 + flat1)
        gp1[at, :] = g.astype(BF16)
        return carry

    lax.fori_loop(0, blocks, back_one, 0)

    for i in range(2):
        height = channels // 2
        gr_refs[i][...] = dot(xt[height * i : height * (i + 1), :], gp1[...]).astype(BF16)
        if own_gather:
            cores(i).start()
    if own_gather:
        far(2)
        near(0)
        near(1)
    from_rows(out_ref, 0).wait()

    def grad_in(i, carry):
        at = pl.ds(pl.multiple_of(i * wide, wide), wide)
        m = mask[at, :]
        back = dot(gp1[at, :], wrt[...])
        for j in range(wide_tiles):
            lanes = slice(LANES * j, LANES * (j + 1))
            out_rows[j, at, :] = (m * back[:, lanes] + gt[at, lanes]).astype(BF16)
        return carry

    lax.fori_loop(0, rows // wide, grad_in, 0)
    if own_gather:
        far(3)
        far(4)
    from_rows(gin_ref, 1).start()

    def own_part(ref, v):
        width = ref.shape[0]
        spot = frame * width
        tile = jnp.zeros((1, LANES), F32)
        for t in range(v.shape[1] // LANES):
            tile = jnp.where(lax.div(spot, LANES) == t, v[:, LANES * t : LANES * (t + 1)], tile)
        tile = pltpu.roll(jnp.concatenate([tile] * 8, axis=0), lax.rem(LANES - lax.rem(spot, LANES), LANES), 1)
        ref[...] = tile[0, 0:width]

    own_part(vec1_gain, slope_gain1)
    own_part(vec1_shift, shift1)
    own_part(vec2_gain, slope_gain2)
    own_part(vec2_shift, shift2)
    own_part(vec3_gain, slope_gain3)
    own_part(vec3_shift, shift3)

    if own_gather:
        owners(5)
        far(0)
        far(1)
        for unit in (2, 3, 4, 0, 1):
            owners(unit)
        ge_out[...] = finished(5)[...].astype(F32)
        for row in range(3):
            fin = finished(2 + row)
            for c in range(3):
                gs_out[3 * row + c] = fin[:, narrow * c : narrow * (c + 1)].astype(F32)
        for i in range(2):
            gr_out[piece * i : piece * (i + 1), :] = finished(i)[...].astype(F32)
    else:
        for i in range(2):
            gr_out[channels // 2 * i : channels // 2 * (i + 1), :] = gr_refs[i][...]
        for row in range(3):
            gs_out[:, 3 * narrow * row : 3 * narrow * (row + 1)] = gs_refs[row][...]
        ge_out[...] = ge_ref[...]
    for index in range(3):
        weight_sent(index)
    if own_gather:
        for unit in range(units):
            sent(unit)
    for buf in (counts, st1, st2, st3, st4, st5, st6):
        most = buf.at[pl.ds(0, devices - 1)]
        pltpu.make_async_copy(most, most, st_send.at[0]).wait()
    most = par.at[pl.ds(0, frames - 1)]
    pltpu.make_async_copy(most, most, st_send.at[1]).wait()
    from_rows(gin_ref, 1).wait()


def deliver_kernel(count, *refs):
    sources, targets, sems = refs[:count], refs[count : 2 * count], refs[2 * count]
    for i in range(2):
        for j in range(sources[i].shape[0]):
            part = targets[i].at[:, :, LANES * j : LANES * (j + 1)]
            pltpu.make_async_copy(sources[i].at[j], part, sems.at[i]).start()
    for i in range(2, count):
        pltpu.make_async_copy(sources[i], targets[i], sems.at[i]).start()
    for i in range(count):
        pltpu.make_async_copy(sources[i], sources[i], sems.at[i]).wait()


def deliver(arrays, big):
    count = len(arrays)
    shapes = [big, big] + [jax.ShapeDtypeStruct(a.shape, a.dtype) for a in arrays[2:]]
    return pl.pallas_call(
        functools.partial(deliver_kernel, count),
        out_shape=tuple(shapes),
        in_specs=[pl.BlockSpec(memory_space=pltpu.VMEM)] * count,
        out_specs=(pl.BlockSpec(memory_space=pl.ANY),) * count,
        scratch_shapes=[pltpu.SemaphoreType.DMA((count,))],
        compiler_params=pltpu.CompilerParams(vmem_limit_bytes=1024 * 1024),
    )(*arrays)


def on_device(
    dims,
    x_in,
    cotangent,
    w_reduce,
    w_spatial,
    w_expand,
    gain_one,
    shift_one,
    gain_two,
    shift_two,
    gain_three,
    shift_three,
    bucket,
    frame_count,
):
    clips, frames = dims
    slots, side, _, channels = x_in.shape
    narrow = w_reduce.shape[1]
    pixels = side * side
    rows = pixels * slots
    tiles = channels // LANES
    devices = clips * frames
    own_gather = clips == 4 and all(n % 32 == 0 for n in (w_reduce.shape[0], w_spatial.shape[2], w_expand.shape[0]))
    w_spatial = w_spatial.reshape(9, -1, narrow)
    if not own_gather:
        w_reduce = lax.all_gather(w_reduce, "frame", axis=0, tiled=True)
        w_spatial = lax.all_gather(w_spatial, "frame", axis=1, tiled=True)
        w_expand = lax.all_gather(w_expand, "frame", axis=0, tiled=True)

    def by_pixel(v):
        return jnp.transpose(v, (1, 2, 0, 3)).reshape(pixels, slots, channels)

    any_spec = pl.BlockSpec(memory_space=pl.ANY)
    vmem = pl.BlockSpec(memory_space=pltpu.VMEM)
    smem = pl.BlockSpec(memory_space=pltpu.SMEM)
    big = jax.ShapeDtypeStruct((pixels, slots, channels), BF16)
    staged = pltpu.VMEM((tiles, pixels, slots, LANES), BF16)
    native = pltpu.VMEM((tiles, rows, LANES), BF16)
    narrow_f32 = pltpu.VMEM((rows, narrow), F32)
    wide_f32 = pltpu.VMEM((rows, channels), F32)
    lanes_f32 = pltpu.VMEM((rows, LANES), F32)
    edges_f32 = pltpu.VMEM((rows + 16, LANES), F32)

    def stats(count):
        return pltpu.VMEM((devices, count, LANES), F32)

    if own_gather:
        grad_shapes = (
            pltpu.VMEM((channels // frames, narrow), F32),
            pltpu.VMEM((9, narrow // frames, narrow), F32),
            pltpu.VMEM((narrow // frames, channels), F32),
        )
    else:
        grad_shapes = (
            jax.ShapeDtypeStruct((channels, narrow), BF16),
            jax.ShapeDtypeStruct((narrow, 9 * narrow), BF16),
            jax.ShapeDtypeStruct((narrow, channels), BF16),
        )
    wholes = (*(((channels // 2, narrow),) * 2), *(((narrow, 3 * narrow),) * 3), (narrow, channels))
    lines = clips // 2
    unit_scratch = [pltpu.VMEM(shape, BF16) for shape in wholes]
    if own_gather:
        cuts = [(height // frames // 2, width) for height, width in wholes]
        unit_scratch += [pltpu.VMEM((frames, half, width), BF16) for half, width in cuts]
        unit_scratch += [
            pltpu.VMEM((frames // 2, half, width) if hop == "x" else (frames, half, width // lines), BF16)
            for (half, width), hop in zip(cuts, NEAR)
        ]
        unit_scratch += [
            pltpu.VMEM((frames if hop else frames * lines, half, width // lines), BF16)
            for (half, width), hop in zip(cuts, NEAR)
        ]
        unit_scratch += [pltpu.VMEM((2 * half, width), BF16) for half, width in cuts]

    results = pl.pallas_call(
        functools.partial(block_kernel, (clips, frames, side, own_gather)),
        out_shape=(
            staged,
            staged,
            *grad_shapes,
            *(pltpu.VMEM((narrow // frames,), F32),) * 4,
            *(pltpu.VMEM((channels // frames,), F32),) * 2,
        ),
        in_specs=[any_spec] * 5 + [vmem] * 6 + [smem] * 2,
        out_specs=(vmem,) * 11,
        scratch_shapes=[
            staged,
            staged,
            native,
            native,
            native,
            pltpu.VMEM((rows, channels), BF16),
            pltpu.VMEM((channels, rows), BF16),
            pltpu.VMEM((narrow, rows), BF16),
            pltpu.VMEM((narrow, rows), BF16),
            lanes_f32,
            edges_f32,
            edges_f32,
            pltpu.VMEM((channels, narrow), BF16),
            pltpu.VMEM((9, narrow, narrow), BF16),
            pltpu.VMEM((narrow, channels), BF16),
            pltpu.VMEM((9 * narrow, narrow), BF16),
            pltpu.VMEM((channels, narrow), BF16),
            pltpu.VMEM((narrow, channels), BF16),
            narrow_f32,
            narrow_f32,
            narrow_f32,
            narrow_f32,
            narrow_f32,
            pltpu.VMEM((rows + 4 * side + 16, narrow), F32),
            pltpu.VMEM((rows, narrow), BF16),
            pltpu.VMEM((3, rows, narrow), BF16),
            pltpu.VMEM((3, rows + 4 * side, narrow), BF16),
            wide_f32,
            wide_f32,
            pltpu.VMEM((rows, channels), BF16),
            pltpu.VMEM((rows, narrow), BF16),
            pltpu.VMEM((frames, 8, LANES), F32),
            stats(1),
            stats(2 * narrow // LANES),
            stats(2 * narrow // LANES),
            pltpu.VMEM((devices, 1, narrow + channels), F32),
            pltpu.VMEM((devices, 2 * tiles, LANES), BF16),
            stats(2 * narrow // LANES),
            stats(2 * narrow // LANES),
            pltpu.SemaphoreType.DMA((5,)),
            pltpu.SemaphoreType.DMA((3,)),
            pltpu.SemaphoreType.DMA((3, frames + 3)),
            pltpu.SemaphoreType.DMA((2,)),
            pltpu.SemaphoreType.DMA((8,)),
            pltpu.SemaphoreType.DMA((2,)),
            pltpu.SemaphoreType.DMA((len(NEAR),)),
            pltpu.SemaphoreType.DMA((len(NEAR), 4)),
            *unit_scratch,
        ],
        compiler_params=pltpu.CompilerParams(
            collective_id=0, has_side_effects=True, vmem_limit_bytes=VMEM_BYTES
        ),
    )(
        by_pixel(x_in),
        by_pixel(cotangent),
        w_reduce,
        w_spatial,
        w_expand,
        gain_one,
        shift_one,
        gain_two,
        shift_two,
        gain_three,
        shift_three,
        bucket,
        frame_count,
    )

    def by_frame(v):
        return jnp.transpose(v.reshape(side, side, slots, channels), (2, 0, 1, 3))

    def owned(v):
        part = lax.psum_scatter(v, "frame", scatter_dimension=0, tiled=True)
        return lax.psum(part, "clip").astype(F32)

    if own_gather:
        out, gin, gr, gs, ge, *vectors = deliver(results, big)
    else:
        gr, gs, ge = [owned(v) for v in results[2:5]]
        gs = gs.reshape(-1, 9, narrow).transpose(1, 0, 2)
        out, gin, gr, gs, ge, *vectors = deliver((*results[:2], gr, gs, ge, *results[5:]), big)
    return (by_frame(out), by_frame(gin), gr, gs.reshape(3, 3, -1, narrow), ge, *vectors)


def solution(mesh):
    by_device = P(("clip", "frame"))
    shard = P("frame")
    spatial = P(None, None, "frame", None)
    return jax.shard_map(
        functools.partial(on_device, (mesh.shape["clip"], mesh.shape["frame"])),
        mesh=mesh,
        in_specs=(by_device, by_device, shard, spatial) + (shard,) * 7 + (by_device, by_device),
        out_specs=(by_device, by_device, shard, spatial) + (shard,) * 7,
        check_vma=False,
    )
```

```python
import functools

import jax
import jax.numpy as jnp
from jax import lax
from jax.experimental import pallas as pl
from jax.experimental.pallas import tpu as pltpu
from jax.sharding import PartitionSpec as P

SMALL_SIDE = 14
EPS = 1e-05
LANES = 128
BLOCK = 80
VMEM_BYTES = 52 * 1024 * 1024
MESH = pl.DeviceIdType.MESH
NEAR = ("x", "y", "y", "x", "y", "x")
F32 = jnp.float32
BF16 = jnp.bfloat16


def sigmoid(v):
    return 0.5 * jnp.tanh(0.5 * v) + 0.5


def part_sum(v):
    rows, width = v.shape
    return jnp.sum(v.reshape(rows // 8, 8, width), axis=0)


def dot(a, b):
    return jnp.dot(a, b, preferred_element_type=F32)


def rows_to_vec(tile, first, count):
    return jnp.concatenate([tile[first + i : first + i + 1] for i in range(count)], axis=1)


def block_kernel(
    dims,
    x_hbm,
    ct_hbm,
    wr_hbm,
    ws_hbm,
    we_hbm,
    g1_ref,
    b1_ref,
    g2_ref,
    b2_ref,
    g3_ref,
    b3_ref,
    bucket_ref,
    count_ref,
    out_ref,
    gin_ref,
    gr_out,
    gs_out,
    ge_out,
    vec1_gain,
    vec1_shift,
    vec2_gain,
    vec2_shift,
    vec3_gain,
    vec3_shift,
    xs,
    cs,
    x_rows,
    ct_rows,
    out_rows,
    xm,
    xt,
    a1t,
    a2t,
    mask,
    left_ok,
    right_ok,
    wr,
    ws,
    we,
    wst,
    wet,
    wrt,
    pre1,
    slope1,
    pre2,
    slope2,
    dz,
    spad,
    act2,
    still,
    moved,
    pre3,
    gt,
    gp3,
    gp1,
    par,
    counts,
    st1,
    st2,
    st3,
    st4,
    st5,
    st6,
    local_sem,
    wsend,
    wrecv,
    st_send,
    st_recv,
    out_sem,
    rs_send,
    rs_recv,
    *unit_refs,
):
    clips, frames, side, own_gather = dims
    units = len(NEAR)
    full_refs, pair_refs, mid_refs, got_refs, fin_refs = [unit_refs[units * i : units * (i + 1)] for i in range(5)]
    gr_refs, gs_refs, ge_ref = full_refs[0:2], full_refs[2:5], full_refs[5]
    devices = clips * frames
    clip = lax.axis_index("clip")
    frame = lax.axis_index("frame")
    me = clip * frames + frame
    core = lax.rem(clip, 2)
    partner = (clip + 1 - 2 * core, frame)
    rows = xm.shape[0]
    channels = xm.shape[1]
    narrow = wr.shape[1]
    wide_tiles = channels // LANES
    nar_tiles = narrow // LANES
    blocks = rows // BLOCK
    step_rows = 2 * side
    pad = step_rows + 8
    lines = clips // 2
    line_me = lax.div(clip, 2)
    y_peer = (lax.rem(clip + 2, clips), frame)

    small = devices <= 32 and clips & (clips - 1) == 0 and frames & (frames - 1) == 0

    def flips(v, size):
        return [(1 - 2 * lax.rem(lax.div(v, 1 << i), 2)) * (1 << i) for i in range(size.bit_length() - 1)]

    clip_flips, frame_flips = flips(clip, clips), flips(frame, frames)

    def to_others(action):
        if small:
            for b in reversed(range(frames)):
                to_frame = sum((d for i, d in enumerate(frame_flips) if b >> i & 1), frame)
                for a in reversed(range(clips)):
                    if a or b:
                        action((sum((d for i, d in enumerate(clip_flips) if a >> i & 1), clip), to_frame))
            return
        for a in range(clips):
            to_clip = lax.rem(clip + a, clips)

            def step(b, carry):
                action((to_clip, lax.rem(frame + b, frames)))
                return carry

            lax.fori_loop(0 if a else 1, frames, step, 0)

    for j in range(wide_tiles):
        lanes = pl.ds(LANES * j, LANES)
        pltpu.make_async_copy(x_hbm.at[:, :, lanes], xs.at[j], local_sem.at[0]).start()
    if own_gather:
        part_r = wr_hbm.shape[0]
        part_s = ws_hbm.shape[1]
        part_e = we_hbm.shape[0]
        own_r = wr.at[pl.ds(pl.multiple_of(frame * part_r, part_r), part_r)]
        own_s = ws.at[:, pl.ds(pl.multiple_of(frame * part_s, part_s), part_s)]
        own_e = we.at[pl.ds(pl.multiple_of(frame * part_e, part_e), part_e)]
    else:
        own_r, own_s, own_e = wr, ws, we
    own_copies = [
        pltpu.make_async_copy(wr_hbm, own_r, local_sem.at[2]),
        pltpu.make_async_copy(ws_hbm, own_s, local_sem.at[3]),
        pltpu.make_async_copy(we_hbm, own_e, local_sem.at[4]),
    ]
    for copy in own_copies:
        copy.start()
    for j in range(wide_tiles):
        lanes = pl.ds(LANES * j, LANES)
        pltpu.make_async_copy(ct_hbm.at[:, :, lanes], cs.at[j], local_sem.at[1]).start()

    def copies_in(staged, index):
        return pltpu.make_async_copy(staged, staged, local_sem.at[index])

    def to_rows(staged, native, index):
        return pltpu.make_async_copy(staged.reshape(wide_tiles, rows, LANES), native, local_sem.at[index])

    barrier = pltpu.get_barrier_semaphore()

    to_others(lambda target: pl.semaphore_signal(barrier, inc=1, device_id=target, device_id_type=MESH))

    row_id = lax.broadcasted_iota(jnp.int32, (rows, LANES), 0)
    pixel = row_id >> 1
    slot = row_id & 1
    line = (pixel * 3277) >> 16
    col = pixel - line * side
    extent = [jnp.where(bucket_ref[f] == 0, SMALL_SIDE, side) for f in range(2)]
    limit = [jnp.where(count_ref[0] > f, extent[f], 0) for f in range(2)]
    bound = jnp.where(slot == 0, limit[0], limit[1])
    live = ((line < bound) & (col < bound)).astype(F32)
    mask[...] = live
    for ref, ok in ((left_ok, col >= 1), (right_ok, col <= side - 2)):
        ref[0:8, :] = jnp.zeros((8, LANES), F32)
        ref[8 : 8 + rows, :] = ok.astype(F32)
        ref[8 + rows : 16 + rows, :] = jnp.zeros((8, LANES), F32)

    par[frame] = jnp.zeros((8, LANES), F32)
    for i, ref in enumerate((g1_ref, b1_ref, g2_ref, b2_ref, g3_ref, b3_ref)):
        width = ref.shape[0]
        par[frame, i : i + 1, 0:width] = ref[...].astype(F32).reshape(1, width)
    counts[me] = jnp.sum(live, axis=0, keepdims=True)

    copies_in(xs, 0).wait()
    to_rows(xs, x_rows, 0).start()
    to_rows(xs, x_rows, 0).wait()

    def block_at(i):
        return pl.ds(pl.multiple_of(i * BLOCK, BLOCK), BLOCK)

    def mask_in(i, carry):
        at = block_at(i)
        m = mask[at, :].astype(BF16)
        for j in range(wide_tiles):
            xm[at, LANES * j : LANES * (j + 1)] = x_rows[j, at, :] * m
        return carry

    lax.fori_loop(0, blocks, mask_in, 0)
    edge = jnp.zeros((pad, narrow), F32)
    spad[0:pad, :] = edge
    spad[pad + rows : 2 * pad + rows, :] = edge
    edge = jnp.zeros((3, step_rows - 8, narrow), BF16)
    moved[:, 0 : step_rows - 8, :] = edge
    moved[:, step_rows + 8 + rows : 2 * step_rows + rows, :] = edge
    turned = xm[...].T
    if own_gather:
        piece = part_r // 2
        for f in range(2 * frames):
            spot = (f % 2) * frames + f // 2
            xt[piece * spot : piece * (spot + 1), :] = turned[piece * f : piece * (f + 1)]
    else:
        xt[...] = turned
    for copy in own_copies:
        copy.wait()

    pl.semaphore_wait(barrier, devices - 1)

    def gather_to_all(buf, index):
        def send(target):
            pltpu.make_async_remote_copy(
                src_ref=buf.at[me],
                dst_ref=buf.at[me],
                send_sem=st_send.at[0],
                recv_sem=st_recv.at[index],
                device_id=target,
                device_id_type=MESH,
            ).start()

        to_others(send)

    def arrived(buf, index):
        most = buf.at[pl.ds(0, devices - 1)]
        pltpu.make_async_copy(most, most, st_recv.at[index]).wait()
        return jnp.sum(buf[...].astype(F32), axis=0)

    across = lax.rem(frame, 2)
    along = lax.div(frame, 2)
    depth = frames // 2
    x_peer = (clip, along * 2 + 1 - across)
    xy_peer = (lax.rem(clip + 2, clips), along * 2 + 1 - across)

    def owner_at(d, side_x):
        return lax.rem(along - d + depth, depth) * 2 + side_x

    if own_gather:

        kinds = ((wr, 0, part_r), (ws, 1, part_s), (we, 0, part_e))

        def piece_of(index, owner, columns=None):
            ref, axis, part = kinds[index]
            at = pl.ds(pl.multiple_of(owner * part + core * (part // 2), part // 2), part // 2)
            if axis == 0:
                return ref.at[at]
            return ref.at[:, at] if columns is None else ref.at[:, at, columns]

        def own_columns(index):
            if index != 1:
                return None
            cut = narrow // lines
            return pl.ds(pl.multiple_of(line_me * cut, LANES), cut)

        def weight_copy(index, sem, owner, target, columns=None):
            part = piece_of(index, owner, columns)
            return pltpu.make_async_remote_copy(
                src_ref=part,
                dst_ref=part,
                send_sem=wsend.at[index],
                recv_sem=wrecv.at[weight_sems[index][sem]],
                device_id=target,
                device_id_type=MESH,
            )

        def blocks_of(index, count, wide=True):
            ref, axis, part = kinds[index]
            size = pl.ds(0, count * (part // 2))
            if axis == 0:
                return ref.at[size]
            return ref.at[:, size] if wide else ref.at[:, size, pl.ds(0, narrow // lines)]

        def blocks_wait(sem, view):
            pltpu.make_async_copy(view, view, sem).wait()

        numbers = iter(range(wrecv.shape[0]))
        weight_sems = []
        for index in range(3):
            own = {d: next(numbers) for d in range(1, depth)}
            together = next(numbers) if index == 1 else None
            own |= {depth + d: next(numbers) if together is None else together for d in range(depth)}
            own |= {2 * depth + k: next(numbers) for k in range(3 if index == 1 else 1)}
            weight_sems.append(own)

        def along_z(index):
            for d in range(1, depth):
                target = (clip, lax.rem(along + d, depth) * 2 + across)
                weight_copy(index, d, frame, target, own_columns(index)).start()

        def along_x(index, d):
            columns = own_columns(index)
            if d:
                weight_copy(index, d, owner_at(d, across), x_peer, columns).wait_recv()
            weight_copy(index, depth + d, owner_at(d, across), x_peer, columns).start()

        def along_y(d):
            weight_copy(1, 2 * depth + 1, owner_at(d, across), y_peer, own_columns(1)).start()

        def along_xy(d):
            weight_copy(1, 2 * depth + 2, owner_at(d, across), xy_peer, own_columns(1)).start()

        def y_to_core():
            blocks_wait(wrecv.at[weight_sems[1][2 * depth + 1]], blocks_of(1, depth - 1, False))
            for d in range(1, depth):
                to_core(1, d)
            blocks_wait(wrecv.at[weight_sems[1][depth]], blocks_of(1, depth, False))
            blocks_wait(wrecv.at[weight_sems[1][2 * depth + 2]], blocks_of(1, depth, False))
            for d in range(depth):
                weight_copy(1, 2 * depth, owner_at(d, 1 - across), partner).start()

        def to_core(index, d):
            weight_copy(index, 2 * depth, owner_at(d, across), partner).start()

        def to_core_late(index, d):
            owner = owner_at(d, 1 - across)
            weight_copy(index, depth + d, owner, partner).wait_recv()
            weight_copy(index, 2 * depth, owner, partner).start()

        def weight_ready(index):
            blocks_wait(wrecv.at[weight_sems[index][2 * depth]], blocks_of(index, 2 * depth - 1))

        def weight_sent(index):
            blocks_wait(wsend.at[index], blocks_of(index, 4 * depth - 2))

    else:

        def nothing(*args):
            pass

        along_z = along_x = along_y = along_xy = y_to_core = nothing
        to_core = to_core_late = weight_ready = weight_sent = nothing

    def send_params():
        def send(b, carry):
            pltpu.make_async_remote_copy(
                src_ref=par.at[frame],
                dst_ref=par.at[frame],
                send_sem=st_send.at[1],
                recv_sem=st_recv.at[0],
                device_id=(clip, lax.rem(frame + b, frames)),
                device_id_type=MESH,
            ).start()
            return carry

        lax.fori_loop(1, frames, send, 0)

    along_z(0)
    along_x(0, 0)
    along_z(1)
    along_x(1, 0)
    along_xy(0)
    gather_to_all(counts, 7)
    send_params()
    for d in range(1, depth):
        along_x(0, d)
        to_core(0, d)
    along_x(1, 1)
    along_xy(1)
    for d in range(depth):
        to_core_late(0, d)

    for d in range(2, depth):
        along_x(1, d)
        along_xy(d)
    for d in range(1, depth):
        along_y(d)

    weight_ready(0)

    def send_sums(buf, index, first, second):
        tiles = first.shape[1] // LANES
        first = jnp.sum(first, axis=0, keepdims=True)
        second = jnp.sum(second, axis=0, keepdims=True)
        for i in range(tiles):
            buf[me, i : i + 1, :] = first[:, LANES * i : LANES * (i + 1)]
            buf[me, tiles + i : tiles + i + 1, :] = second[:, LANES * i : LANES * (i + 1)]
        gather_to_all(buf, index)

    def get_sums(buf, index):
        total = arrived(buf, index)
        tiles = total.shape[0] // 2
        return rows_to_vec(total, 0, tiles), rows_to_vec(total, tiles, tiles)

    def moments(buf, index, inv):
        total, squares = get_sums(buf, index)
        mean = total * inv
        var = squares * inv - mean * mean
        return mean, lax.rsqrt(var + EPS)

    zero_n = jnp.zeros((8, narrow), F32)


    def unit_copy(unit, stage, src, dst, target):
        return pltpu.make_async_remote_copy(
            src_ref=src,
            dst_ref=dst,
            send_sem=rs_send.at[unit],
            recv_sem=rs_recv.at[unit, stage],
            device_id=target,
            device_id_type=MESH,
        )

    def columns(line, cut):
        return pl.ds(pl.multiple_of(line * cut, LANES), cut)

    def cores(unit):
        full, pair = full_refs[unit], pair_refs[unit]
        half = pair.shape[1]
        view = full.reshape(frames, 2 * half, full.shape[1])
        theirs = pl.ds(pl.multiple_of((1 - core) * half, half), half)
        return unit_copy(unit, 0, view.at[:, theirs], pair, partner)

    def near_copy(unit):
        pair, mid = pair_refs[unit], mid_refs[unit]
        half, width = pair.shape[1], pair.shape[2]
        if NEAR[unit] == "x":
            return unit_copy(unit, 1, pair.reshape(depth, 2, half, width).at[:, 1 - across], mid, x_peer)
        return unit_copy(unit, 1, pair.at[:, :, columns(1 - line_me, width // lines)], mid, y_peer)

    def near(unit):
        full, pair = full_refs[unit], pair_refs[unit]
        cores(unit).wait_recv()
        half = pair.shape[1]
        mine = pl.ds(pl.multiple_of(core * half, half), half)
        view = full.reshape(frames, 2 * half, full.shape[1])

        def add(f, carry):
            pair[f] = (pair[f].astype(F32) + view[f, mine, :].astype(F32)).astype(BF16)
            return carry

        lax.fori_loop(0, frames, add, 0)
        near_copy(unit).start()

    def far(unit):
        pair, mid, got = pair_refs[unit], mid_refs[unit], got_refs[unit]
        cut = pair.shape[2] // lines
        near_copy(unit).wait_recv()

        def add(k, carry):
            own = pair[2 * k + across] if NEAR[unit] == "x" else pair[k, :, columns(line_me, cut)]
            mid[k] = (mid[k].astype(F32) + own.astype(F32)).astype(BF16)
            return carry

        lax.fori_loop(0, mid.shape[0], add, 0)
        if NEAR[unit] == "x":
            slot_me = line_me * depth + along
            got[slot_me] = mid[along, :, columns(line_me, cut)]

            def send(k, carry):
                deep, line = lax.div(k, lines), lax.rem(k, lines)

                @pl.when(jnp.logical_or(deep != along, line != line_me))
                def _():
                    src = mid.at[deep, :, columns(line, cut)]
                    unit_copy(unit, 2, src, got.at[slot_me], (line * 2 + core, deep * 2 + across)).start()

                return carry

        else:
            got[frame] = mid[frame]

            def send(owner, carry):
                @pl.when(owner != frame)
                def _():
                    unit_copy(unit, 2, mid.at[owner], got.at[frame], (clip, owner)).start()

                return carry

        lax.fori_loop(0, got.shape[0], send, 0)

    def owners(unit):
        got, fin = got_refs[unit], fin_refs[unit]
        half, cut = got.shape[1], got.shape[2]
        most = got.at[pl.ds(0, got.shape[0] - 1)]
        unit_copy(unit, 2, most, most, partner).wait_recv()
        spot = fin.at[pl.ds(pl.multiple_of(core * half, half), half), columns(line_me, cut)]
        spot[...] = jnp.sum(got[...].astype(F32), axis=0).astype(BF16)

        def send(k, carry):
            unit_copy(unit, 3, spot, spot, (lax.rem(clip + k, clips), frame)).start()
            return carry

        lax.fori_loop(1, clips, send, 0)

    def finished(unit):
        most = got_refs[unit].at[pl.ds(0, clips - 1)]
        unit_copy(unit, 3, most, most, partner).wait_recv()
        return fin_refs[unit]

    def sent(unit):
        pair, got = pair_refs[unit], got_refs[unit]
        unit_copy(unit, 0, pair, pair, partner).wait_send()
        near_copy(unit).wait_send()
        for count in (got.shape[0] - 1, clips - 1):
            most = got.at[pl.ds(0, count)]
            unit_copy(unit, 2, most, most, partner).wait_send()

    big = rows // 2

    def conv_one(i, carry):
        at = pl.ds(pl.multiple_of(i * big, big), big)
        v = dot(xm[at, :], wr[...])
        pre1[at, :] = v
        return carry[0] + part_sum(v), carry[1] + part_sum(v * v)

    sums = lax.fori_loop(0, 2, conv_one, (zero_n, zero_n))
    send_sums(st1, 1, *sums)
    along_z(2)
    along_x(2, 0)
    y_to_core()
    most = par.at[pl.ds(0, frames - 1)]
    pltpu.make_async_copy(most, most, st_recv.at[0]).wait()
    part_n = g1_ref.shape[0]
    part_w = g3_ref.shape[0]
    acc_n = [jnp.zeros((8, LANES), F32) for _ in range(nar_tiles)]
    acc_w = [jnp.zeros((8, LANES), F32) for _ in range(wide_tiles)]
    for f in range(frames):
        tile = par[f]
        spot = f * part_n
        shift = spot % LANES
        acc_n[spot // LANES] += pltpu.roll(tile, shift, 1) if shift else tile
        spot = f * part_w
        shift = spot % LANES
        acc_w[spot // LANES] += pltpu.roll(tile, shift, 1) if shift else tile
    gain1, bias1, gain2, bias2 = [jnp.concatenate([a[i : i + 1] for a in acc_n], axis=1) for i in range(4)]
    gain3, bias3 = [jnp.concatenate([a[i : i + 1] for a in acc_w], axis=1) for i in (4, 5)]
    inv_count = 1.0 / arrived(counts, 7)
    inv_n = jnp.concatenate([inv_count] * nar_tiles, axis=1)
    inv_w = jnp.concatenate([inv_count] * wide_tiles, axis=1)

    mean1, inv1 = moments(st1, 1, inv_n)
    scale1 = inv1 * gain1
    offset1 = bias1 - mean1 * scale1

    def both(v):
        return jnp.concatenate([v] * nar_tiles, axis=1)

    def act_one(i, carry):
        at = block_at(i)
        z = pre1[at, :] * scale1 + offset1
        s = sigmoid(z)
        m = both(mask[at, :])
        ms = m * s
        spad[pl.ds(pl.multiple_of(i * BLOCK + pad, 16), BLOCK), :] = ms * z
        slope1[at, :] = ms * (1.0 + z * (1.0 - s))
        return carry

    lax.fori_loop(0, blocks, act_one, 0)

    def spread():
        def shifted(i, carry):
            at = block_at(i)
            v = spad[pl.ds(pl.multiple_of(i * BLOCK + pad - 8, 8), BLOCK + 24), :]
            span = pl.ds(pl.multiple_of(i * BLOCK + 8, 8), BLOCK + 8)
            three = (
                pltpu.roll(v, 2, 0)[8 : 16 + BLOCK] * both(left_ok[span, :]),
                v[8 : 16 + BLOCK],
                pltpu.roll(v, BLOCK + 22, 0)[8 : 16 + BLOCK] * both(right_ok[span, :]),
            )
            there = pl.ds(pl.multiple_of(i * BLOCK + pad, 16), BLOCK)
            for j in range(3):
                still[j, at, :] = three[j][0:BLOCK].astype(BF16)
                moved[j, there, :] = three[j][8 : 8 + BLOCK].astype(BF16)
            return carry

        lax.fori_loop(0, blocks, shifted, 0)
        for j in range(3):
            head = jnp.concatenate([jnp.zeros((8, narrow), F32), still[j, 0:16, :].astype(F32)[0:8]], axis=0)
            moved[j, pad - 16 : pad, :] = head.astype(BF16)

    def taps(start, count, chosen, flip):
        parts = []
        for tap in chosen:
            row_off, col_off = (tap // 3, tap % 3) if not flip else (2 - tap // 3, 2 - tap % 3)
            ref = still if row_off == 1 else moved
            first = start if row_off < 2 else start + 2 * step_rows
            parts.append(ref[col_off, pl.ds(pl.multiple_of(first, 16), count), :])
        return jnp.concatenate(parts, axis=1)

    spread()
    weight_ready(1)
    for d in range(1, depth):
        along_x(2, d)
        to_core(2, d)

    def conv_two(i, carry):
        at = pl.ds(pl.multiple_of(i * big, big), big)
        v = dot(taps(i * big, big, range(9), False), ws[...].reshape(9 * narrow, narrow))
        pre2[at, :] = v
        mv = both(mask[at, :]) * v
        return carry[0] + part_sum(mv), carry[1] + part_sum(mv * v)

    sums = lax.fori_loop(0, 2, conv_two, (zero_n, zero_n))
    send_sums(st2, 2, *sums)
    wrt[...] = wr[...].T
    a1t[...] = still[1].T
    for d in range(depth):
        to_core_late(2, d)

    mean2, inv2 = moments(st2, 2, inv_n)
    scale2 = inv2 * gain2
    offset2 = bias2 - mean2 * scale2

    def act_two(i, carry):
        at = block_at(i)
        z = pre2[at, :] * scale2 + offset2
        s = sigmoid(z)
        ms = both(mask[at, :]) * s
        a = (ms * z).astype(BF16)
        act2[at, :] = a
        slope2[at, :] = ms * (1.0 + z * (1.0 - s))
        return carry + part_sum(a.astype(F32))

    act_sum = lax.fori_loop(0, blocks, act_two, zero_n)

    weight_ready(2)
    zero_w = jnp.zeros((8, channels), F32)

    wide = big

    def conv_three(i, carry):
        at = pl.ds(pl.multiple_of(i * wide, wide), wide)
        v = dot(act2[at, :], we[...])
        pre3[at, :] = v
        return carry + part_sum(v * v)

    squares = lax.fori_loop(0, rows // wide, conv_three, zero_w)
    st3[me, :, 0:narrow] = jnp.sum(act_sum, axis=0, keepdims=True)
    st3[me, :, narrow : narrow + channels] = jnp.sum(squares, axis=0, keepdims=True)
    gather_to_all(st3, 3)
    for tap in range(9):
        wst[narrow * tap : narrow * (tap + 1), :] = ws[tap].T
    wet[...] = we[...].T
    a2t[...] = act2[...].T
    copies_in(cs, 1).wait()
    to_rows(cs, ct_rows, 1).start()
    to_rows(cs, ct_rows, 1).wait()
    both_sums = arrived(st3, 3)
    left = both_sums[:, 0:narrow]
    parts = []
    for _ in range(3):
        parts.append(left.astype(BF16).astype(F32))
        left = left - parts[-1]
    exact = jnp.concatenate(parts + [jnp.zeros((5, narrow), F32)], axis=0).astype(BF16)
    mean3 = jnp.sum(dot(exact, we[...]), axis=0, keepdims=True) * inv_w
    inv3 = lax.rsqrt(both_sums[:, narrow:] * inv_w - mean3 * mean3 + EPS)
    scale3 = inv3 * gain3
    offset3 = bias3 - mean3 * scale3

    def from_rows(ref, index):
        return pltpu.make_async_copy(out_rows, ref.reshape(wide_tiles, rows, LANES), out_sem.at[index])

    def finish(i, carry):
        at = block_at(i)
        m = mask[at, :]
        first, second = [], []
        for j in range(wide_tiles):
            lanes = slice(LANES * j, LANES * (j + 1))
            p = pre3[at, lanes]
            t = p * scale3[:, lanes] + offset3[:, lanes] + xm[at, lanes].astype(F32)
            s = sigmoid(t)
            ms = m * s
            o = ms * t
            out_rows[j, at, :] = o.astype(BF16)
            g = ct_rows[j, at, :].astype(F32) * (ms + o * (1.0 - s))
            gt[at, lanes] = g
            first.append(part_sum(g))
            second.append(part_sum(g * p))
        return carry[0] + jnp.concatenate(first, axis=1), carry[1] + jnp.concatenate(second, axis=1)

    shift_own, slope_own = lax.fori_loop(0, blocks, finish, (zero_w, zero_w))
    shift_own = jnp.sum(shift_own, axis=0, keepdims=True)
    slope_own = (jnp.sum(slope_own, axis=0, keepdims=True) - mean3 * shift_own) * inv3
    pieces = [v[:, LANES * j : LANES * (j + 1)] for v in (shift_own, slope_own) for j in range(wide_tiles)]
    st4[me] = jnp.concatenate(pieces, axis=0).astype(BF16)
    gather_to_all(st4, 4)
    from_rows(out_ref, 0).start()
    shift3, slope_gain3 = get_sums(st4, 4)

    def back_terms(scale, inv, mean, shift_sum, gain_sum, inv_cnt):
        along = scale * inv * gain_sum * inv_cnt
        return along, scale * shift_sum * inv_cnt - mean * along

    along3, flat3 = back_terms(scale3, inv3, mean3, shift3, slope_gain3, inv_w)

    def back_three(i, carry):
        at = pl.ds(pl.multiple_of(i * big, big), big)
        m = mask[at, :]
        tiles = []
        for j in range(wide_tiles):
            lanes = slice(LANES * j, LANES * (j + 1))
            g = gt[at, lanes] * scale3[:, lanes] - pre3[at, lanes] * along3[:, lanes] - m * flat3[:, lanes]
            tiles.append(g.astype(BF16))
            gp3[at, lanes] = tiles[-1]
        d = dot(jnp.concatenate(tiles, axis=1), wet[...]) * slope2[at, :]
        dz[at, :] = d
        return carry[0] + part_sum(d), carry[1] + part_sum(d * ((pre2[at, :] - mean2) * inv2))

    sums = lax.fori_loop(0, 2, back_three, (zero_n, zero_n))
    send_sums(st5, 5, *sums)

    def grad_expand(i, carry):
        lanes = pl.ds(pl.multiple_of(i * 256, 256), 256)
        ge_ref[:, lanes] = dot(a2t[...], gp3[:, lanes]).astype(BF16)
        return carry

    lax.fori_loop(0, channels // 256, grad_expand, 0)
    if own_gather:
        cores(5).start()
        near(5)

    shift2, slope_gain2 = get_sums(st5, 5)
    along2, flat2 = back_terms(scale2, inv2, mean2, shift2, slope_gain2, inv_n)

    def back_two(i, carry):
        at = block_at(i)
        here = pl.ds(pl.multiple_of(i * BLOCK + pad, 16), BLOCK)
        m = both(mask[at, :])
        spad[here, :] = dz[at, :] * scale2 - m * (pre2[at, :] * along2 + flat2)
        return carry

    lax.fori_loop(0, blocks, back_two, 0)
    spread()

    def grad_spatial(row):
        gs_refs[row][...] = dot(a1t[...], taps(0, rows, range(3 * row, 3 * row + 3), True)).astype(BF16)
        if own_gather:
            cores(2 + row).start()

    grad_spatial(0)

    def back_spatial(i, carry):
        at = pl.ds(pl.multiple_of(i * big, big), big)
        d = dot(taps(i * big, big, range(9), True), wst[...]) * slope1[at, :]
        dz[at, :] = d
        return carry[0] + part_sum(d), carry[1] + part_sum(d * ((pre1[at, :] - mean1) * inv1))

    sums = lax.fori_loop(0, 2, back_spatial, (zero_n, zero_n))
    send_sums(st6, 6, *sums)
    if own_gather:
        near(2)
    grad_spatial(1)
    grad_spatial(2)
    if own_gather:
        near(3)
        near(4)
        far(5)

    shift1, slope_gain1 = get_sums(st6, 6)
    along1, flat1 = back_terms(scale1, inv1, mean1, shift1, slope_gain1, inv_n)

    def back_one(i, carry):
        at = block_at(i)
        g = dz[at, :] * scale1 - both(mask[at, :]) * (pre1[at, :] * along1 + flat1)
        gp1[at, :] = g.astype(BF16)
        return carry

    lax.fori_loop(0, blocks, back_one, 0)

    for i in range(2):
        height = channels // 2
        gr_refs[i][...] = dot(xt[height * i : height * (i + 1), :], gp1[...]).astype(BF16)
        if own_gather:
            cores(i).start()
    if own_gather:
        far(2)
        near(0)
        near(1)
    from_rows(out_ref, 0).wait()

    def grad_in(i, carry):
        at = pl.ds(pl.multiple_of(i * wide, wide), wide)
        m = mask[at, :]
        back = dot(gp1[at, :], wrt[...])
        for j in range(wide_tiles):
            lanes = slice(LANES * j, LANES * (j + 1))
            out_rows[j, at, :] = (m * back[:, lanes] + gt[at, lanes]).astype(BF16)
        return carry

    lax.fori_loop(0, rows // wide, grad_in, 0)
    if own_gather:
        far(3)
        far(4)
    from_rows(gin_ref, 1).start()

    def own_part(ref, v):
        width = ref.shape[0]
        spot = frame * width
        tile = jnp.zeros((1, LANES), F32)
        for t in range(v.shape[1] // LANES):
            tile = jnp.where(lax.div(spot, LANES) == t, v[:, LANES * t : LANES * (t + 1)], tile)
        tile = pltpu.roll(jnp.concatenate([tile] * 8, axis=0), lax.rem(LANES - lax.rem(spot, LANES), LANES), 1)
        ref[...] = tile[0, 0:width]

    own_part(vec1_gain, slope_gain1)
    own_part(vec1_shift, shift1)
    own_part(vec2_gain, slope_gain2)
    own_part(vec2_shift, shift2)
    own_part(vec3_gain, slope_gain3)
    own_part(vec3_shift, shift3)

    if own_gather:
        owners(5)
        far(0)
        far(1)
        for unit in (2, 3, 4, 0, 1):
            owners(unit)
        ge_out[...] = finished(5)[...].astype(F32)
        for row in range(3):
            fin = finished(2 + row)
            for c in range(3):
                gs_out[3 * row + c] = fin[:, narrow * c : narrow * (c + 1)].astype(F32)
        for i in range(2):
            gr_out[piece * i : piece * (i + 1), :] = finished(i)[...].astype(F32)
    else:
        for i in range(2):
            gr_out[channels // 2 * i : channels // 2 * (i + 1), :] = gr_refs[i][...]
        for row in range(3):
            gs_out[:, 3 * narrow * row : 3 * narrow * (row + 1)] = gs_refs[row][...]
        ge_out[...] = ge_ref[...]
    for index in range(3):
        weight_sent(index)
    if own_gather:
        for unit in range(units):
            sent(unit)
    for buf in (counts, st1, st2, st3, st4, st5, st6):
        most = buf.at[pl.ds(0, devices - 1)]
        pltpu.make_async_copy(most, most, st_send.at[0]).wait()
    most = par.at[pl.ds(0, frames - 1)]
    pltpu.make_async_copy(most, most, st_send.at[1]).wait()
    from_rows(gin_ref, 1).wait()


def deliver_kernel(count, *refs):
    sources, targets, sems = refs[:count], refs[count : 2 * count], refs[2 * count]
    for i in range(2):
        for j in range(sources[i].shape[0]):
            part = targets[i].at[:, :, LANES * j : LANES * (j + 1)]
            pltpu.make_async_copy(sources[i].at[j], part, sems.at[i]).start()
    for i in range(2, count):
        pltpu.make_async_copy(sources[i], targets[i], sems.at[i]).start()
    for i in range(count):
        pltpu.make_async_copy(sources[i], sources[i], sems.at[i]).wait()


def deliver(arrays, big):
    count = len(arrays)
    shapes = [big, big] + [jax.ShapeDtypeStruct(a.shape, a.dtype) for a in arrays[2:]]
    return pl.pallas_call(
        functools.partial(deliver_kernel, count),
        out_shape=tuple(shapes),
        in_specs=[pl.BlockSpec(memory_space=pltpu.VMEM)] * count,
        out_specs=(pl.BlockSpec(memory_space=pl.ANY),) * count,
        scratch_shapes=[pltpu.SemaphoreType.DMA((count,))],
        compiler_params=pltpu.CompilerParams(vmem_limit_bytes=1024 * 1024),
    )(*arrays)


def on_device(
    dims,
    x_in,
    cotangent,
    w_reduce,
    w_spatial,
    w_expand,
    gain_one,
    shift_one,
    gain_two,
    shift_two,
    gain_three,
    shift_three,
    bucket,
    frame_count,
):
    clips, frames = dims
    slots, side, _, channels = x_in.shape
    narrow = w_reduce.shape[1]
    pixels = side * side
    rows = pixels * slots
    tiles = channels // LANES
    devices = clips * frames
    own_gather = clips == 4 and all(n % 32 == 0 for n in (w_reduce.shape[0], w_spatial.shape[2], w_expand.shape[0]))
    w_spatial = w_spatial.reshape(9, -1, narrow)
    if not own_gather:
        w_reduce = lax.all_gather(w_reduce, "frame", axis=0, tiled=True)
        w_spatial = lax.all_gather(w_spatial, "frame", axis=1, tiled=True)
        w_expand = lax.all_gather(w_expand, "frame", axis=0, tiled=True)

    def by_pixel(v):
        return jnp.transpose(v, (1, 2, 0, 3)).reshape(pixels, slots, channels)

    any_spec = pl.BlockSpec(memory_space=pl.ANY)
    vmem = pl.BlockSpec(memory_space=pltpu.VMEM)
    smem = pl.BlockSpec(memory_space=pltpu.SMEM)
    big = jax.ShapeDtypeStruct((pixels, slots, channels), BF16)
    staged = pltpu.VMEM((tiles, pixels, slots, LANES), BF16)
    native = pltpu.VMEM((tiles, rows, LANES), BF16)
    narrow_f32 = pltpu.VMEM((rows, narrow), F32)
    wide_f32 = pltpu.VMEM((rows, channels), F32)
    lanes_f32 = pltpu.VMEM((rows, LANES), F32)
    edges_f32 = pltpu.VMEM((rows + 16, LANES), F32)

    def stats(count):
        return pltpu.VMEM((devices, count, LANES), F32)

    if own_gather:
        grad_shapes = (
            pltpu.VMEM((channels // frames, narrow), F32),
            pltpu.VMEM((9, narrow // frames, narrow), F32),
            pltpu.VMEM((narrow // frames, channels), F32),
        )
    else:
        grad_shapes = (
            jax.ShapeDtypeStruct((channels, narrow), BF16),
            jax.ShapeDtypeStruct((narrow, 9 * narrow), BF16),
            jax.ShapeDtypeStruct((narrow, channels), BF16),
        )
    wholes = (*(((channels // 2, narrow),) * 2), *(((narrow, 3 * narrow),) * 3), (narrow, channels))
    lines = clips // 2
    unit_scratch = [pltpu.VMEM(shape, BF16) for shape in wholes]
    if own_gather:
        cuts = [(height // frames // 2, width) for height, width in wholes]
        unit_scratch += [pltpu.VMEM((frames, half, width), BF16) for half, width in cuts]
        unit_scratch += [
            pltpu.VMEM((frames // 2, half, width) if hop == "x" else (frames, half, width // lines), BF16)
            for (half, width), hop in zip(cuts, NEAR)
        ]
        unit_scratch += [
            pltpu.VMEM((frames if hop else frames * lines, half, width // lines), BF16)
            for (half, width), hop in zip(cuts, NEAR)
        ]
        unit_scratch += [pltpu.VMEM((2 * half, width), BF16) for half, width in cuts]

    results = pl.pallas_call(
        functools.partial(block_kernel, (clips, frames, side, own_gather)),
        out_shape=(
            staged,
            staged,
            *grad_shapes,
            *(pltpu.VMEM((narrow // frames,), F32),) * 4,
            *(pltpu.VMEM((channels // frames,), F32),) * 2,
        ),
        in_specs=[any_spec] * 5 + [vmem] * 6 + [smem] * 2,
        out_specs=(vmem,) * 11,
        scratch_shapes=[
            staged,
            staged,
            native,
            native,
            native,
            pltpu.VMEM((rows, channels), BF16),
            pltpu.VMEM((channels, rows), BF16),
            pltpu.VMEM((narrow, rows), BF16),
            pltpu.VMEM((narrow, rows), BF16),
            lanes_f32,
            edges_f32,
            edges_f32,
            pltpu.VMEM((channels, narrow), BF16),
            pltpu.VMEM((9, narrow, narrow), BF16),
            pltpu.VMEM((narrow, channels), BF16),
            pltpu.VMEM((9 * narrow, narrow), BF16),
            pltpu.VMEM((channels, narrow), BF16),
            pltpu.VMEM((narrow, channels), BF16),
            narrow_f32,
            narrow_f32,
            narrow_f32,
            narrow_f32,
            narrow_f32,
            pltpu.VMEM((rows + 4 * side + 16, narrow), F32),
            pltpu.VMEM((rows, narrow), BF16),
            pltpu.VMEM((3, rows, narrow), BF16),
            pltpu.VMEM((3, rows + 4 * side, narrow), BF16),
            wide_f32,
            wide_f32,
            pltpu.VMEM((rows, channels), BF16),
            pltpu.VMEM((rows, narrow), BF16),
            pltpu.VMEM((frames, 8, LANES), F32),
            stats(1),
            stats(2 * narrow // LANES),
            stats(2 * narrow // LANES),
            pltpu.VMEM((devices, 1, narrow + channels), F32),
            pltpu.VMEM((devices, 2 * tiles, LANES), BF16),
            stats(2 * narrow // LANES),
            stats(2 * narrow // LANES),
            pltpu.SemaphoreType.DMA((5,)),
            pltpu.SemaphoreType.DMA((3,)),
            pltpu.SemaphoreType.DMA((3 * frames,)),
            pltpu.SemaphoreType.DMA((2,)),
            pltpu.SemaphoreType.DMA((8,)),
            pltpu.SemaphoreType.DMA((2,)),
            pltpu.SemaphoreType.DMA((len(NEAR),)),
            pltpu.SemaphoreType.DMA((len(NEAR), 4)),
            *unit_scratch,
        ],
        compiler_params=pltpu.CompilerParams(
            collective_id=0, has_side_effects=True, vmem_limit_bytes=VMEM_BYTES
        ),
    )(
        by_pixel(x_in),
        by_pixel(cotangent),
        w_reduce,
        w_spatial,
        w_expand,
        gain_one,
        shift_one,
        gain_two,
        shift_two,
        gain_three,
        shift_three,
        bucket,
        frame_count,
    )

    def by_frame(v):
        return jnp.transpose(v.reshape(side, side, slots, channels), (2, 0, 1, 3))

    def owned(v):
        part = lax.psum_scatter(v, "frame", scatter_dimension=0, tiled=True)
        return lax.psum(part, "clip").astype(F32)

    if own_gather:
        out, gin, gr, gs, ge, *vectors = deliver(results, big)
    else:
        gr, gs, ge = [owned(v) for v in results[2:5]]
        gs = gs.reshape(-1, 9, narrow).transpose(1, 0, 2)
        out, gin, gr, gs, ge, *vectors = deliver((*results[:2], gr, gs, ge, *results[5:]), big)
    return (by_frame(out), by_frame(gin), gr, gs.reshape(3, 3, -1, narrow), ge, *vectors)


def solution(mesh):
    by_device = P(("clip", "frame"))
    shard = P("frame")
    spatial = P(None, None, "frame", None)
    return jax.shard_map(
        functools.partial(on_device, (mesh.shape["clip"], mesh.shape["frame"])),
        mesh=mesh,
        in_specs=(by_device, by_device, shard, spatial) + (shard,) * 7 + (by_device, by_device),
        out_specs=(by_device, by_device, shard, spatial) + (shard,) * 7,
        check_vma=False,
    )
```

```python
import functools

import jax
import jax.numpy as jnp
from jax import lax
from jax.experimental import pallas as pl
from jax.experimental.pallas import tpu as pltpu
from jax.sharding import PartitionSpec as P

SMALL_SIDE = 14
EPS = 1e-05
LANES = 128
BLOCK = 80
VMEM_BYTES = 52 * 1024 * 1024
MESH = pl.DeviceIdType.MESH
NEAR = ("x", "y", "x", "y", "x", "y")
F32 = jnp.float32
BF16 = jnp.bfloat16


def sigmoid(v):
    return 0.5 * jnp.tanh(0.5 * v) + 0.5


def part_sum(v):
    rows, width = v.shape
    return jnp.sum(v.reshape(rows // 8, 8, width), axis=0)


def dot(a, b):
    return jnp.dot(a, b, preferred_element_type=F32)


def rows_to_vec(tile, first, count):
    return jnp.concatenate([tile[first + i : first + i + 1] for i in range(count)], axis=1)


def block_kernel(
    dims,
    x_hbm,
    ct_hbm,
    wr_hbm,
    ws_hbm,
    we_hbm,
    g1_ref,
    b1_ref,
    g2_ref,
    b2_ref,
    g3_ref,
    b3_ref,
    bucket_ref,
    count_ref,
    out_ref,
    gin_ref,
    gr_out,
    gs_out,
    ge_out,
    vec1_gain,
    vec1_shift,
    vec2_gain,
    vec2_shift,
    vec3_gain,
    vec3_shift,
    xs,
    cs,
    x_rows,
    ct_rows,
    out_rows,
    xm,
    xt,
    a1t,
    a2t,
    mask,
    left_ok,
    right_ok,
    wr,
    ws,
    we,
    wst,
    wet,
    wrt,
    pre1,
    slope1,
    pre2,
    slope2,
    dz,
    spad,
    act2,
    still,
    moved,
    pre3,
    gt,
    gp3,
    gp1,
    par,
    counts,
    st1,
    st2,
    st3,
    st4,
    st5,
    st6,
    local_sem,
    wsend,
    wrecv,
    st_send,
    st_recv,
    out_sem,
    rs_send,
    rs_recv,
    *unit_refs,
):
    clips, frames, side, own_gather = dims
    units = len(NEAR)
    full_refs, pair_refs, mid_refs, got_refs, fin_refs = [unit_refs[units * i : units * (i + 1)] for i in range(5)]
    gr_refs, gs_refs, ge_ref = full_refs[0:2], full_refs[2:5], full_refs[5]
    devices = clips * frames
    clip = lax.axis_index("clip")
    frame = lax.axis_index("frame")
    me = clip * frames + frame
    core = lax.rem(clip, 2)
    partner = (clip + 1 - 2 * core, frame)
    rows = xm.shape[0]
    channels = xm.shape[1]
    narrow = wr.shape[1]
    wide_tiles = channels // LANES
    nar_tiles = narrow // LANES
    blocks = rows // BLOCK
    step_rows = 2 * side
    pad = step_rows + 8
    lines = clips // 2
    line_me = lax.div(clip, 2)
    y_peer = (lax.rem(clip + 2, clips), frame)

    small = devices <= 32 and clips & (clips - 1) == 0 and frames & (frames - 1) == 0

    def flips(v, size):
        return [(1 - 2 * lax.rem(lax.div(v, 1 << i), 2)) * (1 << i) for i in range(size.bit_length() - 1)]

    clip_flips, frame_flips = flips(clip, clips), flips(frame, frames)

    def to_others(action):
        if small:
            for b in reversed(range(frames)):
                to_frame = sum((d for i, d in enumerate(frame_flips) if b >> i & 1), frame)
                for a in reversed(range(clips)):
                    if a or b:
                        action((sum((d for i, d in enumerate(clip_flips) if a >> i & 1), clip), to_frame))
            return
        for a in range(clips):
            to_clip = lax.rem(clip + a, clips)

            def step(b, carry):
                action((to_clip, lax.rem(frame + b, frames)))
                return carry

            lax.fori_loop(0 if a else 1, frames, step, 0)

    for j in range(wide_tiles):
        lanes = pl.ds(LANES * j, LANES)
        pltpu.make_async_copy(x_hbm.at[:, :, lanes], xs.at[j], local_sem.at[0]).start()
    if own_gather:
        part_r = wr_hbm.shape[0]
        part_s = ws_hbm.shape[1]
        part_e = we_hbm.shape[0]
        own_r = wr.at[pl.ds(pl.multiple_of(frame * part_r, part_r), part_r)]
        own_s = ws.at[:, pl.ds(pl.multiple_of(frame * part_s, part_s), part_s)]
        own_e = we.at[pl.ds(pl.multiple_of(frame * part_e, part_e), part_e)]
    else:
        own_r, own_s, own_e = wr, ws, we
    own_copies = [
        pltpu.make_async_copy(wr_hbm, own_r, local_sem.at[2]),
        pltpu.make_async_copy(ws_hbm, own_s, local_sem.at[3]),
        pltpu.make_async_copy(we_hbm, own_e, local_sem.at[4]),
    ]
    for copy in own_copies:
        copy.start()
    for j in range(wide_tiles):
        lanes = pl.ds(LANES * j, LANES)
        pltpu.make_async_copy(ct_hbm.at[:, :, lanes], cs.at[j], local_sem.at[1]).start()

    def copies_in(staged, index):
        return pltpu.make_async_copy(staged, staged, local_sem.at[index])

    def to_rows(staged, native, index):
        return pltpu.make_async_copy(staged.reshape(wide_tiles, rows, LANES), native, local_sem.at[index])

    barrier = pltpu.get_barrier_semaphore()

    to_others(lambda target: pl.semaphore_signal(barrier, inc=1, device_id=target, device_id_type=MESH))

    row_id = lax.broadcasted_iota(jnp.int32, (rows, LANES), 0)
    pixel = row_id >> 1
    slot = row_id & 1
    line = (pixel * 3277) >> 16
    col = pixel - line * side
    extent = [jnp.where(bucket_ref[f] == 0, SMALL_SIDE, side) for f in range(2)]
    limit = [jnp.where(count_ref[0] > f, extent[f], 0) for f in range(2)]
    bound = jnp.where(slot == 0, limit[0], limit[1])
    live = ((line < bound) & (col < bound)).astype(F32)
    mask[...] = live
    for ref, ok in ((left_ok, col >= 1), (right_ok, col <= side - 2)):
        ref[0:8, :] = jnp.zeros((8, LANES), F32)
        ref[8 : 8 + rows, :] = ok.astype(F32)
        ref[8 + rows : 16 + rows, :] = jnp.zeros((8, LANES), F32)

    par[frame] = jnp.zeros((8, LANES), F32)
    for i, ref in enumerate((g1_ref, b1_ref, g2_ref, b2_ref, g3_ref, b3_ref)):
        width = ref.shape[0]
        par[frame, i : i + 1, 0:width] = ref[...].astype(F32).reshape(1, width)
    counts[me] = jnp.sum(live, axis=0, keepdims=True)

    copies_in(xs, 0).wait()
    to_rows(xs, x_rows, 0).start()
    to_rows(xs, x_rows, 0).wait()

    def block_at(i):
        return pl.ds(pl.multiple_of(i * BLOCK, BLOCK), BLOCK)

    def mask_in(i, carry):
        at = block_at(i)
        m = mask[at, :].astype(BF16)
        for j in range(wide_tiles):
            xm[at, LANES * j : LANES * (j + 1)] = x_rows[j, at, :] * m
        return carry

    lax.fori_loop(0, blocks, mask_in, 0)
    edge = jnp.zeros((pad, narrow), F32)
    spad[0:pad, :] = edge
    spad[pad + rows : 2 * pad + rows, :] = edge
    edge = jnp.zeros((3, step_rows - 8, narrow), BF16)
    moved[:, 0 : step_rows - 8, :] = edge
    moved[:, step_rows + 8 + rows : 2 * step_rows + rows, :] = edge
    turned = xm[...].T
    if own_gather:
        piece = part_r // 2
        for f in range(2 * frames):
            spot = (f % 2) * frames + f // 2
            xt[piece * spot : piece * (spot + 1), :] = turned[piece * f : piece * (f + 1)]
    else:
        xt[...] = turned
    for copy in own_copies:
        copy.wait()

    pl.semaphore_wait(barrier, devices - 1)

    def gather_to_all(buf, index):
        def send(target):
            pltpu.make_async_remote_copy(
                src_ref=buf.at[me],
                dst_ref=buf.at[me],
                send_sem=st_send.at[0],
                recv_sem=st_recv.at[index],
                device_id=target,
                device_id_type=MESH,
            ).start()

        to_others(send)

    def arrived(buf, index):
        most = buf.at[pl.ds(0, devices - 1)]
        pltpu.make_async_copy(most, most, st_recv.at[index]).wait()
        return jnp.sum(buf[...].astype(F32), axis=0)

    across = lax.rem(frame, 2)
    along = lax.div(frame, 2)
    depth = frames // 2
    x_peer = (clip, along * 2 + 1 - across)
    xy_peer = (lax.rem(clip + 2, clips), along * 2 + 1 - across)

    def owner_at(d, side_x):
        return lax.rem(along - d + depth, depth) * 2 + side_x

    if own_gather:

        kinds = ((wr, 0, part_r), (ws, 1, part_s), (we, 0, part_e))

        def piece_of(index, owner, columns=None):
            ref, axis, part = kinds[index]
            at = pl.ds(pl.multiple_of(owner * part + core * (part // 2), part // 2), part // 2)
            if axis == 0:
                return ref.at[at]
            return ref.at[:, at] if columns is None else ref.at[:, at, columns]

        def own_columns(index):
            if index != 1:
                return None
            cut = narrow // lines
            return pl.ds(pl.multiple_of(line_me * cut, LANES), cut)

        def weight_copy(index, sem, owner, target, columns=None):
            part = piece_of(index, owner, columns)
            return pltpu.make_async_remote_copy(
                src_ref=part,
                dst_ref=part,
                send_sem=wsend.at[index],
                recv_sem=wrecv.at[weight_sems[index][sem]],
                device_id=target,
                device_id_type=MESH,
            )

        def blocks_of(index, count, wide=True):
            ref, axis, part = kinds[index]
            size = pl.ds(0, count * (part // 2))
            if axis == 0:
                return ref.at[size]
            return ref.at[:, size] if wide else ref.at[:, size, pl.ds(0, narrow // lines)]

        def blocks_wait(sem, view):
            pltpu.make_async_copy(view, view, sem).wait()

        numbers = iter(range(wrecv.shape[0]))
        weight_sems = []
        for index in range(3):
            own = {d: next(numbers) for d in range(1, depth)}
            together = next(numbers) if index == 1 else None
            own |= {depth + d: next(numbers) if together is None else together for d in range(depth)}
            own |= {2 * depth + k: next(numbers) for k in range(3 if index == 1 else 1)}
            weight_sems.append(own)

        def along_z(index):
            for d in range(1, depth):
                target = (clip, lax.rem(along + d, depth) * 2 + across)
                weight_copy(index, d, frame, target, own_columns(index)).start()

        def along_x(index, d):
            columns = own_columns(index)
            if d:
                weight_copy(index, d, owner_at(d, across), x_peer, columns).wait_recv()
            weight_copy(index, depth + d, owner_at(d, across), x_peer, columns).start()

        def along_y(d):
            weight_copy(1, 2 * depth + 1, owner_at(d, across), y_peer, own_columns(1)).start()

        def along_xy(d):
            weight_copy(1, 2 * depth + 2, owner_at(d, across), xy_peer, own_columns(1)).start()

        def y_to_core():
            blocks_wait(wrecv.at[weight_sems[1][2 * depth + 1]], blocks_of(1, depth - 1, False))
            for d in range(1, depth):
                to_core(1, d)
            blocks_wait(wrecv.at[weight_sems[1][depth]], blocks_of(1, depth, False))
            blocks_wait(wrecv.at[weight_sems[1][2 * depth + 2]], blocks_of(1, depth, False))
            for d in range(depth):
                weight_copy(1, 2 * depth, owner_at(d, 1 - across), partner).start()

        def to_core(index, d):
            weight_copy(index, 2 * depth, owner_at(d, across), partner).start()

        def to_core_late(index, d):
            owner = owner_at(d, 1 - across)
            weight_copy(index, depth + d, owner, partner).wait_recv()
            weight_copy(index, 2 * depth, owner, partner).start()

        def weight_ready(index):
            blocks_wait(wrecv.at[weight_sems[index][2 * depth]], blocks_of(index, 2 * depth - 1))

        def weight_sent(index):
            blocks_wait(wsend.at[index], blocks_of(index, 4 * depth - 2))

    else:

        def nothing(*args):
            pass

        along_z = along_x = along_y = along_xy = y_to_core = nothing
        to_core = to_core_late = weight_ready = weight_sent = nothing

    def send_params():
        def send(b, carry):
            pltpu.make_async_remote_copy(
                src_ref=par.at[frame],
                dst_ref=par.at[frame],
                send_sem=st_send.at[1],
                recv_sem=st_recv.at[0],
                device_id=(clip, lax.rem(frame + b, frames)),
                device_id_type=MESH,
            ).start()
            return carry

        lax.fori_loop(1, frames, send, 0)

    along_z(0)
    along_x(0, 0)
    along_z(1)
    along_x(1, 0)
    along_xy(0)
    gather_to_all(counts, 7)
    send_params()
    for d in range(1, depth):
        along_x(0, d)
        to_core(0, d)
    along_x(1, 1)
    along_xy(1)
    for d in range(depth):
        to_core_late(0, d)

    for d in range(2, depth):
        along_x(1, d)
        along_xy(d)
    for d in range(1, depth):
        along_y(d)

    weight_ready(0)

    def send_sums(buf, index, first, second):
        tiles = first.shape[1] // LANES
        first = jnp.sum(first, axis=0, keepdims=True)
        second = jnp.sum(second, axis=0, keepdims=True)
        for i in range(tiles):
            buf[me, i : i + 1, :] = first[:, LANES * i : LANES * (i + 1)]
            buf[me, tiles + i : tiles + i + 1, :] = second[:, LANES * i : LANES * (i + 1)]
        gather_to_all(buf, index)

    def get_sums(buf, index):
        total = arrived(buf, index)
        tiles = total.shape[0] // 2
        return rows_to_vec(total, 0, tiles), rows_to_vec(total, tiles, tiles)

    def moments(buf, index, inv):
        total, squares = get_sums(buf, index)
        mean = total * inv
        var = squares * inv - mean * mean
        return mean, lax.rsqrt(var + EPS)

    zero_n = jnp.zeros((8, narrow), F32)


    def unit_copy(unit, stage, src, dst, target):
        return pltpu.make_async_remote_copy(
            src_ref=src,
            dst_ref=dst,
            send_sem=rs_send.at[unit],
            recv_sem=rs_recv.at[unit, stage],
            device_id=target,
            device_id_type=MESH,
        )

    def columns(line, cut):
        return pl.ds(pl.multiple_of(line * cut, LANES), cut)

    def cores(unit):
        full, pair = full_refs[unit], pair_refs[unit]
        half = pair.shape[1]
        view = full.reshape(frames, 2 * half, full.shape[1])
        theirs = pl.ds(pl.multiple_of((1 - core) * half, half), half)
        return unit_copy(unit, 0, view.at[:, theirs], pair, partner)

    def near_copy(unit):
        pair, mid = pair_refs[unit], mid_refs[unit]
        half, width = pair.shape[1], pair.shape[2]
        if NEAR[unit] == "x":
            return unit_copy(unit, 1, pair.reshape(depth, 2, half, width).at[:, 1 - across], mid, x_peer)
        return unit_copy(unit, 1, pair.at[:, :, columns(1 - line_me, width // lines)], mid, y_peer)

    def near(unit):
        full, pair = full_refs[unit], pair_refs[unit]
        cores(unit).wait_recv()
        half = pair.shape[1]
        mine = pl.ds(pl.multiple_of(core * half, half), half)
        view = full.reshape(frames, 2 * half, full.shape[1])

        def add(f, carry):
            pair[f] = (pair[f].astype(F32) + view[f, mine, :].astype(F32)).astype(BF16)
            return carry

        lax.fori_loop(0, frames, add, 0)
        near_copy(unit).start()

    def far(unit):
        pair, mid, got = pair_refs[unit], mid_refs[unit], got_refs[unit]
        cut = pair.shape[2] // lines
        near_copy(unit).wait_recv()

        def add(k, carry):
            own = pair[2 * k + across] if NEAR[unit] == "x" else pair[k, :, columns(line_me, cut)]
            mid[k] = (mid[k].astype(F32) + own.astype(F32)).astype(BF16)
            return carry

        lax.fori_loop(0, mid.shape[0], add, 0)
        if NEAR[unit] == "x":
            slot_me = line_me * depth + along
            got[slot_me] = mid[along, :, columns(line_me, cut)]

            def send(k, carry):
                deep, line = lax.div(k, lines), lax.rem(k, lines)

                @pl.when(jnp.logical_or(deep != along, line != line_me))
                def _():
                    src = mid.at[deep, :, columns(line, cut)]
                    unit_copy(unit, 2, src, got.at[slot_me], (line * 2 + core, deep * 2 + across)).start()

                return carry

        else:
            got[frame] = mid[frame]

            def send(owner, carry):
                @pl.when(owner != frame)
                def _():
                    unit_copy(unit, 2, mid.at[owner], got.at[frame], (clip, owner)).start()

                return carry

        lax.fori_loop(0, got.shape[0], send, 0)

    def owners(unit):
        got, fin = got_refs[unit], fin_refs[unit]
        half, cut = got.shape[1], got.shape[2]
        most = got.at[pl.ds(0, got.shape[0] - 1)]
        unit_copy(unit, 2, most, most, partner).wait_recv()
        spot = fin.at[pl.ds(pl.multiple_of(core * half, half), half), columns(line_me, cut)]
        spot[...] = jnp.sum(got[...].astype(F32), axis=0).astype(BF16)

        def send(k, carry):
            unit_copy(unit, 3, spot, spot, (lax.rem(clip + k, clips), frame)).start()
            return carry

        lax.fori_loop(1, clips, send, 0)

    def finished(unit):
        most = got_refs[unit].at[pl.ds(0, clips - 1)]
        unit_copy(unit, 3, most, most, partner).wait_recv()
        return fin_refs[unit]

    def sent(unit):
        pair, got = pair_refs[unit], got_refs[unit]
        unit_copy(unit, 0, pair, pair, partner).wait_send()
        near_copy(unit).wait_send()
        for count in (got.shape[0] - 1, clips - 1):
            most = got.at[pl.ds(0, count)]
            unit_copy(unit, 2, most, most, partner).wait_send()

    big = rows // 2

    def conv_one(i, carry):
        at = pl.ds(pl.multiple_of(i * big, big), big)
        v = dot(xm[at, :], wr[...])
        pre1[at, :] = v
        return carry[0] + part_sum(v), carry[1] + part_sum(v * v)

    sums = lax.fori_loop(0, 2, conv_one, (zero_n, zero_n))
    send_sums(st1, 1, *sums)
    along_z(2)
    along_x(2, 0)
    y_to_core()
    most = par.at[pl.ds(0, frames - 1)]
    pltpu.make_async_copy(most, most, st_recv.at[0]).wait()
    part_n = g1_ref.shape[0]
    part_w = g3_ref.shape[0]
    acc_n = [jnp.zeros((8, LANES), F32) for _ in range(nar_tiles)]
    acc_w = [jnp.zeros((8, LANES), F32) for _ in range(wide_tiles)]
    for f in range(frames):
        tile = par[f]
        spot = f * part_n
        shift = spot % LANES
        acc_n[spot // LANES] += pltpu.roll(tile, shift, 1) if shift else tile
        spot = f * part_w
        shift = spot % LANES
        acc_w[spot // LANES] += pltpu.roll(tile, shift, 1) if shift else tile
    gain1, bias1, gain2, bias2 = [jnp.concatenate([a[i : i + 1] for a in acc_n], axis=1) for i in range(4)]
    gain3, bias3 = [jnp.concatenate([a[i : i + 1] for a in acc_w], axis=1) for i in (4, 5)]
    inv_count = 1.0 / arrived(counts, 7)
    inv_n = jnp.concatenate([inv_count] * nar_tiles, axis=1)
    inv_w = jnp.concatenate([inv_count] * wide_tiles, axis=1)

    mean1, inv1 = moments(st1, 1, inv_n)
    scale1 = inv1 * gain1
    offset1 = bias1 - mean1 * scale1

    def both(v):
        return jnp.concatenate([v] * nar_tiles, axis=1)

    def act_one(i, carry):
        at = block_at(i)
        z = pre1[at, :] * scale1 + offset1
        s = sigmoid(z)
        m = both(mask[at, :])
        ms = m * s
        spad[pl.ds(pl.multiple_of(i * BLOCK + pad, 16), BLOCK), :] = ms * z
        slope1[at, :] = ms * (1.0 + z * (1.0 - s))
        return carry

    lax.fori_loop(0, blocks, act_one, 0)

    def spread():
        def shifted(i, carry):
            at = block_at(i)
            v = spad[pl.ds(pl.multiple_of(i * BLOCK + pad - 8, 8), BLOCK + 24), :]
            span = pl.ds(pl.multiple_of(i * BLOCK + 8, 8), BLOCK + 8)
            three = (
                pltpu.roll(v, 2, 0)[8 : 16 + BLOCK] * both(left_ok[span, :]),
                v[8 : 16 + BLOCK],
                pltpu.roll(v, BLOCK + 22, 0)[8 : 16 + BLOCK] * both(right_ok[span, :]),
            )
            there = pl.ds(pl.multiple_of(i * BLOCK + pad, 16), BLOCK)
            for j in range(3):
                still[j, at, :] = three[j][0:BLOCK].astype(BF16)
                moved[j, there, :] = three[j][8 : 8 + BLOCK].astype(BF16)
            return carry

        lax.fori_loop(0, blocks, shifted, 0)
        for j in range(3):
            head = jnp.concatenate([jnp.zeros((8, narrow), F32), still[j, 0:16, :].astype(F32)[0:8]], axis=0)
            moved[j, pad - 16 : pad, :] = head.astype(BF16)

    def taps(start, count, chosen, flip):
        parts = []
        for tap in chosen:
            row_off, col_off = (tap // 3, tap % 3) if not flip else (2 - tap // 3, 2 - tap % 3)
            ref = still if row_off == 1 else moved
            first = start if row_off < 2 else start + 2 * step_rows
            parts.append(ref[col_off, pl.ds(pl.multiple_of(first, 16), count), :])
        return jnp.concatenate(parts, axis=1)

    spread()
    weight_ready(1)
    for d in range(1, depth):
        along_x(2, d)
        to_core(2, d)

    def conv_two(i, carry):
        at = pl.ds(pl.multiple_of(i * big, big), big)
        v = dot(taps(i * big, big, range(9), False), ws[...].reshape(9 * narrow, narrow))
        pre2[at, :] = v
        mv = both(mask[at, :]) * v
        return carry[0] + part_sum(mv), carry[1] + part_sum(mv * v)

    sums = lax.fori_loop(0, 2, conv_two, (zero_n, zero_n))
    send_sums(st2, 2, *sums)
    wrt[...] = wr[...].T
    a1t[...] = still[1].T
    for d in range(depth):
        to_core_late(2, d)

    mean2, inv2 = moments(st2, 2, inv_n)
    scale2 = inv2 * gain2
    offset2 = bias2 - mean2 * scale2

    def act_two(i, carry):
        at = block_at(i)
        z = pre2[at, :] * scale2 + offset2
        s = sigmoid(z)
        ms = both(mask[at, :]) * s
        a = (ms * z).astype(BF16)
        act2[at, :] = a
        slope2[at, :] = ms * (1.0 + z * (1.0 - s))
        return carry + part_sum(a.astype(F32))

    act_sum = lax.fori_loop(0, blocks, act_two, zero_n)

    weight_ready(2)
    zero_w = jnp.zeros((8, channels), F32)

    wide = big

    def conv_three(i, carry):
        at = pl.ds(pl.multiple_of(i * wide, wide), wide)
        v = dot(act2[at, :], we[...])
        pre3[at, :] = v
        return carry + part_sum(v * v)

    squares = lax.fori_loop(0, rows // wide, conv_three, zero_w)
    st3[me, :, 0:narrow] = jnp.sum(act_sum, axis=0, keepdims=True)
    st3[me, :, narrow : narrow + channels] = jnp.sum(squares, axis=0, keepdims=True)
    gather_to_all(st3, 3)
    for tap in range(9):
        wst[narrow * tap : narrow * (tap + 1), :] = ws[tap].T
    wet[...] = we[...].T
    a2t[...] = act2[...].T
    copies_in(cs, 1).wait()
    to_rows(cs, ct_rows, 1).start()
    to_rows(cs, ct_rows, 1).wait()
    both_sums = arrived(st3, 3)
    left = both_sums[:, 0:narrow]
    parts = []
    for _ in range(3):
        parts.append(left.astype(BF16).astype(F32))
        left = left - parts[-1]
    exact = jnp.concatenate(parts + [jnp.zeros((5, narrow), F32)], axis=0).astype(BF16)
    mean3 = jnp.sum(dot(exact, we[...]), axis=0, keepdims=True) * inv_w
    inv3 = lax.rsqrt(both_sums[:, narrow:] * inv_w - mean3 * mean3 + EPS)
    scale3 = inv3 * gain3
    offset3 = bias3 - mean3 * scale3

    def from_rows(ref, index):
        return pltpu.make_async_copy(out_rows, ref.reshape(wide_tiles, rows, LANES), out_sem.at[index])

    def finish(i, carry):
        at = block_at(i)
        m = mask[at, :]
        first, second = [], []
        for j in range(wide_tiles):
            lanes = slice(LANES * j, LANES * (j + 1))
            p = pre3[at, lanes]
            t = p * scale3[:, lanes] + offset3[:, lanes] + xm[at, lanes].astype(F32)
            s = sigmoid(t)
            ms = m * s
            o = ms * t
            out_rows[j, at, :] = o.astype(BF16)
            g = ct_rows[j, at, :].astype(F32) * (ms + o * (1.0 - s))
            gt[at, lanes] = g
            first.append(part_sum(g))
            second.append(part_sum(g * p))
        return carry[0] + jnp.concatenate(first, axis=1), carry[1] + jnp.concatenate(second, axis=1)

    shift_own, slope_own = lax.fori_loop(0, blocks, finish, (zero_w, zero_w))
    shift_own = jnp.sum(shift_own, axis=0, keepdims=True)
    slope_own = (jnp.sum(slope_own, axis=0, keepdims=True) - mean3 * shift_own) * inv3
    pieces = [v[:, LANES * j : LANES * (j + 1)] for v in (shift_own, slope_own) for j in range(wide_tiles)]
    st4[me] = jnp.concatenate(pieces, axis=0).astype(BF16)
    gather_to_all(st4, 4)
    from_rows(out_ref, 0).start()
    shift3, slope_gain3 = get_sums(st4, 4)

    def back_terms(scale, inv, mean, shift_sum, gain_sum, inv_cnt):
        along = scale * inv * gain_sum * inv_cnt
        return along, scale * shift_sum * inv_cnt - mean * along

    along3, flat3 = back_terms(scale3, inv3, mean3, shift3, slope_gain3, inv_w)

    def back_three(i, carry):
        at = pl.ds(pl.multiple_of(i * big, big), big)
        m = mask[at, :]
        tiles = []
        for j in range(wide_tiles):
            lanes = slice(LANES * j, LANES * (j + 1))
            g = gt[at, lanes] * scale3[:, lanes] - pre3[at, lanes] * along3[:, lanes] - m * flat3[:, lanes]
            tiles.append(g.astype(BF16))
            gp3[at, lanes] = tiles[-1]
        d = dot(jnp.concatenate(tiles, axis=1), wet[...]) * slope2[at, :]
        dz[at, :] = d
        return carry[0] + part_sum(d), carry[1] + part_sum(d * ((pre2[at, :] - mean2) * inv2))

    sums = lax.fori_loop(0, 2, back_three, (zero_n, zero_n))
    send_sums(st5, 5, *sums)

    def grad_expand(i, carry):
        lanes = pl.ds(pl.multiple_of(i * 256, 256), 256)
        ge_ref[:, lanes] = dot(a2t[...], gp3[:, lanes]).astype(BF16)
        return carry

    lax.fori_loop(0, channels // 256, grad_expand, 0)
    if own_gather:
        cores(5).start()
        near(5)

    shift2, slope_gain2 = get_sums(st5, 5)
    along2, flat2 = back_terms(scale2, inv2, mean2, shift2, slope_gain2, inv_n)

    def back_two(i, carry):
        at = block_at(i)
        here = pl.ds(pl.multiple_of(i * BLOCK + pad, 16), BLOCK)
        m = both(mask[at, :])
        spad[here, :] = dz[at, :] * scale2 - m * (pre2[at, :] * along2 + flat2)
        return carry

    lax.fori_loop(0, blocks, back_two, 0)
    spread()

    def grad_spatial(row):
        gs_refs[row][...] = dot(a1t[...], taps(0, rows, range(3 * row, 3 * row + 3), True)).astype(BF16)
        if own_gather:
            cores(2 + row).start()

    grad_spatial(0)

    def back_spatial(i, carry):
        at = pl.ds(pl.multiple_of(i * big, big), big)
        d = dot(taps(i * big, big, range(9), True), wst[...]) * slope1[at, :]
        dz[at, :] = d
        return carry[0] + part_sum(d), carry[1] + part_sum(d * ((pre1[at, :] - mean1) * inv1))

    sums = lax.fori_loop(0, 2, back_spatial, (zero_n, zero_n))
    send_sums(st6, 6, *sums)
    if own_gather:
        near(2)
    grad_spatial(1)
    grad_spatial(2)
    if own_gather:
        near(3)
        near(4)
        far(5)

    shift1, slope_gain1 = get_sums(st6, 6)
    along1, flat1 = back_terms(scale1, inv1, mean1, shift1, slope_gain1, inv_n)

    def back_one(i, carry):
        at = block_at(i)
        g = dz[at, :] * scale1 - both(mask[at, :]) * (pre1[at, :] * along1 + flat1)
        gp1[at, :] = g.astype(BF16)
        return carry

    lax.fori_loop(0, blocks, back_one, 0)

    for i in range(2):
        height = channels // 2
        gr_refs[i][...] = dot(xt[height * i : height * (i + 1), :], gp1[...]).astype(BF16)
        if own_gather:
            cores(i).start()
    if own_gather:
        far(2)
        near(0)
        near(1)
    from_rows(out_ref, 0).wait()

    def grad_in(i, carry):
        at = pl.ds(pl.multiple_of(i * wide, wide), wide)
        m = mask[at, :]
        back = dot(gp1[at, :], wrt[...])
        for j in range(wide_tiles):
            lanes = slice(LANES * j, LANES * (j + 1))
            out_rows[j, at, :] = (m * back[:, lanes] + gt[at, lanes]).astype(BF16)
        return carry

    lax.fori_loop(0, rows // wide, grad_in, 0)
    if own_gather:
        far(3)
        far(4)
    from_rows(gin_ref, 1).start()

    def own_part(ref, v):
        width = ref.shape[0]
        spot = frame * width
        tile = jnp.zeros((1, LANES), F32)
        for t in range(v.shape[1] // LANES):
            tile = jnp.where(lax.div(spot, LANES) == t, v[:, LANES * t : LANES * (t + 1)], tile)
        tile = pltpu.roll(jnp.concatenate([tile] * 8, axis=0), lax.rem(LANES - lax.rem(spot, LANES), LANES), 1)
        ref[...] = tile[0, 0:width]

    own_part(vec1_gain, slope_gain1)
    own_part(vec1_shift, shift1)
    own_part(vec2_gain, slope_gain2)
    own_part(vec2_shift, shift2)
    own_part(vec3_gain, slope_gain3)
    own_part(vec3_shift, shift3)

    if own_gather:
        owners(5)
        far(0)
        far(1)
        for unit in (2, 3, 4, 0, 1):
            owners(unit)
        ge_out[...] = finished(5)[...].astype(F32)
        for row in range(3):
            fin = finished(2 + row)
            for c in range(3):
                gs_out[3 * row + c] = fin[:, narrow * c : narrow * (c + 1)].astype(F32)
        for i in range(2):
            gr_out[piece * i : piece * (i + 1), :] = finished(i)[...].astype(F32)
    else:
        for i in range(2):
            gr_out[channels // 2 * i : channels // 2 * (i + 1), :] = gr_refs[i][...]
        for row in range(3):
            gs_out[:, 3 * narrow * row : 3 * narrow * (row + 1)] = gs_refs[row][...]
        ge_out[...] = ge_ref[...]
    for index in range(3):
        weight_sent(index)
    if own_gather:
        for unit in range(units):
            sent(unit)
    for buf in (counts, st1, st2, st3, st4, st5, st6):
        most = buf.at[pl.ds(0, devices - 1)]
        pltpu.make_async_copy(most, most, st_send.at[0]).wait()
    most = par.at[pl.ds(0, frames - 1)]
    pltpu.make_async_copy(most, most, st_send.at[1]).wait()
    from_rows(gin_ref, 1).wait()


def deliver_kernel(count, *refs):
    sources, targets, sems = refs[:count], refs[count : 2 * count], refs[2 * count]
    for i in range(2):
        for j in range(sources[i].shape[0]):
            part = targets[i].at[:, :, LANES * j : LANES * (j + 1)]
            pltpu.make_async_copy(sources[i].at[j], part, sems.at[i]).start()
    for i in range(2, count):
        pltpu.make_async_copy(sources[i], targets[i], sems.at[i]).start()
    for i in range(count):
        pltpu.make_async_copy(sources[i], sources[i], sems.at[i]).wait()


def deliver(arrays, big):
    count = len(arrays)
    shapes = [big, big] + [jax.ShapeDtypeStruct(a.shape, a.dtype) for a in arrays[2:]]
    return pl.pallas_call(
        functools.partial(deliver_kernel, count),
        out_shape=tuple(shapes),
        in_specs=[pl.BlockSpec(memory_space=pltpu.VMEM)] * count,
        out_specs=(pl.BlockSpec(memory_space=pl.ANY),) * count,
        scratch_shapes=[pltpu.SemaphoreType.DMA((count,))],
        compiler_params=pltpu.CompilerParams(vmem_limit_bytes=1024 * 1024),
    )(*arrays)


def on_device(
    dims,
    x_in,
    cotangent,
    w_reduce,
    w_spatial,
    w_expand,
    gain_one,
    shift_one,
    gain_two,
    shift_two,
    gain_three,
    shift_three,
    bucket,
    frame_count,
):
    clips, frames = dims
    slots, side, _, channels = x_in.shape
    narrow = w_reduce.shape[1]
    pixels = side * side
    rows = pixels * slots
    tiles = channels // LANES
    devices = clips * frames
    own_gather = clips == 4 and all(n % 32 == 0 for n in (w_reduce.shape[0], w_spatial.shape[2], w_expand.shape[0]))
    w_spatial = w_spatial.reshape(9, -1, narrow)
    if not own_gather:
        w_reduce = lax.all_gather(w_reduce, "frame", axis=0, tiled=True)
        w_spatial = lax.all_gather(w_spatial, "frame", axis=1, tiled=True)
        w_expand = lax.all_gather(w_expand, "frame", axis=0, tiled=True)

    def by_pixel(v):
        return jnp.transpose(v, (1, 2, 0, 3)).reshape(pixels, slots, channels)

    any_spec = pl.BlockSpec(memory_space=pl.ANY)
    vmem = pl.BlockSpec(memory_space=pltpu.VMEM)
    smem = pl.BlockSpec(memory_space=pltpu.SMEM)
    big = jax.ShapeDtypeStruct((pixels, slots, channels), BF16)
    staged = pltpu.VMEM((tiles, pixels, slots, LANES), BF16)
    native = pltpu.VMEM((tiles, rows, LANES), BF16)
    narrow_f32 = pltpu.VMEM((rows, narrow), F32)
    wide_f32 = pltpu.VMEM((rows, channels), F32)
    lanes_f32 = pltpu.VMEM((rows, LANES), F32)
    edges_f32 = pltpu.VMEM((rows + 16, LANES), F32)

    def stats(count):
        return pltpu.VMEM((devices, count, LANES), F32)

    if own_gather:
        grad_shapes = (
            pltpu.VMEM((channels // frames, narrow), F32),
            pltpu.VMEM((9, narrow // frames, narrow), F32),
            pltpu.VMEM((narrow // frames, channels), F32),
        )
    else:
        grad_shapes = (
            jax.ShapeDtypeStruct((channels, narrow), BF16),
            jax.ShapeDtypeStruct((narrow, 9 * narrow), BF16),
            jax.ShapeDtypeStruct((narrow, channels), BF16),
        )
    wholes = (*(((channels // 2, narrow),) * 2), *(((narrow, 3 * narrow),) * 3), (narrow, channels))
    lines = clips // 2
    unit_scratch = [pltpu.VMEM(shape, BF16) for shape in wholes]
    if own_gather:
        cuts = [(height // frames // 2, width) for height, width in wholes]
        unit_scratch += [pltpu.VMEM((frames, half, width), BF16) for half, width in cuts]
        unit_scratch += [
            pltpu.VMEM((frames // 2, half, width) if hop == "x" else (frames, half, width // lines), BF16)
            for (half, width), hop in zip(cuts, NEAR)
        ]
        unit_scratch += [
            pltpu.VMEM((frames if hop else frames * lines, half, width // lines), BF16)
            for (half, width), hop in zip(cuts, NEAR)
        ]
        unit_scratch += [pltpu.VMEM((2 * half, width), BF16) for half, width in cuts]

    results = pl.pallas_call(
        functools.partial(block_kernel, (clips, frames, side, own_gather)),
        out_shape=(
            staged,
            staged,
            *grad_shapes,
            *(pltpu.VMEM((narrow // frames,), F32),) * 4,
            *(pltpu.VMEM((channels // frames,), F32),) * 2,
        ),
        in_specs=[any_spec] * 5 + [vmem] * 6 + [smem] * 2,
        out_specs=(vmem,) * 11,
        scratch_shapes=[
            staged,
            staged,
            native,
            native,
            native,
            pltpu.VMEM((rows, channels), BF16),
            pltpu.VMEM((channels, rows), BF16),
            pltpu.VMEM((narrow, rows), BF16),
            pltpu.VMEM((narrow, rows), BF16),
            lanes_f32,
            edges_f32,
            edges_f32,
            pltpu.VMEM((channels, narrow), BF16),
            pltpu.VMEM((9, narrow, narrow), BF16),
            pltpu.VMEM((narrow, channels), BF16),
            pltpu.VMEM((9 * narrow, narrow), BF16),
            pltpu.VMEM((channels, narrow), BF16),
            pltpu.VMEM((narrow, channels), BF16),
            narrow_f32,
            narrow_f32,
            narrow_f32,
            narrow_f32,
            narrow_f32,
            pltpu.VMEM((rows + 4 * side + 16, narrow), F32),
            pltpu.VMEM((rows, narrow), BF16),
            pltpu.VMEM((3, rows, narrow), BF16),
            pltpu.VMEM((3, rows + 4 * side, narrow), BF16),
            wide_f32,
            wide_f32,
            pltpu.VMEM((rows, channels), BF16),
            pltpu.VMEM((rows, narrow), BF16),
            pltpu.VMEM((frames, 8, LANES), F32),
            stats(1),
            stats(2 * narrow // LANES),
            stats(2 * narrow // LANES),
            pltpu.VMEM((devices, 1, narrow + channels), F32),
            pltpu.VMEM((devices, 2 * tiles, LANES), BF16),
            stats(2 * narrow // LANES),
            stats(2 * narrow // LANES),
            pltpu.SemaphoreType.DMA((5,)),
            pltpu.SemaphoreType.DMA((3,)),
            pltpu.SemaphoreType.DMA((3 * frames,)),
            pltpu.SemaphoreType.DMA((2,)),
            pltpu.SemaphoreType.DMA((8,)),
            pltpu.SemaphoreType.DMA((2,)),
            pltpu.SemaphoreType.DMA((len(NEAR),)),
            pltpu.SemaphoreType.DMA((len(NEAR), 4)),
            *unit_scratch,
        ],
        compiler_params=pltpu.CompilerParams(
            collective_id=0, has_side_effects=True, vmem_limit_bytes=VMEM_BYTES
        ),
    )(
        by_pixel(x_in),
        by_pixel(cotangent),
        w_reduce,
        w_spatial,
        w_expand,
        gain_one,
        shift_one,
        gain_two,
        shift_two,
        gain_three,
        shift_three,
        bucket,
        frame_count,
    )

    def by_frame(v):
        return jnp.transpose(v.reshape(side, side, slots, channels), (2, 0, 1, 3))

    def owned(v):
        part = lax.psum_scatter(v, "frame", scatter_dimension=0, tiled=True)
        return lax.psum(part, "clip").astype(F32)

    if own_gather:
        out, gin, gr, gs, ge, *vectors = deliver(results, big)
    else:
        gr, gs, ge = [owned(v) for v in results[2:5]]
        gs = gs.reshape(-1, 9, narrow).transpose(1, 0, 2)
        out, gin, gr, gs, ge, *vectors = deliver((*results[:2], gr, gs, ge, *results[5:]), big)
    return (by_frame(out), by_frame(gin), gr, gs.reshape(3, 3, -1, narrow), ge, *vectors)


def solution(mesh):
    by_device = P(("clip", "frame"))
    shard = P("frame")
    spatial = P(None, None, "frame", None)
    return jax.shard_map(
        functools.partial(on_device, (mesh.shape["clip"], mesh.shape["frame"])),
        mesh=mesh,
        in_specs=(by_device, by_device, shard, spatial) + (shard,) * 7 + (by_device, by_device),
        out_specs=(by_device, by_device, shard, spatial) + (shard,) * 7,
        check_vma=False,
    )
```
